32 devices in a mesh: tab: 4 (over y, x), rows: 8 (over z, core).
Axes of the slice: x: 2, y: 2, z: 4, core: 2. Of those that a mesh axis runs over, the one named last changes fastest.
Arguments:
- cells: bfloat16 [4, 1024, 16, 512], P('tab', 'rows'), may hold values from -6 to 6
- missing_mask: int32 [4, 1024, 16], P('tab', 'rows'), may hold values 0 or 1
- context_counts: int32 [4, 8], P('tab', 'rows'), may hold values from 1 to 4, as said below
- missing_embedding: bfloat16 [512], replicated, may hold values from -6 to 6
- gain_feature: bfloat16 [512], replicated, may hold values from 0.5 to 1.5
- w_feature_qkv: bfloat16 [512, 1536], replicated, may hold values from -0.25 to 0.25
- w_feature_out: bfloat16 [512, 512], replicated, may hold values from -0.5 to 0.5
- gain_row: bfloat16 [512], replicated, may hold values from 0.5 to 1.5
- w_row_qkv: bfloat16 [512, 1536], replicated, may hold values from -0.25 to 0.25
- w_row_out: bfloat16 [512, 512], replicated, may hold values from -1 to 1
- gain_mlp: bfloat16 [512], replicated, may hold values from 0.5 to 1.5
- w_up: bfloat16 [512, 2048], replicated, may hold values from -0.25 to 0.25
- w_down: bfloat16 [2048, 512], replicated, may hold values from -0.125 to 0.125
- upstream: bfloat16 [4, 1024, 16, 512], P('tab', 'rows'), may hold values from -6 to 6
Outputs:
- output: bfloat16 [4, 1024, 16, 512], P('tab', 'rows')
- grad_cells: float32 [4, 1024, 16, 512], P('tab', 'rows')
- grad_missing: float32 [512], P('rows')
- grad_gain_feature: float32 [512], P('rows')
- grad_w_feature_qkv: float32 [512, 1536], P('rows')
- grad_w_feature_out: float32 [512, 512], P('rows')
- grad_gain_row: float32 [512], P('rows')
- grad_w_row_qkv: float32 [512, 1536], P('rows')
- grad_w_row_out: float32 [512, 512], P('rows')
- grad_gain_mlp: float32 [512], P('rows')
- grad_w_up: float32 [512, 2048], P('rows')
- grad_w_down: float32 [2048, 512], P('rows')
The draws below stay inside these ranges and needn't reach their ends.
Inputs may be any that keep to these rules, and one draw needn't show every extreme that they name: `context_counts`: every block of every table holds at least one context row; in each table some block holds exactly 4.
All inputs are finite; a program needn't handle non-finite values. No bound on the sum of `missing_mask` on one device may be relied on, other than what follows from the above.
Results may differ from the reference program's by a relative error of at most 0.019.
Values may be sent and summed in bfloat16 or wider, within the bound.
No kernel may reach another device: no remote copies, remote signals or barrier semaphores. Data moves between devices by JAX's collectives and lax.ppermute only.
A program may use at most 192 MiB of HBM per device.

```python
import jax
import jax.numpy as jnp
from jax import lax

D = 512
HEADS = 4
FF = 2048
FEATURES = 16
CTX_DEV = 4
TABLES = 4
ROWS = 1024
RPD = 128
BLOCKS = 8
KEYS = 32


def draw_context_counts(key, part):
    key = jax.random.fold_in(key, 7)
    first_key, second_key, third_key = jax.random.split(key, 3)
    first = jax.random.randint(first_key, (TABLES, BLOCKS), 0, CTX_DEV)
    second = jax.random.randint(second_key, (TABLES, BLOCKS), 0, CTX_DEV + 1)
    counts = 1 + jnp.minimum(first, second)
    full_at = jax.random.randint(third_key, (TABLES, 1), 0, BLOCKS)
    block_ids = jnp.arange(BLOCKS, dtype=jnp.int32)[None, :]
    return jnp.where(block_ids == full_at, CTX_DEV, counts).astype(jnp.int32)


def touch_ends(drawn, rng, smallest, largest):
    index_at = [jax.random.randint(jax.random.fold_in(rng, axis), (), 0, length) for axis, length in enumerate(drawn.shape)]
    main_axis = drawn.shape.index(max(drawn.shape))
    beside = index_at[:main_axis] + [(index_at[main_axis] + 1) % drawn.shape[main_axis]] + index_at[main_axis + 1:]
    return drawn.at[tuple(index_at)].set(smallest).at[tuple(beside)].set(largest)


def block_scale(stream_key, shape, cuts, least, high):
    gain = 1.0
    for axis_at, parts in cuts:
        draws = jax.random.uniform(jax.random.fold_in(jax.random.fold_in(stream_key, 6), axis_at), (parts,), jnp.float32, least / len(cuts), high / len(cuts))
        gain = gain * jnp.repeat(jnp.exp(draws), shape[axis_at] // parts).reshape((-1,) + (1,) * (len(shape) - 1 - axis_at))
    return gain


def gaussian(own_key, shape, width, reach, cuts=(), held_as=jnp.bfloat16):
    array = jax.random.normal(own_key, shape, jnp.float32) * width
    if len(cuts) > 0:
        array = block_scale(own_key, shape, cuts, -0.22, 0.18) * array
    return jnp.clip(array, min=-reach, max=reach).astype(held_as)


def setup_inputs(seed: int = 0) -> dict:
    splits = jax.random.split(jax.random.key(seed), 15)
    cells = gaussian(splits[0], (TABLES, ROWS, FEATURES, D), 1.0, 6.0, ((0, 4), (1, 8)))
    missing_mask = touch_ends((jax.random.randint(splits[1], (TABLES, ROWS, FEATURES), 0, 10) < 1).astype(jnp.int32), jax.random.fold_in(splits[1], 1), 0, 1)
    context_counts = draw_context_counts(jax.random.fold_in(splits[14], 71), 0)
    missing_embedding = gaussian(splits[3], (D,), 1.0, 6.0)
    gain_feature = jnp.clip(1.0 + 0.1 * jax.random.normal(splits[4], (D,), jnp.float32), 0.5, 1.5).astype(jnp.bfloat16)
    w_feature_qkv = gaussian(splits[5], (D, 3 * D), D ** -0.5, 0.25)
    w_feature_out = gaussian(splits[6], (D, D), (D // 4) ** -0.5, 0.5)
    gain_row = jnp.clip(1.0 + 0.1 * jax.random.normal(splits[7], (D,), jnp.float32), 0.5, 1.5).astype(jnp.bfloat16)
    w_row_qkv = gaussian(splits[8], (D, 3 * D), D ** -0.5, 0.25)
    w_row_out = gaussian(splits[9], (D, D), (D // 16) ** -0.5, 1.0)
    gain_mlp = jnp.clip(1.0 + 0.1 * jax.random.normal(splits[10], (D,), jnp.float32), 0.5, 1.5).astype(jnp.bfloat16)
    w_up = gaussian(splits[11], (D, FF), D ** -0.5, 0.25)
    w_down = gaussian(splits[12], (FF, D), FF ** -0.5, 0.125)
    upstream = gaussian(splits[13], (TABLES, ROWS, FEATURES, D), 1.0, 6.0, ((0, 4), (1, 8)))
    return {"cells": cells, "missing_mask": missing_mask, "context_counts": context_counts, "missing_embedding": missing_embedding, "gain_feature": gain_feature, "w_feature_qkv": w_feature_qkv, "w_feature_out": w_feature_out, "gain_row": gain_row, "w_row_qkv": w_row_qkv, "w_row_out": w_row_out, "gain_mlp": gain_mlp, "w_up": w_up, "w_down": w_down, "upstream": upstream}


@jax.custom_vjp
def low(v):
    return lax.optimization_barrier(v.astype(jnp.bfloat16)).astype(jnp.float32)

@jax.custom_vjp
def low_back(v):
    return v

def low_keep(v):
    return (low(v), None)

def low_pass(kept, grad):
    return (grad,)

def back_keep(v):
    return (v, None)

def back_low(kept, grad):
    return (low(grad),)
low.defvjp(low_keep, low_pass)
low_back.defvjp(back_keep, back_low)
PRECISE = lax.Precision.HIGHEST
EPSILON = 1e-05
MASKED = -1e+30

def matmul(left_arg, right_arg):
    return jnp.einsum('...k,kn->...n', left_arg, right_arg, precision=PRECISE)

def layer_norm(tensor, gain_in):
    row_mean = lax.optimization_barrier(jnp.mean(tensor, axis=-1, keepdims=True))
    centred = tensor - row_mean
    spread = lax.optimization_barrier(jnp.mean(centred * centred, axis=-1, keepdims=True))
    return centred * lax.rsqrt(spread + EPSILON) * gain_in

def split_heads(tensor):
    return tensor.reshape(tensor.shape[:-1] + (HEADS, D // HEADS))

def feature_attention(normed, w_qkv, w_out):
    score_scale = (D // HEADS) ** (-0.5)
    packed = low(low_back(matmul(normed, w_qkv)))
    queries = split_heads(packed[..., :D])
    key_heads = split_heads(packed[..., D:2 * D])
    value_heads = split_heads(packed[..., 2 * D:])
    scores = low_back(jnp.einsum('rqhd,rkhd->rhqk', queries, key_heads, precision=PRECISE) * score_scale)
    weights = low(jax.nn.softmax(scores, axis=-1))
    attended = jnp.einsum('rhqk,rkhd->rqhd', weights, value_heads, precision=PRECISE)
    attended = low(low_back(attended.reshape(normed.shape)))
    return low_back(matmul(attended, w_out))

def row_attention(normed, counts, w_qkv, w_out):
    score_scale = (D // HEADS) ** (-0.5)
    queries = low(low_back(matmul(normed, w_qkv[:, :D])))
    context = normed.reshape(BLOCKS, RPD, FEATURES, D)[:, :CTX_DEV].reshape(KEYS, FEATURES, D)
    key_values = low(matmul(context, w_qkv[:, D:]))
    is_context = (jnp.arange(CTX_DEV, dtype=jnp.int32)[None, :] < counts[:, None]).reshape(KEYS)

    def one_feature(feature_block):
        query_f, key_f, value_f = feature_block
        scores = low_back(jnp.einsum('qhd,khd->hqk', query_f, key_f, precision=PRECISE) * score_scale)
        weights = low(jax.nn.softmax(jnp.where(is_context, scores, MASKED), axis=-1))
        return jnp.einsum('hqk,khd->qhd', weights, value_f, precision=PRECISE)
    query_t = jnp.moveaxis(split_heads(queries), 1, 0)
    key_t = jnp.moveaxis(split_heads(key_values[..., :D]), 1, 0)
    value_t = jnp.moveaxis(split_heads(key_values[..., D:]), 1, 0)
    attended = lax.map(jax.checkpoint(one_feature), (query_t, key_t, value_t))
    attended = jnp.moveaxis(attended, 0, 1).reshape(normed.shape)
    attended = low(low_back(attended))
    return low_back(matmul(attended, w_out))

def feed_forward(normed, w_up, w_down):
    pre_gelu = low_back(matmul(normed, w_up))
    hidden = low(jax.nn.gelu(pre_gelu))
    return low_back(matmul(hidden, w_down))

def table_layer(start, counts, weights_all):
    gain_feature, w_fq, w_fo, gain_row, w_rq, w_ro, gain_mlp, w_up, w_down = weights_all
    after_one = start + feature_attention(low(layer_norm(start, gain_feature)), w_fq, w_fo)
    after_two = after_one + row_attention(low(layer_norm(after_one, gain_row)), counts, w_rq, w_ro)
    return after_two + feed_forward(low(layer_norm(after_two, gain_mlp)), w_up, w_down)

def reference(cells, missing_mask, context_counts, missing_embedding, gain_feature, w_feature_qkv, w_feature_out, gain_row, w_row_qkv, w_row_out, gain_mlp, w_up, w_down, upstream):
    absent = (missing_mask == 1)[..., None]
    weights_in = tuple((w.astype(jnp.float32) for w in (gain_feature, w_feature_qkv, w_feature_out, gain_row, w_row_qkv, w_row_out, gain_mlp, w_up, w_down)))

    def forward(cells_f, missing_f, weights_all):
        start = jnp.where(absent, missing_f, cells_f)

        def one_table(table_block):
            return table_layer(table_block[0], table_block[1], weights_all)
        return lax.map(jax.checkpoint(one_table), (start, context_counts))
    result, pullback = jax.vjp(forward, cells.astype(jnp.float32), missing_embedding.astype(jnp.float32), weights_in)
    grad_cells, grad_missing, grad_weights = pullback(upstream.astype(jnp.float32))
    return (result.astype(jnp.bfloat16), grad_cells, grad_missing, grad_weights[0], grad_weights[1], grad_weights[2], grad_weights[3], grad_weights[4], grad_weights[5], grad_weights[6], grad_weights[7], grad_weights[8])
```

```python
import functools

import jax
import jax.numpy as jnp
from jax import lax
from jax.experimental import pallas as pl
from jax.experimental.pallas import tpu as pltpu
from jax.sharding import PartitionSpec as P

HEADS = 4
CTX_DEV = 4
EPSILON = 1e-05
MASKED = -1e30
F32 = jnp.float32
BF16 = jnp.bfloat16
GROUP_ROWS = 8
VMEM_LIMIT = 60 * 1024 * 1024


def dot_nn(left, right):
    return lax.dot_general(left, right, (((1,), (0,)), ((), ())), preferred_element_type=F32)


def dot_nt(left, right):
    return lax.dot_general(left, right, (((1,), (1,)), ((), ())), preferred_element_type=F32)


def dot_tn(left, right):
    return lax.dot_general(left, right, (((0,), (0,)), ((), ())), preferred_element_type=F32)


def normalize(tensor):
    row_mean = jnp.mean(tensor, axis=-1, keepdims=True)
    centred = tensor - row_mean
    scale = lax.rsqrt(jnp.mean(centred * centred, axis=-1, keepdims=True) + EPSILON)
    return centred * scale, scale


def norm_back(xhat, scale, gain, gradient):
    scaled = gradient * gain
    first = jnp.mean(scaled, axis=-1, keepdims=True)
    second = jnp.mean(scaled * xhat, axis=-1, keepdims=True)
    return scale * (scaled - first - xhat * second)


def column_sum(tensor):
    rows, width = tensor.shape
    return jnp.sum(tensor.reshape(rows // 8, 8, width), axis=0)


def missing_column(mask, first, rows):
    features, lanes = mask.shape
    shape = (rows, features, lanes)
    pick = lax.broadcasted_iota(jnp.int32, shape, 2) == first + lax.broadcasted_iota(jnp.int32, shape, 0)
    spread = jnp.broadcast_to(mask.astype(F32)[None], shape)
    return jnp.sum(jnp.where(pick, spread, 0.0), axis=-1, keepdims=True)


def start_cells(cells, mask, first, missing):
    rows, features, width = cells.shape
    absent = missing_column(mask, first, rows) > 0.5
    return jnp.where(absent, missing.reshape(1, 1, width), cells.astype(F32)).reshape(rows * features, width), absent


def same_row_bias(size, features):
    shape = (size, size)
    left = lax.broadcasted_iota(jnp.int32, shape, 0) // features
    right = lax.broadcasted_iota(jnp.int32, shape, 1) // features
    return jnp.where(left == right, 0.0, MASKED)


def head_parts(packed, part, group, head):
    cells, width = packed.shape[0], packed.shape[1] // 3
    return [
        packed[low : low + group, part * width + h * head : part * width + (h + 1) * head]
        for low in range(0, cells, group)
        for h in range(HEADS)
    ]


def join_parts(parts):
    rows = [jnp.concatenate(parts[at : at + HEADS], axis=1) for at in range(0, len(parts), HEADS)]
    return jnp.concatenate(rows, axis=0)


def softmax_keys(scores):
    exp_terms = jnp.exp(scores - jnp.max(scores, axis=1, keepdims=True))
    return exp_terms * (1.0 / jnp.sum(exp_terms, axis=1, keepdims=True))


def feature_forward(start, gain, w_qkv, w_out, features, group):
    cells, width = start.shape
    head = width // HEADS
    xhat, _ = normalize(start)
    qkv = dot_nn((xhat * gain).astype(BF16), w_qkv).astype(BF16)
    queries, keys, values = (head_parts(qkv, part, group, head) for part in range(3))
    scores = jnp.stack([dot_nt(key, query) for key, query in zip(keys, queries)])
    probs = softmax_keys(scores * (head**-0.5) + same_row_bias(group, features)[None]).astype(BF16)
    att = join_parts([dot_tn(probs[at], value).astype(BF16) for at, value in enumerate(values)])
    return start + dot_nn(att, w_out), qkv, probs, att


def context_kernel(count_ref, cells_ref, mask_ref, vectors_ref, w_qkv_ref, w_out_ref, send_ref, after_ref):
    rows, features, width = cells_ref.shape
    cells = rows * features
    start, _ = start_cells(cells_ref[...], mask_ref[...], 0, vectors_ref[0:1])
    after, _, _, _ = feature_forward(start, vectors_ref[1:2], w_qkv_ref[...], w_out_ref[...], features, cells)
    after_ref[...] = after
    xhat, _ = normalize(after)
    send_ref[0:cells, :] = (xhat * vectors_ref[2:3]).astype(BF16)
    count = count_ref[0, 0].astype(F32)
    send_ref[cells : cells + 16, :] = jnp.full((16, width), count, F32).astype(BF16)


def feature_kernel(
    cells_ref, mask_ref, upstream_ref, vectors_ref, w_qkv_ref, w_out_ref,
    after_ref, upstream_t_ref, qkv_ref, probs_ref, att_ref,
):
    rows, features, width = cells_ref.shape
    start, _ = start_cells(cells_ref[...], mask_ref[...], pl.program_id(0) * rows, vectors_ref[0:1])
    after, qkv, probs, att = feature_forward(
        start, vectors_ref[1:2], w_qkv_ref[...], w_out_ref[...], features, GROUP_ROWS * features
    )
    qkv_ref[...] = qkv
    probs_ref[...] = probs.reshape(probs_ref.shape)
    att_ref[...] = att
    after_ref[...] = jnp.swapaxes(after.reshape(rows, features, width), 0, 1)
    upstream_t_ref[...] = jnp.swapaxes(upstream_ref[...].astype(F32), 0, 1).astype(BF16)


def head_blocks(tensor):
    keys, width = tensor.shape
    tiled = jnp.concatenate([tensor] * HEADS, axis=0)
    row_head = lax.broadcasted_iota(jnp.int32, tiled.shape, 0) // keys
    lane_head = lax.broadcasted_iota(jnp.int32, tiled.shape, 1) // (width // HEADS)
    return jnp.where(row_head == lane_head, tiled, jnp.zeros_like(tiled))


def own_heads(tensor, keys):
    head = tensor.shape[1] // HEADS
    return jnp.concatenate([tensor[h * keys : (h + 1) * keys, h * head : (h + 1) * head] for h in range(HEADS)], axis=1)


def gelu_parts(inner):
    const = 0.7978845608028654
    square = inner * inner
    tanh = jnp.tanh(inner * (const + (const * 0.044715) * square))
    half = 0.5 + 0.5 * tanh
    hidden = inner * half
    slope = half + (0.5 - 0.5 * tanh * tanh) * inner * (const + (3.0 * const * 0.044715) * square)
    return hidden, slope


def read_slots(gathered, idx_ref, slots_ref, bias_ref, features):
    keys, width = slots_ref.shape[1], slots_ref.shape[2]
    blocks = keys // CTX_DEV
    block = CTX_DEV * features
    piece = block + 16
    slot = lax.broadcasted_iota(jnp.int32, (keys, 128), 0)
    counts = jnp.zeros((keys, 128), F32)
    core, line = idx_ref[1] % 2, idx_ref[1] // 2
    for pair in range(blocks // 2):
        if len(gathered) == 2:
            mine, other = (ref[pair * piece : (pair + 1) * piece, :].astype(F32) for ref in gathered)
            even, odd = jnp.where(core == 0, mine, other), jnp.where(core == 0, other, mine)
            at = line ^ pair
        else:
            even, odd = (gathered[0][(2 * pair + j) * piece : (2 * pair + j + 1) * piece, :].astype(F32) for j in range(2))
            at = pair
        both = jnp.concatenate([even[0:block], odd[0:block]], axis=0).reshape(2 * CTX_DEV, features, width)
        slots_ref[:, pl.ds(pl.multiple_of(at * 2 * CTX_DEV, 2 * CTX_DEV), 2 * CTX_DEV), :] = jnp.swapaxes(both, 0, 1)
        for j, part in enumerate((even, odd)):
            counts = jnp.where(slot // CTX_DEV == 2 * at + j, part[block : block + 1, 0:128], counts)
    bias = jnp.where((slot % CTX_DEV).astype(F32) < counts, 0.0, MASKED)
    bias_ref[...] = jnp.concatenate([bias] * HEADS, axis=0)


def emit(idx_ref, keep_ref, send_ref, sources):
    tab, block = idx_ref[0], idx_ref[1]
    core, line = block % 2, block // 2
    tabs, lines, rows, _ = keep_ref.shape
    for u in range(tabs):
        for q in range(lines):
            for ref, shard in ((keep_ref, core), (send_ref, 1 - core)):
                for acc, column in sources:
                    height, width = acc.shape
                    part = height // (2 * lines * tabs)
                    low = (((line ^ q) * 2 + shard) * tabs + (tab ^ u)) * part
                    for at in range(part // rows):
                        low_at = pl.multiple_of(low + at * rows, rows)
                        ref[u, q, :, column + at * width : column + (at + 1) * width] = acc[pl.ds(low_at, rows), :].astype(BF16)


def rows_kernel(pieces, fast, *refs):
    (idx_ref, after_ref, upstream_ref, vectors_ref, w_row_ref, w_out_ref, w_up_ref, w_down_ref), refs = refs[:8], refs[8:]
    gathered, refs = refs[:pieces], refs[pieces:]
    (output_ref, grad_after_ref, gains_ref, slot_out), refs = refs[:4], refs[4:]
    if fast:
        outs, refs = refs[:2], refs[2:]
    grad_up, grad_down, grad_qkv, grad_out, slots_ref, bias_ref, gain_acc = refs
    feats, rows, width = after_ref.shape
    features, keys, _ = slots_ref.shape
    hidden_all = w_up_ref.shape[1]
    cells = feats * rows
    head = width // HEADS
    step = pl.program_id(0)
    gain_row, gain_mlp = vectors_ref[2:3], vectors_ref[3:4]

    @pl.when(step == 0)
    def _():
        read_slots(gathered, idx_ref, slots_ref, bias_ref, features)
        for ref in (grad_qkv, grad_out, grad_up, grad_down, gain_acc):
            ref[...] = jnp.zeros_like(ref)

    after = after_ref[...].reshape(cells, width)
    xhat2, scale2 = normalize(after)
    normed_two = (xhat2 * gain_row).astype(BF16)
    query = dot_nn(normed_two, w_row_ref[:, 0:width]).astype(BF16)
    slots = slots_ref[pl.ds(step * feats, feats)].reshape(feats * keys, width).astype(BF16)
    kv = dot_nn(slots, w_row_ref[:, width : 3 * width]).astype(BF16)
    keys_b = [head_blocks(kv[f * keys : (f + 1) * keys, 0:width]) for f in range(feats)]
    values_b = [head_blocks(kv[f * keys : (f + 1) * keys, width : 2 * width]) for f in range(feats)]
    query_f = [query[f * rows : (f + 1) * rows] for f in range(feats)]
    scores = jnp.stack([dot_nt(keys_b[f], query_f[f]) for f in range(feats)])
    scores = scores * (head**-0.5) + bias_ref[:, 0:rows][None]
    probs = softmax_keys(scores.reshape(feats * HEADS, keys, rows))
    probs_b = probs.reshape(feats, HEADS * keys, rows).astype(BF16)
    att = jnp.concatenate([dot_tn(probs_b[f], values_b[f]).astype(BF16) for f in range(feats)], axis=0)
    after_two = after + dot_nn(att, w_out_ref[...])

    xhat3, scale3 = normalize(after_two)
    normed_three = (xhat3 * gain_mlp).astype(BF16)
    upstream = upstream_ref[...].reshape(cells, width)
    total, grad3 = after_two, None
    piece = 512
    for at in range(0, hidden_all, piece):
        w_up = w_up_ref[:, at : at + piece]
        w_down = w_down_ref[at : at + piece, :]
        hidden, slope = gelu_parts(dot_nn(normed_three, w_up))
        hidden = hidden.astype(BF16)
        grad_inner = (dot_nt(upstream, w_down) * slope).astype(BF16)
        total = total + dot_nn(hidden, w_down)
        back = dot_nt(grad_inner, w_up)
        grad3 = back if grad3 is None else grad3 + back
        grad_down[at : at + piece, :] += dot_tn(hidden, upstream)
        grad_up[:, at : at + piece] += dot_tn(normed_three, grad_inner)
    output_ref[...] = total.astype(BF16).reshape(feats, rows, width)
    gain_acc[0] += column_sum(grad3 * xhat3)
    grad_two = upstream.astype(F32) + norm_back(xhat3, scale3, gain_mlp, grad3)

    branch = grad_two.astype(BF16)
    grad_out[...] += dot_tn(att, branch)
    grad_att = dot_nt(branch, w_out_ref[...]).astype(BF16)
    grad_f = [grad_att[f * rows : (f + 1) * rows] for f in range(feats)]
    grad_probs = jnp.stack([dot_nt(values_b[f], grad_f[f]) for f in range(feats)]).reshape(feats * HEADS, keys, rows)
    grad_scores = probs * (grad_probs - jnp.sum(grad_probs * probs, axis=1, keepdims=True))
    grad_scores = grad_scores.reshape(feats, HEADS * keys, rows).astype(BF16)
    grad_query = jnp.concatenate([dot_tn(grad_scores[f], keys_b[f]) for f in range(feats)], axis=0)
    grad_query = (grad_query * (head**-0.5)).astype(BF16)
    grad_keys = [own_heads(dot_nn(grad_scores[f], query_f[f]), keys) for f in range(feats)]
    grad_values = [own_heads(dot_nn(probs_b[f], grad_f[f]), keys) for f in range(feats)]
    grad_kv = jnp.concatenate(
        [jnp.concatenate(grad_keys, axis=0) * (head**-0.5), jnp.concatenate(grad_values, axis=0)], axis=1
    ).astype(BF16)
    grad_qkv[:, 0:width] += dot_tn(normed_two, grad_query)
    grad_qkv[:, width : 3 * width] += dot_tn(slots, grad_kv)
    slots_ref[pl.ds(step * feats, feats)] = dot_nt(grad_kv, w_row_ref[:, width : 3 * width]).reshape(feats, keys, width)
    grad_normed = dot_nt(grad_query, w_row_ref[:, 0:width])
    gain_acc[1] += column_sum(grad_normed * xhat2)
    grad_after_ref[...] = (grad_two + norm_back(xhat2, scale2, gain_row, grad_normed)).reshape(feats, rows, width)

    @pl.when(step == pl.num_programs(0) - 1)
    def _():
        gains_ref[...] = gain_acc[...]
        block = CTX_DEV * features
        for at in range(0, keys, 2 * CTX_DEV):
            both = jnp.swapaxes(slots_ref[:, at : at + 2 * CTX_DEV, :], 0, 1).reshape(2 * block, width)
            slot_out[at * features : at * features + 2 * block, :] = both.astype(BF16)
        if fast:
            emit(
                idx_ref, outs[0], outs[1],
                [(grad_up, 0), (grad_qkv, hidden_all), (grad_out, hidden_all + 3 * width), (grad_down, hidden_all + 4 * width)],
            )


def feature_backward_kernel(first, fast, *refs):
    if first:
        idx_ref, refs = refs[0], refs[1:]
    (
        cells_ref, mask_ref, vectors_ref, w_qkv_ref, w_out_ref, grad_after_ref, qkv_ref, probs_ref, att_ref, output_t_ref,
    ), refs = refs[:10], refs[10:]
    if first:
        (qkv_in, out_in, gains_in, row_gains, _, _, after_ctx_ref, slots_in), refs = refs[:8], refs[8:]
    (output_ref, grad_cells_ref, gains_ref), refs = refs[:3], refs[3:]
    grad_w_qkv, grad_w_out, gain_acc, columns = refs[2:]
    outs = refs[:2]
    rows, features, width = cells_ref.shape
    cells = rows * features
    head = width // HEADS
    group = GROUP_ROWS * features
    step = pl.program_id(0)

    @pl.when(step == 0)
    def _():
        if first:
            grad_w_qkv[...] = qkv_in[...]
            grad_w_out[...] = out_in[...]
            gain_acc[0:2] = gains_in[...]
            gain_acc[2] = row_gains[1]
            gain_acc[3] = row_gains[0]
        else:
            for ref in (grad_w_qkv, grad_w_out, gain_acc):
                ref[...] = jnp.zeros_like(ref)

    output_ref[...] = jnp.swapaxes(output_t_ref[...].astype(F32), 0, 1).astype(BF16)
    grad_one = jnp.swapaxes(grad_after_ref[...], 0, 1).reshape(cells, width)
    if first:
        block = CTX_DEV * features
        total = slots_in[...].astype(F32)
        xhat2, scale2 = normalize(after_ctx_ref[...])
        gain_acc[2] += column_sum(total * xhat2)
        extra = norm_back(xhat2, scale2, vectors_ref[2:3], total)
        grad_one = jnp.concatenate([grad_one[0:block] + extra, grad_one[block:]], axis=0)
    branch = grad_one.astype(BF16)
    grad_w_out[...] += dot_tn(att_ref[...], branch)
    grad_att = dot_nt(branch, w_out_ref[...]).astype(BF16)
    packed = qkv_ref[...]
    queries, keys, values = (head_parts(packed, part, group, head) for part in range(3))
    grads = [
        grad_att[low : low + group, h * head : (h + 1) * head] for low in range(0, cells, group) for h in range(HEADS)
    ]
    probs_b = probs_ref[...].reshape(len(grads), group, group)
    probs = probs_b.astype(F32)
    grad_probs = jnp.stack([dot_nt(value, grad) for value, grad in zip(values, grads)])
    grad_scores = probs * (grad_probs - jnp.sum(grad_probs * probs, axis=1, keepdims=True))
    grad_scores = grad_scores.astype(BF16)
    grad_queries = join_parts([dot_tn(grad_scores[at], key) for at, key in enumerate(keys)]) * (head**-0.5)
    grad_keys = join_parts([dot_nn(grad_scores[at], query) for at, query in enumerate(queries)]) * (head**-0.5)
    grad_values = join_parts([dot_nn(probs_b[at], grad) for at, grad in enumerate(grads)])
    grad_qkv = jnp.concatenate(
        [grad_queries.astype(BF16), grad_keys.astype(BF16), grad_values.astype(BF16)], axis=1
    )
    at = 0 if first else (step + 1) * rows
    start, absent = start_cells(cells_ref[...], mask_ref[...], at, vectors_ref[0:1])
    xhat, scale = normalize(start)
    gain = vectors_ref[1:2]
    grad_w_qkv[...] += dot_tn((xhat * gain).astype(BF16), grad_qkv)
    grad_normed = dot_nt(grad_qkv, w_qkv_ref[...])
    gain_acc[0] += column_sum(grad_normed * xhat)
    grad_start = (grad_one + norm_back(xhat, scale, gain, grad_normed)).reshape(rows, features, width)
    grad_cells_ref[...] = jnp.where(absent, 0.0, grad_start)
    gain_acc[1] += column_sum(jnp.where(absent, grad_start, 0.0).reshape(cells, width))

    @pl.when(step == pl.num_programs(0) - 1)
    def _():
        if first and fast:
            gains_ref[...] = jnp.zeros_like(gains_ref)
            sums = [jnp.sum(gain_acc[at], axis=0, keepdims=True) for at in range(4)]
            columns[...] = jnp.concatenate(sums + [jnp.zeros((124, width), F32)], axis=0).T
            emit(idx_ref, outs[0], outs[1], [(grad_w_qkv, 0), (grad_w_out, 3 * width), (columns, 4 * width)])
        else:
            gains_ref[...] = gain_acc[0 : gains_ref.shape[0]]
            outs[0][...] = grad_w_qkv[...]
            outs[1][...] = grad_w_out[...]


def whole(array):
    zeros = (0,) * array.ndim
    return pl.BlockSpec(array.shape, lambda i: zeros, pipeline_mode=pl.Buffered(1))


def whole_out(shape):
    zeros = (0,) * len(shape)
    return pl.BlockSpec(shape, lambda i: zeros, pipeline_mode=pl.Buffered(1))


def tiles(shape, axis, offset=0):
    def index(i):
        return tuple(i + offset if d == axis else 0 for d in range(len(shape)))

    return pl.BlockSpec(shape, index)


SCALARS = pl.BlockSpec(memory_space=pltpu.SMEM)
UNTOUCHED = pl.BlockSpec(memory_space=pl.ANY)


def struct(shape, dtype):
    return jax.ShapeDtypeStruct(shape, dtype)


def call(kernel, name, grid, args, in_specs, outs, out_specs, scratch, flops, aliases=None):
    sizes = [a.size * a.dtype.itemsize for a in args] + [o.size * o.dtype.itemsize for o in outs]
    return pl.pallas_call(
        kernel,
        grid=(grid,),
        in_specs=in_specs,
        out_shape=outs,
        out_specs=out_specs,
        scratch_shapes=scratch,
        input_output_aliases=aliases or {},
        compiler_params=pltpu.CompilerParams(vmem_limit_bytes=VMEM_LIMIT, dimension_semantics=("arbitrary",)),
        cost_estimate=pl.CostEstimate(flops=int(flops), bytes_accessed=int(sum(sizes)), transcendentals=0),
        name=name,
    )(*args)


def xor_pairs(size, bit):
    return [(i, i ^ bit) for i in range(size)]


def swap(array, axis, size, bit):
    return lax.ppermute(array, axis, xor_pairs(size, bit))


def add_all(terms):
    total = terms[0].astype(F32)
    for term in terms[1:]:
        total = total + term.astype(F32)
    return total.astype(BF16)


def reduce_shares(keep, send, tabs, blocks):
    lines = blocks // 2
    got = swap(send, "rows", blocks, 1)
    parts = [add_all([keep[u], got[u]]) for u in range(tabs)]
    parts = [parts[0]] + [swap(parts[u], "tab", tabs, u) for u in range(1, tabs)]
    rows = [add_all([part[q] for part in parts]) for q in range(lines)]
    rows = [rows[0]] + [swap(rows[q], "rows", blocks, 2 * q) for q in range(1, lines)]
    own = add_all(rows)
    return [own] + [swap(own, "tab", tabs, u) for u in range(1, tabs)]


def place_kernel(tabs, moves, *refs):
    idx_ref, ins, outs = refs[0], refs[1 : 1 + tabs], refs[1 + tabs :]
    tab = idx_ref[0]
    for out, (count, column) in zip(outs, moves):
        width = out.shape[1]
        for u in range(tabs):
            rows = ins[u].shape[0]
            for at in range(count):
                low = pl.multiple_of(((tab ^ u) * count + at) * rows, 16)
                out[pl.ds(low, rows), :] = ins[u][:, column + at * width : column + (at + 1) * width].astype(F32)


def place(idx, pieces, moves, outs, tabs, name):
    return call(
        functools.partial(place_kernel, tabs, moves),
        name,
        1,
        [idx] + pieces,
        [SCALARS] + [whole(a) for a in pieces],
        outs,
        [whole_out(o.shape) for o in outs],
        [],
        0,
    )


def per_device(
    tabs,
    blocks,
    cells,
    missing_mask,
    context_counts,
    missing_embedding,
    gain_feature,
    w_feature_qkv,
    w_feature_out,
    gain_row,
    w_row_qkv,
    w_row_out,
    gain_mlp,
    w_up,
    w_down,
    upstream,
):
    _, rows, features, width = cells.shape
    hidden = w_up.shape[1]
    keys = CTX_DEV * blocks
    cells, mask, upstream = cells[0], jnp.swapaxes(missing_mask[0], 0, 1), upstream[0]
    vectors = jnp.stack([missing_embedding, gain_feature, gain_row, gain_mlp]).astype(F32)
    all_cells = rows * features
    cost = all_cells * width * width
    fast = tabs == 4 and blocks == 8 and width % (16 * tabs * blocks) == 0 and hidden % (16 * tabs * blocks) == 0
    idx = jnp.stack([lax.axis_index("tab"), lax.axis_index("rows")]).astype(jnp.int32)

    block = CTX_DEV * features
    piece_rows = block + 16
    payload, after_ctx = call(
        context_kernel,
        "context_rows",
        1,
        [context_counts, cells, mask, vectors, w_feature_qkv, w_feature_out],
        [SCALARS, pl.BlockSpec((CTX_DEV, features, width), lambda i: (0, 0, 0))]
        + [whole(a) for a in (mask, vectors, w_feature_qkv, w_feature_out)],
        [struct((piece_rows, width), BF16), struct((block, width), F32)],
        [whole_out((piece_rows, width)), whole_out((block, width))],
        [],
        2 * block * width * 4 * width,
    )
    if fast:
        mine = jnp.concatenate([payload] + [swap(payload, "rows", blocks, 2 * q) for q in range(1, blocks // 2)])
        gathered = [mine, swap(mine, "rows", blocks, 1)]
    else:
        gathered = [lax.all_gather(payload, "rows", axis=0, tiled=True)]

    tile = min(32, rows)
    steps = rows // tile
    groups = tile // GROUP_ROWS
    group = GROUP_ROWS * features
    after_one, upstream_t, qkv, probs, att = call(
        feature_kernel,
        "feature_forward",
        steps,
        [cells, mask, upstream, vectors, w_feature_qkv, w_feature_out],
        [tiles((tile, features, width), 0), whole(mask), tiles((tile, features, width), 0)]
        + [whole(a) for a in (vectors, w_feature_qkv, w_feature_out)],
        [
            struct((features, rows, width), F32),
            struct((features, rows, width), BF16),
            struct((all_cells, 3 * width), BF16),
            struct((rows // GROUP_ROWS, HEADS, group, group), BF16),
            struct((all_cells, width), BF16),
        ],
        [
            tiles((features, tile, width), 1),
            tiles((features, tile, width), 1),
            tiles((tile * features, 3 * width), 0),
            tiles((groups, HEADS, group, group), 0),
            tiles((tile * features, width), 0),
        ],
        [],
        2 * 5 * cost,
    )

    feats = 4
    cell_tile = (feats, rows, width)
    full = [struct(s, F32) for s in ((width, hidden), (hidden, width), (width, 3 * width), (width, width))]
    share_width = (2 * hidden // width + 4) * width
    shares = [struct((tabs, blocks // 2, 16, share_width), BF16)] * 2 if fast else full
    weights = [vectors, w_row_qkv, w_row_out, w_up, w_down]
    output_t, grad_after, row_gains, slot_parts, *row_shares = call(
        functools.partial(rows_kernel, len(gathered), fast),
        "rows_and_feed_forward",
        features // feats,
        [idx, after_one, upstream_t] + weights + gathered,
        [SCALARS] + [tiles(cell_tile, 0)] * 2 + [whole(a) for a in weights + gathered],
        [
            struct((features, rows, width), BF16),
            struct((features, rows, width), F32),
            struct((2, 8, width), F32),
            struct((keys * features, width), BF16),
        ]
        + shares,
        [tiles(cell_tile, 0)] * 2
        + [whole_out((2, 8, width)), whole_out((keys * features, width))]
        + [whole_out(s.shape) for s in shares],
        [pltpu.VMEM(s.shape, F32) for s in (full if fast else [])]
        + [pltpu.VMEM(s, F32) for s in ((features, keys, width), (HEADS * keys, 128), (2, 8, width))],
        2 * 34 * cost,
    )
    own_slots = lax.psum_scatter(slot_parts, "rows", scatter_dimension=0, tiled=True)

    def feature_backward(first, count, offset, extra, extra_specs, gains, share_outs, aliases):
        weights = [mask, vectors, w_feature_qkv, w_feature_out]
        args = ([idx] if first else []) + [cells] + weights + [grad_after, qkv, probs, att, output_t] + extra
        specs = ([SCALARS] if first else []) + [tiles((tile, features, width), 0, offset)] + [whole(a) for a in weights]
        specs += [
            tiles((features, tile, width), 1, offset),
            tiles((tile * features, 3 * width), 0, offset),
            tiles((groups, HEADS, group, group), 0, offset),
            tiles((tile * features, width), 0, offset),
            tiles((features, tile, width), 1, offset),
        ] + extra_specs
        return call(
            functools.partial(feature_backward_kernel, first, fast),
            "feature_backward_first" if first else "feature_backward_rest",
            count,
            args,
            specs,
            [struct((rows, features, width), BF16), struct((rows, features, width), F32), struct((gains, 8, width), F32)]
            + share_outs,
            [tiles((tile, features, width), 0, offset)] * 2
            + [whole_out((gains, 8, width))]
            + [whole_out(s.shape) for s in share_outs],
            [pltpu.VMEM(s, F32) for s in ((width, 3 * width), (width, width), (4, 8, width), (width, 128))],
            2 * 10 * cost * count / steps,
            aliases,
        )

    full = [struct((width, 3 * width), F32), struct((width, width), F32)]
    output, grad_cells, gains, grad_qkv, grad_out = feature_backward(False, steps - 1, 1, [], [], 2, full, None)
    extra = [grad_qkv, grad_out, gains, row_gains, output, grad_cells, after_ctx, own_slots]
    extra_specs = [whole(a) for a in extra[:4]] + [UNTOUCHED, UNTOUCHED] + [whole(a) for a in extra[6:]]
    first_outs = [struct((tabs, blocks // 2, 16, 4 * width + 128), BF16)] * 2 if fast else full
    output, grad_cells, gains, *feature_shares = feature_backward(
        True, 1, 0, extra, extra_specs, 4, first_outs, {11 + 4: 0, 11 + 5: 1}
    )

    if fast:
        shard = lambda height, columns: struct((height // blocks, columns), F32)
        pieces = reduce_shares(*row_shares, tabs, blocks)
        moves = [(1, 0), (1, hidden), (1, hidden + 3 * width), (hidden // width, hidden + 4 * width)]
        outs = [shard(width, hidden), shard(width, 3 * width), shard(width, width), shard(hidden, width)]
        grad_up, grad_row_qkv, grad_row_out, grad_down = place(idx, pieces, moves, outs, tabs, "place_rows")
        pieces = reduce_shares(*feature_shares, tabs, blocks)
        moves = [(1, 0), (1, 3 * width), (1, 4 * width)]
        outs = [shard(width, 3 * width), shard(width, width), shard(width, 128)]
        grad_feature_qkv, grad_feature_out, columns = place(idx, pieces, moves, outs, tabs, "place_features")
        sums = columns.T
    else:
        scatter = lambda a, axis: lax.psum_scatter(a, "rows", scatter_dimension=axis, tiled=True)
        sums = lax.psum(scatter(jnp.sum(gains, axis=1), 1), "tab")
        weights = lax.psum([scatter(w, 0) for w in row_shares + feature_shares], "tab")
        grad_up, grad_down, grad_row_qkv, grad_row_out, grad_feature_qkv, grad_feature_out = weights
    return (
        output[None],
        grad_cells[None],
        sums[1],
        sums[0],
        grad_feature_qkv,
        grad_feature_out,
        sums[2],
        grad_row_qkv,
        grad_row_out,
        sums[3],
        grad_up,
        grad_down,
    )


def solution(mesh):
    in_specs = (
        P("tab", "rows", None, None),
        P("tab", "rows", None),
        P("tab", "rows"),
        P(),
        P(),
        P(),
        P(),
        P(),
        P(),
        P(),
        P(),
        P(),
        P(),
        P("tab", "rows", None, None),
    )
    out_specs = (
        P("tab", "rows", None, None),
        P("tab", "rows", None, None),
        P("rows"),
        P("rows"),
        P("rows", None),
        P("rows", None),
        P("rows"),
        P("rows", None),
        P("rows", None),
        P("rows"),
        P("rows", None),
        P("rows", None),
    )
    return jax.shard_map(
        functools.partial(per_device, mesh.shape["tab"], mesh.shape["rows"]),
        mesh=mesh,
        in_specs=in_specs,
        out_specs=out_specs,
        check_vma=False,
    )
```

```python
import functools
import math

import jax
import jax.numpy as jnp
from jax import lax
from jax.experimental import pallas as pl
from jax.experimental.pallas import tpu as pltpu
from jax.sharding import PartitionSpec as P

HEADS = 4
CTX_DEV = 4
EPSILON = 1e-05
MASKED = -1e30
F32 = jnp.float32
BF16 = jnp.bfloat16
GROUP_ROWS = 8
MIB = 1024 * 1024
VMEM_LIMIT = 24 * MIB


def dot_nn(left, right):
    return lax.dot_general(left, right, (((1,), (0,)), ((), ())), preferred_element_type=F32)


def dot_nt(left, right):
    return lax.dot_general(left, right, (((1,), (1,)), ((), ())), preferred_element_type=F32)


def dot_tn(left, right):
    return lax.dot_general(left, right, (((0,), (0,)), ((), ())), preferred_element_type=F32)


def normalize(tensor):
    row_mean = jnp.mean(tensor, axis=-1, keepdims=True)
    centred = tensor - row_mean
    scale = lax.rsqrt(jnp.mean(centred * centred, axis=-1, keepdims=True) + EPSILON)
    return centred * scale, scale


def norm_back(xhat, scale, gain, gradient):
    scaled = gradient * gain
    first = jnp.mean(scaled, axis=-1, keepdims=True)
    second = jnp.mean(scaled * xhat, axis=-1, keepdims=True)
    return scale * (scaled - first - xhat * second)


def column_sum(tensor):
    rows, width = tensor.shape
    return jnp.sum(tensor.reshape(rows // 8, 8, width), axis=0)


def missing_column(mask, first, rows):
    features, lanes = mask.shape
    shape = (rows, features, lanes)
    pick = lax.broadcasted_iota(jnp.int32, shape, 2) == first + lax.broadcasted_iota(jnp.int32, shape, 0)
    spread = jnp.broadcast_to(mask.astype(F32)[None], shape)
    return jnp.sum(jnp.where(pick, spread, 0.0), axis=-1, keepdims=True)


def vector(ref, at):
    count = ref.shape[0] // 4
    return jnp.concatenate([ref[at * count + i : at * count + i + 1, :] for i in range(count)], axis=1)


def start_cells(cells, mask, first, missing):
    rows, features, width = cells.shape
    absent = missing_column(mask, first, rows) > 0.5
    return jnp.where(absent, missing.reshape(1, 1, width), cells.astype(F32)).reshape(rows * features, width), absent


def same_row_bias(size, features):
    shape = (size, size)
    left = lax.broadcasted_iota(jnp.int32, shape, 0) // features
    right = lax.broadcasted_iota(jnp.int32, shape, 1) // features
    return jnp.where(left == right, 0.0, MASKED)


def head_parts(packed, part, group, head):
    cells, width = packed.shape[0], packed.shape[1] // 3
    return [
        packed[low : low + group, part * width + h * head : part * width + (h + 1) * head]
        for low in range(0, cells, group)
        for h in range(HEADS)
    ]


def join_parts(parts):
    rows = [jnp.concatenate(parts[at : at + HEADS], axis=1) for at in range(0, len(parts), HEADS)]
    return jnp.concatenate(rows, axis=0)


def softmax_keys(scores):
    exp_terms = jnp.exp(scores - jnp.max(scores, axis=1, keepdims=True))
    return exp_terms * (1.0 / jnp.sum(exp_terms, axis=1, keepdims=True))


def feature_forward(start, gain, w_qkv, w_out, features, group):
    cells, width = start.shape
    head = width // HEADS
    xhat, _ = normalize(start)
    qkv = dot_nn((xhat * gain).astype(BF16), w_qkv).astype(BF16)
    queries, keys, values = (head_parts(qkv, part, group, head) for part in range(3))
    scores = jnp.stack([dot_nt(key, query) for key, query in zip(keys, queries)])
    probs = softmax_keys(scores * (head**-0.5) + same_row_bias(group, features)[None]).astype(BF16)
    att = join_parts([dot_tn(probs[at], value).astype(BF16) for at, value in enumerate(values)])
    return start + dot_nn(att, w_out), qkv, probs, att


def context_kernel(count_ref, cells_ref, mask_ref, vectors_ref, w_qkv_ref, w_out_ref, send_ref, after_ref):
    rows, features, width = cells_ref.shape
    cells = rows * features
    start, _ = start_cells(cells_ref[...], mask_ref[...], 0, vector(vectors_ref, 0))
    after, _, _, _ = feature_forward(start, vector(vectors_ref, 1), w_qkv_ref[...], w_out_ref[...], features, cells)
    after_ref[...] = after
    xhat, _ = normalize(after)
    send_ref[0:cells, :] = (xhat * vector(vectors_ref, 2)).astype(BF16)
    count = count_ref[0, 0].astype(F32)
    send_ref[cells : cells + 16, :] = jnp.full((16, width), count, F32).astype(BF16)


def feature_kernel(
    cells_ref, mask_ref, upstream_ref, vectors_ref, w_qkv_ref, w_out_ref,
    after_ref, upstream_t_ref, qkv_ref, probs_ref, att_ref,
):
    rows, features, width = cells_ref.shape
    start, _ = start_cells(cells_ref[...], mask_ref[...], pl.program_id(0) * rows, vector(vectors_ref, 0))
    after, qkv, probs, att = feature_forward(
        start, vector(vectors_ref, 1), w_qkv_ref[...], w_out_ref[...], features, GROUP_ROWS * features
    )
    qkv_ref[...] = qkv
    probs_ref[...] = probs.reshape(probs_ref.shape)
    att_ref[...] = att
    after_ref[...] = jnp.swapaxes(after.reshape(rows, features, width), 0, 1)
    upstream_t_ref[...] = jnp.swapaxes(upstream_ref[...].astype(F32), 0, 1).astype(BF16)


def head_blocks(tensor):
    keys, width = tensor.shape
    tiled = jnp.concatenate([tensor] * HEADS, axis=0)
    row_head = lax.broadcasted_iota(jnp.int32, tiled.shape, 0) // keys
    lane_head = lax.broadcasted_iota(jnp.int32, tiled.shape, 1) // (width // HEADS)
    return jnp.where(row_head == lane_head, tiled, jnp.zeros_like(tiled))


def own_heads(tensor, keys):
    head = tensor.shape[1] // HEADS
    return jnp.concatenate([tensor[h * keys : (h + 1) * keys, h * head : (h + 1) * head] for h in range(HEADS)], axis=1)


def gelu_parts(inner):
    const = 0.7978845608028654
    cubic = const * 0.044715
    square = inner * inner
    half = 0.5 + 0.5 * jnp.tanh(inner * (const + cubic * square))
    hidden = inner * half
    slope = half + (hidden - hidden * half) * (2.0 * const + (6.0 * cubic) * square)
    return hidden, slope


def read_slots(gathered, idx_ref, slots_ref, bias_ref, features):
    keys, width = slots_ref.shape[1], slots_ref.shape[2]
    blocks = keys // CTX_DEV
    block = CTX_DEV * features
    piece = block + 16
    slot = lax.broadcasted_iota(jnp.int32, (keys, 128), 0)
    counts = jnp.zeros((keys, 128), F32)
    core, line = idx_ref[1] % 2, idx_ref[1] // 2
    for pair in range(blocks // 2):
        if len(gathered) == 2:
            mine, other = (ref[pair * piece : (pair + 1) * piece, :].astype(F32) for ref in gathered)
            even, odd = jnp.where(core == 0, mine, other), jnp.where(core == 0, other, mine)
            at = line ^ pair
        else:
            even, odd = (gathered[0][(2 * pair + j) * piece : (2 * pair + j + 1) * piece, :].astype(F32) for j in range(2))
            at = pair
        both = jnp.concatenate([even[0:block], odd[0:block]], axis=0).reshape(2 * CTX_DEV, features, width)
        slots_ref[:, pl.ds(pl.multiple_of(at * 2 * CTX_DEV, 2 * CTX_DEV), 2 * CTX_DEV), :] = jnp.swapaxes(both, 0, 1)
        for j, part in enumerate((even, odd)):
            counts = jnp.where(slot // CTX_DEV == 2 * at + j, part[block : block + 1, 0:128], counts)
    bias = jnp.where((slot % CTX_DEV).astype(F32) < counts, 0.0, MASKED)
    bias_ref[...] = jnp.concatenate([bias] * HEADS, axis=0)


def emit(idx_ref, keep_ref, send_ref, sources):
    tab, block = idx_ref[0], idx_ref[1]
    core, line = block % 2, block // 2
    tabs, lines, rows, _ = keep_ref.shape
    for u in range(tabs):
        for q in range(lines):
            for ref, shard in ((keep_ref, core), (send_ref, 1 - core)):
                for acc, column in sources:
                    height, width = acc.shape
                    part = height // (2 * lines * tabs)
                    low = (((line ^ q) * 2 + shard) * tabs + (tab ^ u)) * part
                    for at in range(part // rows):
                        low_at = pl.multiple_of(low + at * rows, rows)
                        ref[u, q, :, column + at * width : column + (at + 1) * width] = acc[pl.ds(low_at, rows), :].astype(BF16)


def rows_kernel(pieces, fast, *refs):
    (idx_ref, after_ref, upstream_ref, vectors_ref, w_row_ref, w_out_ref, w_up_hbm, w_down_hbm), refs = refs[:8], refs[8:]
    gathered, refs = refs[:pieces], refs[pieces:]
    (output_ref, grad_after_ref, gains_ref, slot_out), refs = refs[:4], refs[4:]
    if fast:
        outs, refs = refs[:2], refs[2:]
        stages, copies, refs = refs[-5:-1], refs[-1], refs[:-5]
    *refs, w_up_ref, w_down_ref, loads = refs
    grad_up, grad_down, grad_qkv, grad_out, slots_ref, bias_ref, gain_acc = refs
    feats, rows, width = after_ref.shape
    features, keys, _ = slots_ref.shape
    hidden_all = w_up_ref.shape[1]
    cells = feats * rows
    head = width // HEADS
    step = pl.program_id(0)
    gain_row, gain_mlp = vector(vectors_ref, 2), vector(vectors_ref, 3)

    last = pl.num_programs(0) - 1
    fetches = [
        pltpu.make_async_copy(source, target, loads.at[at])
        for at, (source, target) in enumerate(((w_up_hbm, w_up_ref), (w_down_hbm, w_down_ref)))
    ]

    @pl.when(step == 0)
    def _():
        for fetch in fetches:
            fetch.start()
        read_slots(gathered, idx_ref, slots_ref, bias_ref, features)
        for ref in (grad_qkv, grad_out, grad_up, grad_down, gain_acc):
            ref[...] = jnp.zeros_like(ref)

    after = after_ref[...].reshape(cells, width)
    xhat2, scale2 = normalize(after)
    normed_two = (xhat2 * gain_row).astype(BF16)
    query = dot_nn(normed_two, w_row_ref[:, 0:width]).astype(BF16)
    slots = slots_ref[pl.ds(step * feats, feats)].reshape(feats * keys, width).astype(BF16)
    kv = dot_nn(slots, w_row_ref[:, width : 3 * width]).astype(BF16)
    keys_b = [head_blocks(kv[f * keys : (f + 1) * keys, 0:width]) for f in range(feats)]
    values_b = [head_blocks(kv[f * keys : (f + 1) * keys, width : 2 * width]) for f in range(feats)]
    query_f = [query[f * rows : (f + 1) * rows] for f in range(feats)]
    scores = jnp.stack([dot_nt(keys_b[f], query_f[f]) for f in range(feats)])
    scores = scores * (head**-0.5) + bias_ref[:, 0:rows][None]
    probs = softmax_keys(scores.reshape(feats * HEADS, keys, rows))
    probs_b = probs.reshape(feats, HEADS * keys, rows).astype(BF16)
    att = jnp.concatenate([dot_tn(probs_b[f], values_b[f]).astype(BF16) for f in range(feats)], axis=0)
    after_two = after + dot_nn(att, w_out_ref[...])

    @pl.when(step == 0)
    def _():
        for fetch in fetches:
            fetch.wait()

    xhat3, scale3 = normalize(after_two)
    normed_three = (xhat3 * gain_mlp).astype(BF16)
    upstream = upstream_ref[...].reshape(cells, width)
    total, grad3 = after_two, None
    piece = 512
    for at in range(0, hidden_all, piece):
        w_up = w_up_ref[:, at : at + piece]
        w_down = w_down_ref[at : at + piece, :]
        hidden, slope = gelu_parts(dot_nn(normed_three, w_up))
        hidden = hidden.astype(BF16)
        grad_inner = (dot_nt(upstream, w_down) * slope).astype(BF16)
        total = total + dot_nn(hidden, w_down)
        back = dot_nt(grad_inner, w_up)
        grad3 = back if grad3 is None else grad3 + back
        grad_down[at : at + piece, :] += dot_tn(hidden, upstream)
        grad_up[:, at : at + piece] += dot_tn(normed_three, grad_inner)
    output_ref[...] = total.astype(BF16).reshape(feats, rows, width)
    gain_acc[0] += column_sum(grad3 * xhat3)
    grad_two = upstream.astype(F32) + norm_back(xhat3, scale3, gain_mlp, grad3)

    if fast:
        wide, narrow = stages[0].shape[-1], stages[2].shape[-1]
        sends = [
            pltpu.make_async_copy(stage, out.at[:, :, :, low : low + width_of], copies.at[at])
            for at, (stage, out, low, width_of) in enumerate(
                (
                    (stages[0], outs[0], 0, wide),
                    (stages[1], outs[1], 0, wide),
                    (stages[2], outs[0], wide, narrow),
                    (stages[3], outs[1], wide, narrow),
                )
            )
        ]

        @pl.when(step == last)
        def _():
            emit(idx_ref, stages[0], stages[1], [(grad_up, 0), (grad_down, hidden_all)])
            sends[0].start()
            sends[1].start()

    branch = grad_two.astype(BF16)
    grad_out[...] += dot_tn(att, branch)
    grad_att = dot_nt(branch, w_out_ref[...]).astype(BF16)
    grad_f = [grad_att[f * rows : (f + 1) * rows] for f in range(feats)]
    grad_probs = jnp.stack([dot_nt(values_b[f], grad_f[f]) for f in range(feats)]).reshape(feats * HEADS, keys, rows)
    grad_scores = probs * (grad_probs - jnp.sum(grad_probs * probs, axis=1, keepdims=True))
    grad_scores = grad_scores.reshape(feats, HEADS * keys, rows).astype(BF16)
    grad_query = jnp.concatenate([dot_tn(grad_scores[f], keys_b[f]) for f in range(feats)], axis=0)
    grad_query = (grad_query * (head**-0.5)).astype(BF16)
    grad_keys = [own_heads(dot_nn(grad_scores[f], query_f[f]), keys) for f in range(feats)]
    grad_values = [own_heads(dot_nn(probs_b[f], grad_f[f]), keys) for f in range(feats)]
    grad_kv = jnp.concatenate(
        [jnp.concatenate(grad_keys, axis=0) * (head**-0.5), jnp.concatenate(grad_values, axis=0)], axis=1
    ).astype(BF16)
    grad_qkv[:, 0:width] += dot_tn(normed_two, grad_query)
    grad_qkv[:, width : 3 * width] += dot_tn(slots, grad_kv)
    slots_ref[pl.ds(step * feats, feats)] = dot_nt(grad_kv, w_row_ref[:, width : 3 * width]).reshape(feats, keys, width)
    grad_normed = dot_nt(grad_query, w_row_ref[:, 0:width])
    gain_acc[1] += column_sum(grad_normed * xhat2)
    grad_after_ref[...] = (grad_two + norm_back(xhat2, scale2, gain_row, grad_normed)).reshape(feats, rows, width)

    @pl.when(step == last)
    def _():
        if fast:
            emit(idx_ref, stages[2], stages[3], [(grad_qkv, 0), (grad_out, 3 * width)])
            sends[2].start()
            sends[3].start()
        gains_ref[...] = gain_acc[...]
        block = CTX_DEV * features
        for at in range(0, keys, 2 * CTX_DEV):
            both = jnp.swapaxes(slots_ref[:, at : at + 2 * CTX_DEV, :], 0, 1).reshape(2 * block, width)
            slot_out[at * features : at * features + 2 * block, :] = both.astype(BF16)
        if fast:
            for send in sends:
                send.wait()


def feature_backward(grad_one, packed, probs_b, att, start, gain, w_qkv, w_out, group):
    cells, width = start.shape
    head = width // HEADS
    branch = grad_one.astype(BF16)
    grad_w_out = dot_tn(att, branch)
    grad_att = dot_nt(branch, w_out).astype(BF16)
    queries, keys, values = (head_parts(packed, part, group, head) for part in range(3))
    grads = [
        grad_att[low : low + group, h * head : (h + 1) * head] for low in range(0, cells, group) for h in range(HEADS)
    ]
    probs = probs_b.astype(F32)
    grad_probs = jnp.stack([dot_nt(value, grad) for value, grad in zip(values, grads)])
    grad_scores = probs * (grad_probs - jnp.sum(grad_probs * probs, axis=1, keepdims=True))
    grad_scores = grad_scores.astype(BF16)
    grad_queries = join_parts([dot_tn(grad_scores[at], key) for at, key in enumerate(keys)]) * (head**-0.5)
    grad_keys = join_parts([dot_nn(grad_scores[at], query) for at, query in enumerate(queries)]) * (head**-0.5)
    grad_values = join_parts([dot_nn(probs_b[at], grad) for at, grad in enumerate(grads)])
    grad_qkv = jnp.concatenate([grad_queries.astype(BF16), grad_keys.astype(BF16), grad_values.astype(BF16)], axis=1)
    xhat, scale = normalize(start)
    grad_w_qkv = dot_tn((xhat * gain).astype(BF16), grad_qkv)
    grad_normed = dot_nt(grad_qkv, w_qkv)
    grad_start = grad_one + norm_back(xhat, scale, gain, grad_normed)
    return grad_w_qkv, grad_w_out, column_sum(grad_normed * xhat), grad_start


def feature_backward_kernel(waits, *refs):
    (
        cells_ref, mask_ref, vectors_ref, w_qkv_ref, w_out_ref, grad_after_ref, qkv_ref, probs_ref, att_ref,
    ), refs = refs[:9], refs[9 + waits :]
    grad_cells_ref, grad_w_qkv, grad_w_out, gains = refs
    rows, features, width = cells_ref.shape
    cells = rows * features
    group = GROUP_ROWS * features
    step = pl.program_id(0)

    @pl.when(step == 0)
    def _():
        for ref in (grad_w_qkv, grad_w_out, gains):
            ref[...] = jnp.zeros_like(ref)

    grad_one = jnp.swapaxes(grad_after_ref[...], 0, 1).reshape(cells, width)
    cell = lax.broadcasted_iota(jnp.int32, (cells, 1), 0) + step * cells
    grad_one = jnp.where(cell < CTX_DEV * features, 0.0, grad_one)
    start, absent = start_cells(cells_ref[...], mask_ref[...], step * rows, vector(vectors_ref, 0))
    add_qkv, add_out, add_gain, grad_start = feature_backward(
        grad_one, qkv_ref[...], probs_ref[...].reshape(cells // group * HEADS, group, group), att_ref[...],
        start, vector(vectors_ref, 1), w_qkv_ref[...], w_out_ref[...], group,
    )
    grad_w_qkv[...] += add_qkv
    grad_w_out[...] += add_out
    gains[0] += add_gain
    grad_start = grad_start.reshape(rows, features, width)
    grad_cells_ref[...] = jnp.where(absent, 0.0, grad_start)
    gains[1] += column_sum(jnp.where(absent, grad_start, 0.0).reshape(cells, width))


def output_kernel(output_t_ref, output_ref):
    output_ref[...] = jnp.swapaxes(output_t_ref[...].astype(F32), 0, 1).astype(BF16)


def context_backward_kernel(fast, *refs):
    (
        idx_ref, cells_ref, mask_ref, vectors_ref, w_qkv_ref, w_out_ref, grad_after_ref, qkv_ref, probs_ref, att_ref,
        after_ref, slots_ref, sum_qkv, sum_out, sum_gains, row_gains, _,
    ), refs = refs[:17], refs[17:]
    grad_cells_ref, gains_ref, out_a, out_b, grad_w_qkv, grad_w_out, columns = refs
    rows, features, width = cells_ref.shape
    cells = rows * features
    total = slots_ref[...].astype(F32)
    xhat2, scale2 = normalize(after_ref[...])
    grad_one = jnp.swapaxes(grad_after_ref[...], 0, 1)[0:rows].reshape(cells, width)
    grad_one = grad_one + norm_back(xhat2, scale2, vector(vectors_ref, 2), total)
    start, absent = start_cells(cells_ref[...], mask_ref[...], 0, vector(vectors_ref, 0))
    add_qkv, add_out, add_gain, grad_start = feature_backward(
        grad_one, qkv_ref[...], probs_ref[0, :, 0:cells, 0:cells], att_ref[...],
        start, vector(vectors_ref, 1), w_qkv_ref[...], w_out_ref[...], cells,
    )
    grad_w_qkv[...] = sum_qkv[...] + add_qkv
    grad_w_out[...] = sum_out[...] + add_out
    grad_start = grad_start.reshape(rows, features, width)
    grad_cells_ref[...] = jnp.where(absent, 0.0, grad_start)
    gains = [
        sum_gains[0] + add_gain,
        sum_gains[1] + column_sum(jnp.where(absent, grad_start, 0.0).reshape(cells, width)),
        row_gains[1] + column_sum(total * xhat2),
        row_gains[0],
    ]
    gains = jnp.concatenate([jnp.sum(g, axis=0, keepdims=True) for g in gains], axis=0)
    gains_ref[...] = gains
    if fast:
        columns[...] = jnp.concatenate([gains, jnp.zeros((124, width), F32)], axis=0).T
        emit(idx_ref, out_a, out_b, [(grad_w_qkv, 0), (grad_w_out, 3 * width), (columns, 4 * width)])
    else:
        out_a[...] = grad_w_qkv[...]
        out_b[...] = grad_w_out[...]


def join_kernel(count, *refs):
    rows = refs[0].shape[0]
    for at in range(count):
        refs[-1][at * rows : (at + 1) * rows, :] = refs[at][...]


def sum_kernel(count, groups, *refs):
    ins, outs = refs[:count], refs[len(refs) - len(groups) :]
    for group, out in zip(groups, outs):
        for at, part in enumerate(group):
            total = ins[0][part].astype(F32)
            for ref in ins[1:]:
                total = total + ref[part].astype(F32)
            out[at] = total.astype(BF16)


def whole(array):
    zeros = (0,) * array.ndim
    return pl.BlockSpec(array.shape, lambda i: zeros, pipeline_mode=pl.Buffered(1))


def whole_out(shape):
    zeros = (0,) * len(shape)
    return pl.BlockSpec(shape, lambda i: zeros, pipeline_mode=pl.Buffered(1))


def tiles(shape, axis, offset=0):
    def index(i):
        return tuple(i + offset if d == axis else 0 for d in range(len(shape)))

    return pl.BlockSpec(shape, index)


WAITS = 1e14
SCALARS = pl.BlockSpec(memory_space=pltpu.SMEM)
UNTOUCHED = pl.BlockSpec(memory_space=pl.ANY)


def struct(shape, dtype):
    return jax.ShapeDtypeStruct(shape, dtype)


def call(kernel, name, grid, args, in_specs, outs, out_specs, scratch, flops, aliases=None, vmem=VMEM_LIMIT, pinned=True):
    small = 1 << 15
    large = lambda a: pinned and math.prod(a.shape) >= 1 << 15
    args = [pltpu.with_memory_space_constraint(a, pltpu.HBM) if large(a) else a for a in args]
    outs = [pltpu.HBM(o.shape, o.dtype) if large(o) else o for o in outs]
    sizes = [math.prod(a.shape) * a.dtype.itemsize for a in [*args, *outs]]
    return pl.pallas_call(
        kernel,
        grid=(grid,),
        in_specs=in_specs,
        out_shape=outs,
        out_specs=out_specs,
        scratch_shapes=scratch,
        input_output_aliases=aliases or {},
        compiler_params=pltpu.CompilerParams(vmem_limit_bytes=vmem, dimension_semantics=("arbitrary",)),
        cost_estimate=pl.CostEstimate(flops=int(flops), bytes_accessed=int(sum(sizes)), transcendentals=0),
        name=name,
    )(*args)


def xor_pairs(size, bit):
    return [(i, i ^ bit) for i in range(size)]


def swap(array, axis, size, bit):
    return lax.ppermute(array, axis, xor_pairs(size, bit))


def add_all(terms):
    total = terms[0].astype(F32)
    for term in terms[1:]:
        total = total + term.astype(F32)
    return total.astype(BF16)


def exchange(parts, axis, size, unit):
    return [parts[0]] + [swap(parts[at], axis, size, at * unit) for at in range(1, len(parts))]


def sum_parts(parts, groups, name, after=(), flops=WAITS):
    outs = [struct((len(group), *parts[0].shape[1:]), BF16) for group in groups]
    return call(
        functools.partial(sum_kernel, len(parts), groups),
        name,
        1,
        [*parts, *after],
        [whole(a) for a in parts] + [UNTOUCHED] * len(after),
        outs,
        [whole_out(o.shape) for o in outs],
        [],
        flops,
        pinned=False,
    )


def place_kernel(tabs, moves, *refs):
    idx_ref, ins, outs = refs[0], refs[1 : 1 + tabs], refs[len(refs) - len(moves) :]
    tab = idx_ref[0]
    for out, (count, column) in zip(outs, moves):
        width = out.shape[1]
        for u in range(tabs):
            rows = ins[u].shape[0]
            for at in range(count):
                low = pl.multiple_of(((tab ^ u) * count + at) * rows, 16)
                out[pl.ds(low, rows), :] = ins[u][:, column + at * width : column + (at + 1) * width].astype(F32)


def place(idx, pieces, moves, outs, tabs, name, after):
    return call(
        functools.partial(place_kernel, tabs, moves),
        name,
        1,
        [idx, *pieces, *after],
        [SCALARS] + [whole(a) for a in pieces] + [UNTOUCHED] * len(after),
        outs,
        [whole_out(o.shape) for o in outs],
        [],
        WAITS,
        pinned=False,
    )


def per_device(
    tabs,
    blocks,
    cells,
    missing_mask,
    context_counts,
    missing_embedding,
    gain_feature,
    w_feature_qkv,
    w_feature_out,
    gain_row,
    w_row_qkv,
    w_row_out,
    gain_mlp,
    w_up,
    w_down,
    upstream,
):
    _, rows, features, width = cells.shape
    hidden = w_up.shape[1]
    keys = CTX_DEV * blocks
    cells, mask, upstream = cells[0], jnp.swapaxes(missing_mask[0], 0, 1), upstream[0]
    vectors = jnp.concatenate([missing_embedding, gain_feature, gain_row, gain_mlp]).astype(F32).reshape(-1, 128)
    all_cells = rows * features
    cost = all_cells * width * width
    fast = tabs == 4 and blocks == 8 and width == 16 * tabs * blocks and hidden % (16 * tabs * blocks) == 0
    tall = hidden // (16 * tabs * blocks)
    idx = jnp.stack([lax.axis_index("tab"), lax.axis_index("rows")]).astype(jnp.int32)

    block = CTX_DEV * features
    piece_rows = block + 16
    payload, after_ctx = call(
        context_kernel,
        "context_rows",
        1,
        [context_counts, cells, mask, vectors, w_feature_qkv, w_feature_out],
        [SCALARS, pl.BlockSpec((CTX_DEV, features, width), lambda i: (0, 0, 0))]
        + [whole(a) for a in (mask, vectors, w_feature_qkv, w_feature_out)],
        [struct((piece_rows, width), BF16), struct((block, width), F32)],
        [whole_out((piece_rows, width)), whole_out((block, width))],
        [],
        2 * block * width * 4 * width,
    )
    if fast:
        received = exchange([payload] * (blocks // 2), "rows", blocks, 2)


    tile = min(32, rows)
    steps = rows // tile
    groups = tile // GROUP_ROWS
    group = GROUP_ROWS * features
    after_one, upstream_t, qkv, probs, att = call(
        feature_kernel,
        "feature_forward",
        steps,
        [cells, mask, upstream, vectors, w_feature_qkv, w_feature_out],
        [tiles((tile, features, width), 0), whole(mask), tiles((tile, features, width), 0)]
        + [whole(a) for a in (vectors, w_feature_qkv, w_feature_out)],
        [
            struct((features, rows, width), F32),
            struct((features, rows, width), BF16),
            struct((all_cells, 3 * width), BF16),
            struct((rows // GROUP_ROWS, HEADS, group, group), BF16),
            struct((all_cells, width), BF16),
        ],
        [
            tiles((features, tile, width), 1),
            tiles((features, tile, width), 1),
            tiles((tile * features, 3 * width), 0),
            tiles((groups, HEADS, group, group), 0),
            tiles((tile * features, width), 0),
        ],
        [],
        2 * 5 * cost,
    )

    if fast:
        mine = call(
            functools.partial(join_kernel, len(received)),
            "join",
            1,
            received + [att],
            [whole(a) for a in received] + [UNTOUCHED],
            [struct((len(received) * piece_rows, width), BF16)],
            [whole_out((len(received) * piece_rows, width))],
            [],
            0,
        )[0]
        gathered = [mine, swap(mine, "rows", blocks, 1)]
    else:
        gathered = [lax.all_gather(payload, "rows", axis=0, tiled=True)]

    feats = 4
    cell_tile = (feats, rows, width)
    full = [struct(s, F32) for s in ((width, hidden), (hidden, width), (width, 3 * width), (width, width))]
    if fast:
        shares = [struct((tabs, blocks // 2, 16, hidden + (4 + tall) * width), BF16)] * 2
        stages = [pltpu.VMEM((tabs, blocks // 2, 16, w), BF16) for w in (hidden + tall * width, 4 * width) for _ in range(2)]
        stages += [pltpu.SemaphoreType.DMA((4,))]
    else:
        shares = full
    weights = [vectors, w_row_qkv, w_row_out, w_up, w_down]
    output_t, grad_after, row_gains, slot_parts, *row_shares = call(
        functools.partial(rows_kernel, len(gathered), fast),
        "rows_and_feed_forward",
        features // feats,
        [idx, after_one, upstream_t] + weights + gathered,
        [SCALARS] + [tiles(cell_tile, 0)] * 2 + [whole(a) for a in weights[:3]] + [UNTOUCHED] * 2 + [whole(a) for a in gathered],
        [
            struct((features, rows, width), BF16),
            struct((features, rows, width), F32),
            struct((2, 8, width), F32),
            struct((keys * features, width), BF16),
        ]
        + shares,
        [tiles(cell_tile, 0)] * 2
        + [whole_out((2, 8, width)), whole_out((keys * features, width))]
        + [UNTOUCHED if fast else whole_out(s.shape) for s in shares],
        [pltpu.VMEM(s.shape, F32) for s in (full if fast else [])]
        + [pltpu.VMEM(s, F32) for s in ((features, keys, width), (HEADS * keys, 128), (2, 8, width))]
        + [pltpu.VMEM(a.shape, BF16) for a in (w_up, w_down)]
        + [pltpu.SemaphoreType.DMA((2,))]
        + (stages if fast else []),
        2 * 34 * cost,
        vmem=(48 if fast else 62) * MIB,
    )
    own_slots = lax.psum_scatter(slot_parts, "rows", scatter_dimension=0, tiled=True)

    output = call(
        output_kernel,
        "output",
        steps,
        [output_t],
        [tiles((features, tile, width), 1)],
        [struct((rows, features, width), BF16)],
        [tiles((tile, features, width), 0)],
        [],
        0,
    )[0]
    parts = []
    if fast:
        keep, send = row_shares
        got = swap(send, "rows", blocks, 1)
        parts = [add_all([keep[u], got[u]]) for u in range(tabs)]
        row_parts = exchange(parts, "tab", tabs, 1)

    weights = [mask, vectors, w_feature_qkv, w_feature_out]
    sums = [struct((width, 3 * width), F32), struct((width, width), F32), struct((2, 8, width), F32)]
    big = struct((rows, features, width), F32)
    grad_cells, *sums = call(
        functools.partial(feature_backward_kernel, 1 + len(parts[:1])),
        "feature_backward",
        steps,
        [cells] + weights + [grad_after, qkv, probs, att, output] + parts[:1],
        [tiles((tile, features, width), 0)]
        + [whole(a) for a in weights]
        + [
            tiles((features, tile, width), 1),
            tiles((tile * features, 3 * width), 0),
            tiles((groups, HEADS, group, group), 0),
            tiles((tile * features, width), 0),
        ]
        + [UNTOUCHED] * (1 + len(parts[:1])),
        [big] + sums,
        [tiles((tile, features, width), 0)] + [whole_out(s.shape) for s in sums],
        [],
        2 * 10 * cost,
        vmem=32 * MIB,
    )
    args = [idx, cells] + weights + [grad_after, qkv, probs, att, after_ctx, own_slots] + sums + [row_gains, grad_cells]
    outs = [struct((tabs, blocks // 2, 16, 4 * width + 128), BF16)] * 2 if fast else [struct(s.shape, F32) for s in sums[:2]]
    context_cells = pl.BlockSpec((CTX_DEV, features, width), lambda i: (0, 0, 0))
    grad_cells, gains, *feature_shares = call(
        functools.partial(context_backward_kernel, fast),
        "context_backward",
        1,
        args,
        [SCALARS, context_cells]
        + [whole(a) for a in weights]
        + [
            pl.BlockSpec((features, 8, width), lambda i: (0, 0, 0)),
            pl.BlockSpec((block, 3 * width), lambda i: (0, 0)),
            pl.BlockSpec((1, HEADS, group, group), lambda i: (0, 0, 0, 0)),
            pl.BlockSpec((block, width), lambda i: (0, 0)),
        ]
        + [whole(a) for a in args[10:16]]
        + [UNTOUCHED],
        [big, struct((4, width), F32)] + outs,
        [context_cells, whole_out((4, width))] + [whole_out(o.shape) for o in outs],
        [pltpu.VMEM(s, F32) for s in ((width, 3 * width), (width, width), (width, 128))],
        0,
        {16: 0},
    )

    if fast:
        shard = lambda height, columns: struct((height // blocks, columns), F32)
        keep, send = feature_shares
        got = swap(send, "rows", blocks, 1)
        one = [(q,) for q in range(blocks // 2)]
        lines = sum_parts(row_parts, one, "sum_tab_rows", [keep])
        row_parts = exchange(lines, "rows", blocks, 2)
        parts = sum_parts([keep, got], [(u,) for u in range(tabs)], "sum_core_features", [lines[0]], 0)
        parts = [part[0] for part in parts]
        lines = sum_parts(exchange(parts, "tab", tabs, 1), one, "sum_tab_features")
        parts = exchange(lines, "rows", blocks, 2)
        (own_rows,) = sum_parts(row_parts, [(0,)], "sum_rows_rows", [lines[0]])
        row_pieces = exchange([own_rows[0]] * tabs, "tab", tabs, 1)
        (own,) = sum_parts(parts, [(0,)], "sum_rows_features", [own_rows])
        pieces = exchange([own[0]] * tabs, "tab", tabs, 1)
        wide = hidden + tall * width
        moves = [(1, 0), (tall, hidden), (1, wide), (1, wide + 3 * width)]
        outs = [shard(width, hidden), shard(hidden, width), shard(width, 3 * width), shard(width, width)]
        grad_up, grad_down, grad_row_qkv, grad_row_out = place(idx, row_pieces, moves, outs, tabs, "place_rows", [])
        moves = [(1, 0), (1, 3 * width), (1, 4 * width)]
        outs = [shard(width, 3 * width), shard(width, width), shard(width, 128)]
        grad_feature_qkv, grad_feature_out, columns = place(idx, pieces, moves, outs, tabs, "place_features", [grad_up])
        gains = columns.T
    else:
        scatter = lambda a, axis: lax.psum_scatter(a, "rows", scatter_dimension=axis, tiled=True)
        gains = lax.psum(scatter(gains, 1), "tab")
        weights = lax.psum([scatter(w, 0) for w in [*row_shares, *feature_shares]], "tab")
        grad_up, grad_down, grad_row_qkv, grad_row_out, grad_feature_qkv, grad_feature_out = weights
    return (
        output[None],
        grad_cells[None],
        gains[1],
        gains[0],
        grad_feature_qkv,
        grad_feature_out,
        gains[2],
        grad_row_qkv,
        grad_row_out,
        gains[3],
        grad_up,
        grad_down,
    )


def solution(mesh):
    in_specs = (
        P("tab", "rows", None, None),
        P("tab", "rows", None),
        P("tab", "rows"),
        P(),
        P(),
        P(),
        P(),
        P(),
        P(),
        P(),
        P(),
        P(),
        P(),
        P("tab", "rows", None, None),
    )
    out_specs = (
        P("tab", "rows", None, None),
        P("tab", "rows", None, None),
        P("rows"),
        P("rows"),
        P("rows", None),
        P("rows", None),
        P("rows"),
        P("rows", None),
        P("rows", None),
        P("rows"),
        P("rows", None),
        P("rows", None),
    )
    return jax.shard_map(
        functools.partial(per_device, mesh.shape["tab"], mesh.shape["rows"]),
        mesh=mesh,
        in_specs=in_specs,
        out_specs=out_specs,
        check_vma=False,
    )
```

```python
import functools
import math

import jax
import jax.numpy as jnp
from jax import lax
from jax.experimental import pallas as pl
from jax.experimental.pallas import tpu as pltpu
from jax.sharding import PartitionSpec as P

HEADS = 4
CTX_DEV = 4
EPSILON = 1e-05
MASKED = -1e30
F32 = jnp.float32
BF16 = jnp.bfloat16
GROUP_ROWS = 8
MIB = 1024 * 1024
VMEM_LIMIT = 24 * MIB


def dot_nn(left, right):
    return lax.dot_general(left, right, (((1,), (0,)), ((), ())), preferred_element_type=F32)


def dot_nt(left, right):
    return lax.dot_general(left, right, (((1,), (1,)), ((), ())), preferred_element_type=F32)


def dot_tn(left, right):
    return lax.dot_general(left, right, (((0,), (0,)), ((), ())), preferred_element_type=F32)


def normalize(tensor):
    row_mean = jnp.mean(tensor, axis=-1, keepdims=True)
    centred = tensor - row_mean
    scale = lax.rsqrt(jnp.mean(centred * centred, axis=-1, keepdims=True) + EPSILON)
    return centred * scale, scale


def norm_back(xhat, scale, gain, gradient):
    scaled = gradient * gain
    first = jnp.mean(scaled, axis=-1, keepdims=True)
    second = jnp.mean(scaled * xhat, axis=-1, keepdims=True)
    return scale * (scaled - first - xhat * second)


def column_sum(tensor):
    rows, width = tensor.shape
    return jnp.sum(tensor.reshape(rows // 8, 8, width), axis=0)


def missing_column(mask, first, rows):
    features, lanes = mask.shape
    shape = (rows, features, lanes)
    pick = lax.broadcasted_iota(jnp.int32, shape, 2) == first + lax.broadcasted_iota(jnp.int32, shape, 0)
    spread = jnp.broadcast_to(mask.astype(F32)[None], shape)
    return jnp.sum(jnp.where(pick, spread, 0.0), axis=-1, keepdims=True)


def vector(ref, at):
    count = ref.shape[0] // 4
    return jnp.concatenate([ref[at * count + i : at * count + i + 1, :] for i in range(count)], axis=1)


def start_cells(cells, mask, first, missing):
    rows, features, width = cells.shape
    absent = missing_column(mask, first, rows) > 0.5
    return jnp.where(absent, missing.reshape(1, 1, width), cells.astype(F32)).reshape(rows * features, width), absent


def same_row_bias(size, features):
    shape = (size, size)
    left = lax.broadcasted_iota(jnp.int32, shape, 0) // features
    right = lax.broadcasted_iota(jnp.int32, shape, 1) // features
    return jnp.where(left == right, 0.0, MASKED)


def head_parts(packed, part, group, head):
    cells, width = packed.shape[0], packed.shape[1] // 3
    return [
        packed[low : low + group, part * width + h * head : part * width + (h + 1) * head]
        for low in range(0, cells, group)
        for h in range(HEADS)
    ]


def join_parts(parts):
    rows = [jnp.concatenate(parts[at : at + HEADS], axis=1) for at in range(0, len(parts), HEADS)]
    return jnp.concatenate(rows, axis=0)


def softmax_keys(scores):
    exp_terms = jnp.exp(scores - jnp.max(scores, axis=1, keepdims=True))
    return exp_terms * (1.0 / jnp.sum(exp_terms, axis=1, keepdims=True))


def feature_forward(start, gain, w_qkv, w_out, features, group):
    cells, width = start.shape
    head = width // HEADS
    xhat, _ = normalize(start)
    qkv = dot_nn((xhat * gain).astype(BF16), w_qkv).astype(BF16)
    queries, keys, values = (head_parts(qkv, part, group, head) for part in range(3))
    scores = jnp.stack([dot_nt(key, query) for key, query in zip(keys, queries)])
    probs = softmax_keys(scores * (head**-0.5) + same_row_bias(group, features)[None]).astype(BF16)
    att = join_parts([dot_tn(probs[at], value).astype(BF16) for at, value in enumerate(values)])
    return start + dot_nn(att, w_out), qkv, probs, att


def context_kernel(count_ref, cells_ref, mask_ref, vectors_ref, w_qkv_ref, w_out_ref, send_ref, after_ref):
    rows, features, width = cells_ref.shape
    cells = rows * features
    start, _ = start_cells(cells_ref[...], mask_ref[...], 0, vector(vectors_ref, 0))
    after, _, _, _ = feature_forward(start, vector(vectors_ref, 1), w_qkv_ref[...], w_out_ref[...], features, cells)
    after_ref[...] = after
    xhat, _ = normalize(after)
    send_ref[0:cells, :] = (xhat * vector(vectors_ref, 2)).astype(BF16)
    count = count_ref[0, 0].astype(F32)
    send_ref[cells : cells + 16, :] = jnp.full((16, width), count, F32).astype(BF16)


def feature_kernel(
    cells_ref, mask_ref, upstream_ref, vectors_ref, w_qkv_ref, w_out_ref,
    after_ref, upstream_t_ref, qkv_ref, probs_ref, att_ref,
):
    rows, features, width = cells_ref.shape
    start, _ = start_cells(cells_ref[...], mask_ref[...], pl.program_id(0) * rows, vector(vectors_ref, 0))
    after, qkv, probs, att = feature_forward(
        start, vector(vectors_ref, 1), w_qkv_ref[...], w_out_ref[...], features, GROUP_ROWS * features
    )
    qkv_ref[...] = qkv
    probs_ref[...] = probs.reshape(probs_ref.shape)
    att_ref[...] = att
    after_ref[...] = jnp.swapaxes(after.reshape(rows, features, width), 0, 1)
    upstream_t_ref[...] = jnp.swapaxes(upstream_ref[...].astype(F32), 0, 1).astype(BF16)


def head_blocks(tensor):
    keys, width = tensor.shape
    tiled = jnp.concatenate([tensor] * HEADS, axis=0)
    row_head = lax.broadcasted_iota(jnp.int32, tiled.shape, 0) // keys
    lane_head = lax.broadcasted_iota(jnp.int32, tiled.shape, 1) // (width // HEADS)
    return jnp.where(row_head == lane_head, tiled, jnp.zeros_like(tiled))


def own_heads(tensor, keys):
    head = tensor.shape[1] // HEADS
    return jnp.concatenate([tensor[h * keys : (h + 1) * keys, h * head : (h + 1) * head] for h in range(HEADS)], axis=1)


def gelu_parts(inner):
    const = 0.7978845608028654
    cubic = const * 0.044715
    inner = inner.astype(BF16)
    square = inner * inner
    half = 0.5 + 0.5 * jnp.tanh(inner * (const + cubic * square))
    hidden = inner * half
    slope = half + (hidden - hidden * half) * (2.0 * const + (6.0 * cubic) * square)
    return hidden, slope


def read_slots(gathered, idx_ref, slots_ref, bias_ref, features):
    keys, width = slots_ref.shape[1], slots_ref.shape[2]
    blocks = keys // CTX_DEV
    block = CTX_DEV * features
    piece = block + 16
    slot = lax.broadcasted_iota(jnp.int32, (keys, 128), 0)
    counts = jnp.zeros((keys, 128), F32)
    core, line = idx_ref[1] % 2, idx_ref[1] // 2
    for pair in range(blocks // 2):
        if len(gathered) == 2:
            mine, other = (ref[pair * piece : (pair + 1) * piece, :].astype(F32) for ref in gathered)
            even, odd = jnp.where(core == 0, mine, other), jnp.where(core == 0, other, mine)
            at = line ^ pair
        else:
            even, odd = (gathered[0][(2 * pair + j) * piece : (2 * pair + j + 1) * piece, :].astype(F32) for j in range(2))
            at = pair
        both = jnp.concatenate([even[0:block], odd[0:block]], axis=0).reshape(2 * CTX_DEV, features, width)
        slots_ref[:, pl.ds(pl.multiple_of(at * 2 * CTX_DEV, 2 * CTX_DEV), 2 * CTX_DEV), :] = jnp.swapaxes(both, 0, 1)
        for j, part in enumerate((even, odd)):
            counts = jnp.where(slot // CTX_DEV == 2 * at + j, part[block : block + 1, 0:128], counts)
    bias = jnp.where((slot % CTX_DEV).astype(F32) < counts, 0.0, MASKED)
    bias_ref[...] = jnp.concatenate([bias] * HEADS, axis=0)


def emit(idx_ref, keep_ref, send_ref, sources):
    tab, block = idx_ref[0], idx_ref[1]
    core, line = block % 2, block // 2
    tabs, lines, rows, _ = keep_ref.shape
    for u in range(tabs):
        for q in range(lines):
            for ref, shard in ((keep_ref, core), (send_ref, 1 - core)):
                for acc, column in sources:
                    height, width = acc.shape
                    part = height // (2 * lines * tabs)
                    low = (((line ^ q) * 2 + shard) * tabs + (tab ^ u)) * part
                    for at in range(part // rows):
                        low_at = pl.multiple_of(low + at * rows, rows)
                        ref[u, q, :, column + at * width : column + (at + 1) * width] = acc[pl.ds(low_at, rows), :].astype(BF16)


def rows_kernel(pieces, fast, *refs):
    (idx_ref, after_ref, upstream_ref, vectors_ref, w_row_ref, w_out_ref, w_up_hbm, w_down_hbm), refs = refs[:8], refs[8:]
    gathered, refs = refs[:pieces], refs[pieces:]
    (output_ref, grad_after_ref, gains_ref, slot_out), refs = refs[:4], refs[4:]
    if fast:
        outs, refs = refs[:2], refs[2:]
        stages, copies, refs = refs[-5:-1], refs[-1], refs[:-5]
    *refs, w_up_ref, w_down_ref, loads = refs
    grad_up, grad_down, grad_qkv, grad_out, slots_ref, bias_ref, gain_acc = refs
    feats, rows, width = after_ref.shape
    features, keys, _ = slots_ref.shape
    hidden_all = w_up_ref.shape[1]
    cells = feats * rows
    head = width // HEADS
    step = pl.program_id(0)
    gain_row, gain_mlp = vector(vectors_ref, 2), vector(vectors_ref, 3)

    last = pl.num_programs(0) - 1
    fetches = [
        pltpu.make_async_copy(source, target, loads.at[at])
        for at, (source, target) in enumerate(((w_up_hbm, w_up_ref), (w_down_hbm, w_down_ref)))
    ]

    @pl.when(step == 0)
    def _():
        for fetch in fetches:
            fetch.start()
        read_slots(gathered, idx_ref, slots_ref, bias_ref, features)
        for ref in (grad_qkv, grad_out, grad_up, grad_down, gain_acc):
            ref[...] = jnp.zeros_like(ref)

    after = after_ref[...].reshape(cells, width)
    xhat2, scale2 = normalize(after)
    normed_two = (xhat2 * gain_row).astype(BF16)
    query = dot_nn(normed_two, w_row_ref[:, 0:width]).astype(BF16)
    slots = slots_ref[pl.ds(step * feats, feats)].reshape(feats * keys, width).astype(BF16)
    kv = dot_nn(slots, w_row_ref[:, width : 3 * width]).astype(BF16)
    keys_b = [head_blocks(kv[f * keys : (f + 1) * keys, 0:width]) for f in range(feats)]
    values_b = [head_blocks(kv[f * keys : (f + 1) * keys, width : 2 * width]) for f in range(feats)]
    query_f = [query[f * rows : (f + 1) * rows] for f in range(feats)]
    scores = jnp.stack([dot_nt(keys_b[f], query_f[f]) for f in range(feats)])
    scores = scores * (head**-0.5) + bias_ref[:, 0:rows][None]
    probs = softmax_keys(scores.reshape(feats * HEADS, keys, rows))
    probs_b = probs.reshape(feats, HEADS * keys, rows).astype(BF16)
    att = jnp.concatenate([dot_tn(probs_b[f], values_b[f]).astype(BF16) for f in range(feats)], axis=0)
    after_two = after + dot_nn(att, w_out_ref[...])

    @pl.when(step == 0)
    def _():
        for fetch in fetches:
            fetch.wait()

    xhat3, scale3 = normalize(after_two)
    normed_three = (xhat3 * gain_mlp).astype(BF16)
    upstream = upstream_ref[...].reshape(cells, width)
    piece = 256
    hidden, grad_inner = [], []
    first = lambda at: (dot_nn(normed_three, w_up_ref[:, at : at + piece]), dot_nt(upstream, w_down_ref[at : at + piece, :]))
    ahead = first(0)
    for at in range(0, hidden_all, piece):
        inner, back = ahead
        if at + piece < hidden_all:
            ahead = first(at + piece)
        part, slope = gelu_parts(inner)
        hidden.append(part)
        grad_inner.append(back.astype(BF16) * slope)
    hidden = jnp.concatenate(hidden, axis=1)
    grad_inner = jnp.concatenate(grad_inner, axis=1)
    total = after_two + dot_nn(hidden, w_down_ref[...])
    grad3 = dot_nt(grad_inner, w_up_ref[...])
    grad_down[...] += dot_tn(hidden, upstream)
    grad_up[...] += dot_tn(normed_three, grad_inner)
    output_ref[...] = total.astype(BF16).reshape(feats, rows, width)
    gain_acc[0] += column_sum(grad3 * xhat3)
    grad_two = upstream.astype(F32) + norm_back(xhat3, scale3, gain_mlp, grad3)

    if fast:
        wide, narrow = stages[0].shape[-1], stages[2].shape[-1]
        sends = [
            pltpu.make_async_copy(stage, out.at[:, :, :, low : low + width_of], copies.at[at])
            for at, (stage, out, low, width_of) in enumerate(
                (
                    (stages[0], outs[0], 0, wide),
                    (stages[1], outs[1], 0, wide),
                    (stages[2], outs[0], wide, narrow),
                    (stages[3], outs[1], wide, narrow),
                )
            )
        ]

        @pl.when(step == last)
        def _():
            emit(idx_ref, stages[0], stages[1], [(grad_up, 0), (grad_down, hidden_all)])
            sends[0].start()
            sends[1].start()

    branch = grad_two.astype(BF16)
    grad_out[...] += dot_tn(att, branch)
    grad_att = dot_nt(branch, w_out_ref[...]).astype(BF16)
    grad_f = [grad_att[f * rows : (f + 1) * rows] for f in range(feats)]
    grad_probs = jnp.stack([dot_nt(values_b[f], grad_f[f]) for f in range(feats)]).reshape(feats * HEADS, keys, rows)
    grad_scores = probs * (grad_probs - jnp.sum(grad_probs * probs, axis=1, keepdims=True))
    grad_scores = grad_scores.reshape(feats, HEADS * keys, rows).astype(BF16)
    grad_query = jnp.concatenate([dot_tn(grad_scores[f], keys_b[f]) for f in range(feats)], axis=0)
    grad_query = (grad_query * (head**-0.5)).astype(BF16)
    grad_keys = [own_heads(dot_nn(grad_scores[f], query_f[f]), keys) for f in range(feats)]
    grad_values = [own_heads(dot_nn(probs_b[f], grad_f[f]), keys) for f in range(feats)]
    grad_kv = jnp.concatenate(
        [jnp.concatenate(grad_keys, axis=0) * (head**-0.5), jnp.concatenate(grad_values, axis=0)], axis=1
    ).astype(BF16)
    grad_qkv[:, 0:width] += dot_tn(normed_two, grad_query)
    grad_qkv[:, width : 3 * width] += dot_tn(slots, grad_kv)
    slots_ref[pl.ds(step * feats, feats)] = dot_nt(grad_kv, w_row_ref[:, width : 3 * width]).reshape(feats, keys, width)
    grad_normed = dot_nt(grad_query, w_row_ref[:, 0:width])
    gain_acc[1] += column_sum(grad_normed * xhat2)
    grad_after_ref[...] = (grad_two + norm_back(xhat2, scale2, gain_row, grad_normed)).reshape(feats, rows, width)

    @pl.when(step == last)
    def _():
        if fast:
            emit(idx_ref, stages[2], stages[3], [(grad_qkv, 0), (grad_out, 3 * width)])
            sends[2].start()
            sends[3].start()
        gains_ref[...] = gain_acc[...]
        block = CTX_DEV * features
        for at in range(0, keys, 2 * CTX_DEV):
            both = jnp.swapaxes(slots_ref[:, at : at + 2 * CTX_DEV, :], 0, 1).reshape(2 * block, width)
            slot_out[at * features : at * features + 2 * block, :] = both.astype(BF16)
        if fast:
            for send in sends:
                send.wait()


def feature_backward(grad_one, packed, probs_b, att, start, gain, w_qkv, w_out, group):
    cells, width = start.shape
    head = width // HEADS
    branch = grad_one.astype(BF16)
    grad_w_out = dot_tn(att, branch)
    grad_att = dot_nt(branch, w_out).astype(BF16)
    queries, keys, values = (head_parts(packed, part, group, head) for part in range(3))
    grads = [
        grad_att[low : low + group, h * head : (h + 1) * head] for low in range(0, cells, group) for h in range(HEADS)
    ]
    probs = probs_b.astype(F32)
    grad_probs = jnp.stack([dot_nt(value, grad) for value, grad in zip(values, grads)])
    grad_scores = probs * (grad_probs - jnp.sum(grad_probs * probs, axis=1, keepdims=True))
    grad_scores = grad_scores.astype(BF16)
    grad_queries = join_parts([dot_tn(grad_scores[at], key) for at, key in enumerate(keys)]) * (head**-0.5)
    grad_keys = join_parts([dot_nn(grad_scores[at], query) for at, query in enumerate(queries)]) * (head**-0.5)
    grad_values = join_parts([dot_nn(probs_b[at], grad) for at, grad in enumerate(grads)])
    grad_qkv = jnp.concatenate([grad_queries.astype(BF16), grad_keys.astype(BF16), grad_values.astype(BF16)], axis=1)
    xhat, scale = normalize(start)
    grad_w_qkv = dot_tn((xhat * gain).astype(BF16), grad_qkv)
    grad_normed = dot_nt(grad_qkv, w_qkv)
    grad_start = grad_one + norm_back(xhat, scale, gain, grad_normed)
    return grad_w_qkv, grad_w_out, column_sum(grad_normed * xhat), grad_start


def feature_backward_kernel(waits, *refs):
    (
        cells_ref, mask_ref, vectors_ref, w_qkv_ref, w_out_ref, grad_after_ref, qkv_ref, probs_ref, att_ref,
    ), refs = refs[:9], refs[9 + waits :]
    grad_cells_ref, grad_w_qkv, grad_w_out, gains = refs
    rows, features, width = cells_ref.shape
    cells = rows * features
    group = GROUP_ROWS * features
    step = pl.program_id(0)

    @pl.when(step == 0)
    def _():
        for ref in (grad_w_qkv, grad_w_out, gains):
            ref[...] = jnp.zeros_like(ref)

    grad_one = jnp.swapaxes(grad_after_ref[...], 0, 1).reshape(cells, width)
    cell = lax.broadcasted_iota(jnp.int32, (cells, 1), 0) + step * cells
    grad_one = jnp.where(cell < CTX_DEV * features, 0.0, grad_one)
    start, absent = start_cells(cells_ref[...], mask_ref[...], step * rows, vector(vectors_ref, 0))
    add_qkv, add_out, add_gain, grad_start = feature_backward(
        grad_one, qkv_ref[...], probs_ref[...].reshape(cells // group * HEADS, group, group), att_ref[...],
        start, vector(vectors_ref, 1), w_qkv_ref[...], w_out_ref[...], group,
    )
    grad_w_qkv[...] += add_qkv
    grad_w_out[...] += add_out
    gains[0] += add_gain
    grad_start = grad_start.reshape(rows, features, width)
    grad_cells_ref[...] = jnp.where(absent, 0.0, grad_start)
    gains[1] += column_sum(jnp.where(absent, grad_start, 0.0).reshape(cells, width))


def output_kernel(output_t_ref, output_ref):
    output_ref[...] = jnp.swapaxes(output_t_ref[...].astype(F32), 0, 1).astype(BF16)


def context_backward_kernel(fast, *refs):
    (
        idx_ref, cells_ref, mask_ref, vectors_ref, w_qkv_ref, w_out_ref, grad_after_ref, qkv_ref, probs_ref, att_ref,
        after_ref, slots_ref, sum_qkv, sum_out, sum_gains, row_gains, _,
    ), refs = refs[:17], refs[17:]
    grad_cells_ref, gains_ref, out_a, out_b, grad_w_qkv, grad_w_out, columns = refs
    rows, features, width = cells_ref.shape
    cells = rows * features
    total = slots_ref[...].astype(F32)
    xhat2, scale2 = normalize(after_ref[...])
    grad_one = jnp.swapaxes(grad_after_ref[...], 0, 1)[0:rows].reshape(cells, width)
    grad_one = grad_one + norm_back(xhat2, scale2, vector(vectors_ref, 2), total)
    start, absent = start_cells(cells_ref[...], mask_ref[...], 0, vector(vectors_ref, 0))
    add_qkv, add_out, add_gain, grad_start = feature_backward(
        grad_one, qkv_ref[...], probs_ref[0, :, 0:cells, 0:cells], att_ref[...],
        start, vector(vectors_ref, 1), w_qkv_ref[...], w_out_ref[...], cells,
    )
    grad_w_qkv[...] = sum_qkv[...] + add_qkv
    grad_w_out[...] = sum_out[...] + add_out
    grad_start = grad_start.reshape(rows, features, width)
    grad_cells_ref[...] = jnp.where(absent, 0.0, grad_start)
    gains = [
        sum_gains[0] + add_gain,
        sum_gains[1] + column_sum(jnp.where(absent, grad_start, 0.0).reshape(cells, width)),
        row_gains[1] + column_sum(total * xhat2),
        row_gains[0],
    ]
    gains = jnp.concatenate([jnp.sum(g, axis=0, keepdims=True) for g in gains], axis=0)
    gains_ref[...] = gains
    if fast:
        columns[...] = jnp.concatenate([gains, jnp.zeros((124, width), F32)], axis=0).T
        emit(idx_ref, out_a, out_b, [(grad_w_qkv, 0), (grad_w_out, 3 * width), (columns, 4 * width)])
    else:
        out_a[...] = grad_w_qkv[...]
        out_b[...] = grad_w_out[...]


def join_kernel(count, *refs):
    rows = refs[0].shape[0]
    for at in range(count):
        refs[-1][at * rows : (at + 1) * rows, :] = refs[at][...]


def sum_kernel(count, groups, *refs):
    ins, outs = refs[:count], refs[len(refs) - len(groups) :]
    for group, out in zip(groups, outs):
        for at, part in enumerate(group):
            total = ins[0][part].astype(F32)
            for ref in ins[1:]:
                total = total + ref[part].astype(F32)
            out[at] = total.astype(BF16)


def whole(array):
    zeros = (0,) * array.ndim
    return pl.BlockSpec(array.shape, lambda i: zeros, pipeline_mode=pl.Buffered(1))


def whole_out(shape):
    zeros = (0,) * len(shape)
    return pl.BlockSpec(shape, lambda i: zeros, pipeline_mode=pl.Buffered(1))


def tiles(shape, axis, offset=0):
    def index(i):
        return tuple(i + offset if d == axis else 0 for d in range(len(shape)))

    return pl.BlockSpec(shape, index)


WAITS = 1e14
SCALARS = pl.BlockSpec(memory_space=pltpu.SMEM)
UNTOUCHED = pl.BlockSpec(memory_space=pl.ANY)


def struct(shape, dtype):
    return jax.ShapeDtypeStruct(shape, dtype)


def call(kernel, name, grid, args, in_specs, outs, out_specs, scratch, flops, aliases=None, vmem=VMEM_LIMIT, pinned=True):
    small = 1 << 15
    large = lambda a: pinned and math.prod(a.shape) >= 1 << 15
    args = [pltpu.with_memory_space_constraint(a, pltpu.HBM) if large(a) else a for a in args]
    outs = [pltpu.HBM(o.shape, o.dtype) if large(o) else o for o in outs]
    sizes = [math.prod(a.shape) * a.dtype.itemsize for a in [*args, *outs]]
    return pl.pallas_call(
        kernel,
        grid=(grid,),
        in_specs=in_specs,
        out_shape=outs,
        out_specs=out_specs,
        scratch_shapes=scratch,
        input_output_aliases=aliases or {},
        compiler_params=pltpu.CompilerParams(vmem_limit_bytes=vmem, dimension_semantics=("arbitrary",)),
        cost_estimate=pl.CostEstimate(flops=int(flops), bytes_accessed=int(sum(sizes)), transcendentals=0),
        name=name,
    )(*args)


def xor_pairs(size, bit):
    return [(i, i ^ bit) for i in range(size)]


def swap(array, axis, size, bit):
    return lax.ppermute(array, axis, xor_pairs(size, bit))


def add_all(terms):
    total = terms[0].astype(F32)
    for term in terms[1:]:
        total = total + term.astype(F32)
    return total.astype(BF16)


def exchange(parts, axis, size, unit):
    return [parts[0]] + [swap(parts[at], axis, size, at * unit) for at in range(1, len(parts))]


def sum_parts(parts, groups, name, after=(), flops=WAITS):
    outs = [struct((len(group), *parts[0].shape[1:]), BF16) for group in groups]
    return call(
        functools.partial(sum_kernel, len(parts), groups),
        name,
        1,
        [*parts, *after],
        [whole(a) for a in parts] + [UNTOUCHED] * len(after),
        outs,
        [whole_out(o.shape) for o in outs],
        [],
        flops,
        pinned=False,
    )


def place_kernel(tabs, moves, *refs):
    idx_ref, ins, outs = refs[0], refs[1 : 1 + tabs], refs[len(refs) - len(moves) :]
    tab = idx_ref[0]
    for out, (count, column) in zip(outs, moves):
        width = out.shape[1]
        for u in range(tabs):
            rows = ins[u].shape[0]
            for at in range(count):
                low = pl.multiple_of(((tab ^ u) * count + at) * rows, 16)
                out[pl.ds(low, rows), :] = ins[u][:, column + at * width : column + (at + 1) * width].astype(F32)


def place(idx, pieces, moves, outs, tabs, name, after):
    return call(
        functools.partial(place_kernel, tabs, moves),
        name,
        1,
        [idx, *pieces, *after],
        [SCALARS] + [whole(a) for a in pieces] + [UNTOUCHED] * len(after),
        outs,
        [whole_out(o.shape) for o in outs],
        [],
        WAITS,
        pinned=False,
    )


def per_device(
    tabs,
    blocks,
    cells,
    missing_mask,
    context_counts,
    missing_embedding,
    gain_feature,
    w_feature_qkv,
    w_feature_out,
    gain_row,
    w_row_qkv,
    w_row_out,
    gain_mlp,
    w_up,
    w_down,
    upstream,
):
    _, rows, features, width = cells.shape
    hidden = w_up.shape[1]
    keys = CTX_DEV * blocks
    cells, mask, upstream = cells[0], jnp.swapaxes(missing_mask[0], 0, 1), upstream[0]
    vectors = jnp.concatenate([missing_embedding, gain_feature, gain_row, gain_mlp]).astype(F32).reshape(-1, 128)
    all_cells = rows * features
    cost = all_cells * width * width
    fast = tabs == 4 and blocks == 8 and width == 16 * tabs * blocks and hidden % (16 * tabs * blocks) == 0
    tall = hidden // (16 * tabs * blocks)
    idx = jnp.stack([lax.axis_index("tab"), lax.axis_index("rows")]).astype(jnp.int32)

    block = CTX_DEV * features
    piece_rows = block + 16
    payload, after_ctx = call(
        context_kernel,
        "context_rows",
        1,
        [context_counts, cells, mask, vectors, w_feature_qkv, w_feature_out],
        [SCALARS, pl.BlockSpec((CTX_DEV, features, width), lambda i: (0, 0, 0))]
        + [whole(a) for a in (mask, vectors, w_feature_qkv, w_feature_out)],
        [struct((piece_rows, width), BF16), struct((block, width), F32)],
        [whole_out((piece_rows, width)), whole_out((block, width))],
        [],
        2 * block * width * 4 * width,
    )
    if fast:
        received = exchange([payload] * (blocks // 2), "rows", blocks, 2)


    tile = min(32, rows)
    steps = rows // tile
    groups = tile // GROUP_ROWS
    group = GROUP_ROWS * features
    after_one, upstream_t, qkv, probs, att = call(
        feature_kernel,
        "feature_forward",
        steps,
        [cells, mask, upstream, vectors, w_feature_qkv, w_feature_out],
        [tiles((tile, features, width), 0), whole(mask), tiles((tile, features, width), 0)]
        + [whole(a) for a in (vectors, w_feature_qkv, w_feature_out)],
        [
            struct((features, rows, width), F32),
            struct((features, rows, width), BF16),
            struct((all_cells, 3 * width), BF16),
            struct((rows // GROUP_ROWS, HEADS, group, group), BF16),
            struct((all_cells, width), BF16),
        ],
        [
            tiles((features, tile, width), 1),
            tiles((features, tile, width), 1),
            tiles((tile * features, 3 * width), 0),
            tiles((groups, HEADS, group, group), 0),
            tiles((tile * features, width), 0),
        ],
        [],
        2 * 5 * cost,
    )

    if fast:
        mine = call(
            functools.partial(join_kernel, len(received)),
            "join",
            1,
            received + [att],
            [whole(a) for a in received] + [UNTOUCHED],
            [struct((len(received) * piece_rows, width), BF16)],
            [whole_out((len(received) * piece_rows, width))],
            [],
            0,
        )[0]
        gathered = [mine, swap(mine, "rows", blocks, 1)]
    else:
        gathered = [lax.all_gather(payload, "rows", axis=0, tiled=True)]

    feats = 4
    cell_tile = (feats, rows, width)
    full = [struct(s, F32) for s in ((width, hidden), (hidden, width), (width, 3 * width), (width, width))]
    if fast:
        shares = [struct((tabs, blocks // 2, 16, hidden + (4 + tall) * width), BF16)] * 2
        stages = [pltpu.VMEM((tabs, blocks // 2, 16, w), BF16) for w in (hidden + tall * width, 4 * width) for _ in range(2)]
        stages += [pltpu.SemaphoreType.DMA((4,))]
    else:
        shares = full
    weights = [vectors, w_row_qkv, w_row_out, w_up, w_down]
    output_t, grad_after, row_gains, slot_parts, *row_shares = call(
        functools.partial(rows_kernel, len(gathered), fast),
        "rows_and_feed_forward",
        features // feats,
        [idx, after_one, upstream_t] + weights + gathered,
        [SCALARS] + [tiles(cell_tile, 0)] * 2 + [whole(a) for a in weights[:3]] + [UNTOUCHED] * 2 + [whole(a) for a in gathered],
        [
            struct((features, rows, width), BF16),
            struct((features, rows, width), F32),
            struct((2, 8, width), F32),
            struct((keys * features, width), BF16),
        ]
        + shares,
        [tiles(cell_tile, 0)] * 2
        + [whole_out((2, 8, width)), whole_out((keys * features, width))]
        + [UNTOUCHED if fast else whole_out(s.shape) for s in shares],
        [pltpu.VMEM(s.shape, F32) for s in (full if fast else [])]
        + [pltpu.VMEM(s, F32) for s in ((features, keys, width), (HEADS * keys, 128), (2, 8, width))]
        + [pltpu.VMEM(a.shape, BF16) for a in (w_up, w_down)]
        + [pltpu.SemaphoreType.DMA((2,))]
        + (stages if fast else []),
        2 * 34 * cost,
        vmem=(48 if fast else 62) * MIB,
    )
    own_slots = lax.psum_scatter(slot_parts, "rows", scatter_dimension=0, tiled=True)

    output = call(
        output_kernel,
        "output",
        steps,
        [output_t],
        [tiles((features, tile, width), 1)],
        [struct((rows, features, width), BF16)],
        [tiles((tile, features, width), 0)],
        [],
        0,
    )[0]
    parts = []
    if fast:
        keep, send = row_shares
        got = swap(send, "rows", blocks, 1)
        parts = [add_all([keep[u], got[u]]) for u in range(tabs)]
        row_parts = exchange(parts, "tab", tabs, 1)

    weights = [mask, vectors, w_feature_qkv, w_feature_out]
    sums = [struct((width, 3 * width), F32), struct((width, width), F32), struct((2, 8, width), F32)]
    big = struct((rows, features, width), F32)
    grad_cells, *sums = call(
        functools.partial(feature_backward_kernel, 1 + len(parts[:1])),
        "feature_backward",
        steps,
        [cells] + weights + [grad_after, qkv, probs, att, output] + parts[:1],
        [tiles((tile, features, width), 0)]
        + [whole(a) for a in weights]
        + [
            tiles((features, tile, width), 1),
            tiles((tile * features, 3 * width), 0),
            tiles((groups, HEADS, group, group), 0),
            tiles((tile * features, width), 0),
        ]
        + [UNTOUCHED] * (1 + len(parts[:1])),
        [big] + sums,
        [tiles((tile, features, width), 0)] + [whole_out(s.shape) for s in sums],
        [],
        2 * 10 * cost,
        vmem=32 * MIB,
    )
    args = [idx, cells] + weights + [grad_after, qkv, probs, att, after_ctx, own_slots] + sums + [row_gains, grad_cells]
    outs = [struct((tabs, blocks // 2, 16, 4 * width + 128), BF16)] * 2 if fast else [struct(s.shape, F32) for s in sums[:2]]
    context_cells = pl.BlockSpec((CTX_DEV, features, width), lambda i: (0, 0, 0))
    grad_cells, gains, *feature_shares = call(
        functools.partial(context_backward_kernel, fast),
        "context_backward",
        1,
        args,
        [SCALARS, context_cells]
        + [whole(a) for a in weights]
        + [
            pl.BlockSpec((features, 8, width), lambda i: (0, 0, 0)),
            pl.BlockSpec((block, 3 * width), lambda i: (0, 0)),
            pl.BlockSpec((1, HEADS, group, group), lambda i: (0, 0, 0, 0)),
            pl.BlockSpec((block, width), lambda i: (0, 0)),
        ]
        + [whole(a) for a in args[10:16]]
        + [UNTOUCHED],
        [big, struct((4, width), F32)] + outs,
        [context_cells, whole_out((4, width))] + [whole_out(o.shape) for o in outs],
        [pltpu.VMEM(s, F32) for s in ((width, 3 * width), (width, width), (width, 128))],
        0,
        {16: 0},
    )

    if fast:
        shard = lambda height, columns: struct((height // blocks, columns), F32)
        keep, send = feature_shares
        got = swap(send, "rows", blocks, 1)
        one = [(q,) for q in range(blocks // 2)]
        lines = sum_parts(row_parts, one, "sum_tab_rows", [keep])
        row_parts = exchange(lines, "rows", blocks, 2)
        parts = sum_parts([keep, got], [(u,) for u in range(tabs)], "sum_core_features", [lines[0]], 0)
        parts = [part[0] for part in parts]
        lines = sum_parts(exchange(parts, "tab", tabs, 1), one, "sum_tab_features")
        parts = exchange(lines, "rows", blocks, 2)
        (own_rows,) = sum_parts(row_parts, [(0,)], "sum_rows_rows", [lines[0]])
        row_pieces = exchange([own_rows[0]] * tabs, "tab", tabs, 1)
        (own,) = sum_parts(parts, [(0,)], "sum_rows_features", [own_rows])
        pieces = exchange([own[0]] * tabs, "tab", tabs, 1)
        wide = hidden + tall * width
        moves = [(1, 0), (tall, hidden), (1, wide), (1, wide + 3 * width)]
        outs = [shard(width, hidden), shard(hidden, width), shard(width, 3 * width), shard(width, width)]
        grad_up, grad_down, grad_row_qkv, grad_row_out = place(idx, row_pieces, moves, outs, tabs, "place_rows", [])
        moves = [(1, 0), (1, 3 * width), (1, 4 * width)]
        outs = [shard(width, 3 * width), shard(width, width), shard(width, 128)]
        grad_feature_qkv, grad_feature_out, columns = place(idx, pieces, moves, outs, tabs, "place_features", [grad_up])
        gains = columns.T
    else:
        scatter = lambda a, axis: lax.psum_scatter(a, "rows", scatter_dimension=axis, tiled=True)
        gains = lax.psum(scatter(gains, 1), "tab")
        weights = lax.psum([scatter(w, 0) for w in [*row_shares, *feature_shares]], "tab")
        grad_up, grad_down, grad_row_qkv, grad_row_out, grad_feature_qkv, grad_feature_out = weights
    return (
        output[None],
        grad_cells[None],
        gains[1],
        gains[0],
        grad_feature_qkv,
        grad_feature_out,
        gains[2],
        grad_row_qkv,
        grad_row_out,
        gains[3],
        grad_up,
        grad_down,
    )


def solution(mesh):
    in_specs = (
        P("tab", "rows", None, None),
        P("tab", "rows", None),
        P("tab", "rows"),
        P(),
        P(),
        P(),
        P(),
        P(),
        P(),
        P(),
        P(),
        P(),
        P(),
        P("tab", "rows", None, None),
    )
    out_specs = (
        P("tab", "rows", None, None),
        P("tab", "rows", None, None),
        P("rows"),
        P("rows"),
        P("rows", None),
        P("rows", None),
        P("rows"),
        P("rows", None),
        P("rows", None),
        P("rows"),
        P("rows", None),
        P("rows", None),
    )
    return jax.shard_map(
        functools.partial(per_device, mesh.shape["tab"], mesh.shape["rows"]),
        mesh=mesh,
        in_specs=in_specs,
        out_specs=out_specs,
        check_vma=False,
    )
```

```python
import functools
import math

import jax
import jax.numpy as jnp
from jax import lax
from jax.experimental import pallas as pl
from jax.experimental.pallas import tpu as pltpu
from jax.sharding import PartitionSpec as P

HEADS = 4
CTX_DEV = 4
EPSILON = 1e-05
MASKED = -1e30
F32 = jnp.float32
BF16 = jnp.bfloat16
GROUP_ROWS = 8
MIB = 1024 * 1024
VMEM_LIMIT = 24 * MIB


def dot_nn(left, right):
    return lax.dot_general(left, right, (((1,), (0,)), ((), ())), preferred_element_type=F32)


def dot_nt(left, right):
    return lax.dot_general(left, right, (((1,), (1,)), ((), ())), preferred_element_type=F32)


def dot_tn(left, right):
    return lax.dot_general(left, right, (((0,), (0,)), ((), ())), preferred_element_type=F32)


def normalize(tensor):
    row_mean = jnp.mean(tensor, axis=-1, keepdims=True)
    centred = tensor - row_mean
    scale = lax.rsqrt(jnp.mean(centred * centred, axis=-1, keepdims=True) + EPSILON)
    return centred * scale, scale


def norm_back(xhat, scale, gain, gradient):
    scaled = gradient * gain
    first = jnp.mean(scaled, axis=-1, keepdims=True)
    second = jnp.mean(scaled * xhat, axis=-1, keepdims=True)
    return scale * (scaled - first - xhat * second)


def column_sum(tensor):
    rows, width = tensor.shape
    return jnp.sum(tensor.reshape(rows // 8, 8, width), axis=0)


def missing_column(mask, first, rows):
    features, lanes = mask.shape
    shape = (rows, features, lanes)
    pick = lax.broadcasted_iota(jnp.int32, shape, 2) == first + lax.broadcasted_iota(jnp.int32, shape, 0)
    spread = jnp.broadcast_to(mask.astype(F32)[None], shape)
    return jnp.sum(jnp.where(pick, spread, 0.0), axis=-1, keepdims=True)


def vector(ref, at):
    count = ref.shape[0] // 4
    return jnp.concatenate([ref[at * count + i : at * count + i + 1, :] for i in range(count)], axis=1)


def start_cells(cells, mask, first, missing):
    rows, features, width = cells.shape
    absent = missing_column(mask, first, rows) > 0.5
    return jnp.where(absent, missing.reshape(1, 1, width), cells.astype(F32)).reshape(rows * features, width), absent


def same_row_bias(size, features):
    shape = (size, size)
    left = lax.broadcasted_iota(jnp.int32, shape, 0) // features
    right = lax.broadcasted_iota(jnp.int32, shape, 1) // features
    return jnp.where(left == right, 0.0, MASKED)


def head_parts(packed, part, group, head):
    cells, width = packed.shape[0], packed.shape[1] // 3
    return [
        packed[low : low + group, part * width + h * head : part * width + (h + 1) * head]
        for low in range(0, cells, group)
        for h in range(HEADS)
    ]


def join_parts(parts):
    rows = [jnp.concatenate(parts[at : at + HEADS], axis=1) for at in range(0, len(parts), HEADS)]
    return jnp.concatenate(rows, axis=0)


def softmax_keys(scores):
    exp_terms = jnp.exp(scores - jnp.max(scores, axis=1, keepdims=True))
    return exp_terms * (1.0 / jnp.sum(exp_terms, axis=1, keepdims=True))


def feature_forward(start, gain, w_qkv, w_out, features, group):
    cells, width = start.shape
    head = width // HEADS
    xhat, _ = normalize(start)
    qkv = dot_nn((xhat * gain).astype(BF16), w_qkv).astype(BF16)
    queries, keys, values = (head_parts(qkv, part, group, head) for part in range(3))
    scores = jnp.stack([dot_nt(key, query) for key, query in zip(keys, queries)])
    probs = softmax_keys(scores * (head**-0.5) + same_row_bias(group, features)[None]).astype(BF16)
    att = join_parts([dot_tn(probs[at], value).astype(BF16) for at, value in enumerate(values)])
    return start + dot_nn(att, w_out), qkv, probs, att


def context_kernel(count_ref, cells_ref, mask_ref, vectors_ref, w_qkv_ref, w_out_ref, send_ref, after_ref):
    rows, features, width = cells_ref.shape
    cells = rows * features
    start, _ = start_cells(cells_ref[...], mask_ref[...], 0, vector(vectors_ref, 0))
    after, _, _, _ = feature_forward(start, vector(vectors_ref, 1), w_qkv_ref[...], w_out_ref[...], features, cells)
    after_ref[...] = after
    xhat, _ = normalize(after)
    send_ref[0:cells, :] = (xhat * vector(vectors_ref, 2)).astype(BF16)
    count = count_ref[0, 0].astype(F32)
    send_ref[cells : cells + 16, :] = jnp.full((16, width), count, F32).astype(BF16)


def feature_kernel(
    cells_ref, mask_ref, upstream_ref, vectors_ref, w_qkv_ref, w_out_ref,
    after_ref, upstream_t_ref, qkv_ref, probs_ref, att_ref,
):
    rows, features, width = cells_ref.shape
    start, _ = start_cells(cells_ref[...], mask_ref[...], pl.program_id(0) * rows, vector(vectors_ref, 0))
    after, qkv, probs, att = feature_forward(
        start, vector(vectors_ref, 1), w_qkv_ref[...], w_out_ref[...], features, GROUP_ROWS * features
    )
    qkv_ref[...] = qkv
    probs_ref[...] = probs.reshape(probs_ref.shape)
    att_ref[...] = att
    after_ref[...] = jnp.swapaxes(after.reshape(rows, features, width), 0, 1)
    upstream_t_ref[...] = jnp.swapaxes(upstream_ref[...].astype(F32), 0, 1).astype(BF16)


def head_blocks(tensor):
    keys, width = tensor.shape
    tiled = jnp.concatenate([tensor] * HEADS, axis=0)
    row_head = lax.broadcasted_iota(jnp.int32, tiled.shape, 0) // keys
    lane_head = lax.broadcasted_iota(jnp.int32, tiled.shape, 1) // (width // HEADS)
    return jnp.where(row_head == lane_head, tiled, jnp.zeros_like(tiled))


def own_heads(tensor, keys):
    head = tensor.shape[1] // HEADS
    return jnp.concatenate([tensor[h * keys : (h + 1) * keys, h * head : (h + 1) * head] for h in range(HEADS)], axis=1)


def gelu_parts(inner):
    const = 0.7978845608028654
    cubic = const * 0.044715
    inner = inner.astype(BF16)
    square = inner * inner
    half = 0.5 + 0.5 * jnp.tanh(inner * (const + cubic * square))
    hidden = inner * half
    slope = half + (hidden - hidden * half) * (2.0 * const + (6.0 * cubic) * square)
    return hidden, slope


def read_slots(gathered, idx_ref, slots_ref, bias_ref, features):
    keys, width = slots_ref.shape[1], slots_ref.shape[2]
    blocks = keys // CTX_DEV
    block = CTX_DEV * features
    piece = block + 16
    slot = lax.broadcasted_iota(jnp.int32, (keys, 128), 0)
    counts = jnp.zeros((keys, 128), F32)
    core, line = idx_ref[1] % 2, idx_ref[1] // 2
    for pair in range(blocks // 2):
        if len(gathered) == 2:
            mine, other = (ref[pair * piece : (pair + 1) * piece, :].astype(F32) for ref in gathered)
            even, odd = jnp.where(core == 0, mine, other), jnp.where(core == 0, other, mine)
            at = line ^ pair
        else:
            even, odd = (gathered[0][(2 * pair + j) * piece : (2 * pair + j + 1) * piece, :].astype(F32) for j in range(2))
            at = pair
        both = jnp.concatenate([even[0:block], odd[0:block]], axis=0).reshape(2 * CTX_DEV, features, width)
        slots_ref[:, pl.ds(pl.multiple_of(at * 2 * CTX_DEV, 2 * CTX_DEV), 2 * CTX_DEV), :] = jnp.swapaxes(both, 0, 1)
        for j, part in enumerate((even, odd)):
            counts = jnp.where(slot // CTX_DEV == 2 * at + j, part[block : block + 1, 0:128], counts)
    bias = jnp.where((slot % CTX_DEV).astype(F32) < counts, 0.0, MASKED)
    bias_ref[...] = jnp.concatenate([bias] * HEADS, axis=0)


def emit(idx_ref, keep, send, sources):
    tab, block = idx_ref[0], idx_ref[1]
    core, line = block % 2, block // 2
    lines, rows, _ = keep[0].shape
    tabs = keep[1].shape[0] + 1
    for u in range(tabs):
        for q in range(lines):
            for refs, shard in ((keep, core), (send, 1 - core)):
                ref = refs[0].at[q] if u == 0 else refs[1].at[u - 1, q]
                for acc, column in sources:
                    height, width = acc.shape
                    part = height // (2 * lines * tabs)
                    low = (((line ^ q) * 2 + shard) * tabs + (tab ^ u)) * part
                    for at in range(part // rows):
                        low_at = pl.multiple_of(low + at * rows, rows)
                        ref[:, column + at * width : column + (at + 1) * width] = acc[pl.ds(low_at, rows), :].astype(BF16)


def rows_kernel(pieces, fast, *refs):
    (idx_ref, after_ref, upstream_ref, vectors_ref, w_row_ref, w_out_ref, w_up_hbm, w_down_hbm), refs = refs[:8], refs[8:]
    gathered, refs = refs[:pieces], refs[pieces:]
    (output_ref, grad_after_ref, gains_ref), refs = refs[:3], refs[3:]
    slot_outs, refs = (refs[:2], refs[2:]) if fast else (refs[:1], refs[1:])
    if fast:
        outs, refs = refs[:4], refs[4:]
        stages, copies, refs = refs[-9:-1], refs[-1], refs[:-9]
    *refs, w_up_ref, w_down_ref, loads = refs
    grad_up, grad_down, grad_qkv, grad_out, slots_ref, bias_ref, gain_acc = refs
    feats, rows, width = after_ref.shape
    features, keys, _ = slots_ref.shape
    hidden_all = w_up_ref.shape[1]
    cells = feats * rows
    head = width // HEADS
    step = pl.program_id(0)
    gain_row, gain_mlp = vector(vectors_ref, 2), vector(vectors_ref, 3)

    last = pl.num_programs(0) - 1
    fetches = [
        pltpu.make_async_copy(source, target, loads.at[at])
        for at, (source, target) in enumerate(((w_up_hbm, w_up_ref), (w_down_hbm, w_down_ref)))
    ]

    @pl.when(step == 0)
    def _():
        for fetch in fetches:
            fetch.start()
        read_slots(gathered, idx_ref, slots_ref, bias_ref, features)
        for ref in (grad_qkv, grad_out, grad_up, grad_down, gain_acc):
            ref[...] = jnp.zeros_like(ref)

    after = after_ref[...].reshape(cells, width)
    xhat2, scale2 = normalize(after)
    normed_two = (xhat2 * gain_row).astype(BF16)
    query = dot_nn(normed_two, w_row_ref[:, 0:width]).astype(BF16)
    slots = slots_ref[pl.ds(step * feats, feats)].reshape(feats * keys, width).astype(BF16)
    kv = dot_nn(slots, w_row_ref[:, width : 3 * width]).astype(BF16)
    keys_b = [head_blocks(kv[f * keys : (f + 1) * keys, 0:width]) for f in range(feats)]
    values_b = [head_blocks(kv[f * keys : (f + 1) * keys, width : 2 * width]) for f in range(feats)]
    query_f = [query[f * rows : (f + 1) * rows] for f in range(feats)]
    scores = jnp.stack([dot_nt(keys_b[f], query_f[f]) for f in range(feats)])
    scores = scores * (head**-0.5) + bias_ref[:, 0:rows][None]
    probs = softmax_keys(scores.reshape(feats * HEADS, keys, rows))
    probs_b = probs.reshape(feats, HEADS * keys, rows).astype(BF16)
    att = jnp.concatenate([dot_tn(probs_b[f], values_b[f]).astype(BF16) for f in range(feats)], axis=0)
    after_two = after + dot_nn(att, w_out_ref[...])

    @pl.when(step == 0)
    def _():
        for fetch in fetches:
            fetch.wait()

    xhat3, scale3 = normalize(after_two)
    normed_three = (xhat3 * gain_mlp).astype(BF16)
    upstream = upstream_ref[...].reshape(cells, width)
    piece = 256
    hidden, grad_inner = [], []
    first = lambda at: (dot_nn(normed_three, w_up_ref[:, at : at + piece]), dot_nt(upstream, w_down_ref[at : at + piece, :]))
    ahead = first(0)
    for at in range(0, hidden_all, piece):
        inner, back = ahead
        if at + piece < hidden_all:
            ahead = first(at + piece)
        part, slope = gelu_parts(inner)
        hidden.append(part)
        grad_inner.append(back.astype(BF16) * slope)
    hidden = jnp.concatenate(hidden, axis=1)
    grad_inner = jnp.concatenate(grad_inner, axis=1)
    total = after_two + dot_nn(hidden, w_down_ref[...])
    grad3 = dot_nt(grad_inner, w_up_ref[...])
    grad_down[...] += dot_tn(hidden, upstream)
    grad_up[...] += dot_tn(normed_three, grad_inner)
    output_ref[...] = total.astype(BF16).reshape(feats, rows, width)
    gain_acc[0] += column_sum(grad3 * xhat3)
    grad_two = upstream.astype(F32) + norm_back(xhat3, scale3, gain_mlp, grad3)

    if fast:
        wide, narrow = stages[0].shape[-1], stages[4].shape[-1]
        sends = []
        for at, stage in enumerate(stages):
            low, size = (0, wide) if at < 4 else (wide, narrow)
            lead = (slice(None),) * (len(stage.shape) - 1)
            sends.append(pltpu.make_async_copy(stage, outs[at % 4].at[(*lead, pl.ds(low, size))], copies.at[at]))

        @pl.when(step == last)
        def _():
            emit(idx_ref, stages[0:2], stages[2:4], [(grad_up, 0), (grad_down, hidden_all)])
            for send in sends[0:4]:
                send.start()

    branch = grad_two.astype(BF16)
    grad_out[...] += dot_tn(att, branch)
    grad_att = dot_nt(branch, w_out_ref[...]).astype(BF16)
    grad_f = [grad_att[f * rows : (f + 1) * rows] for f in range(feats)]
    grad_probs = jnp.stack([dot_nt(values_b[f], grad_f[f]) for f in range(feats)]).reshape(feats * HEADS, keys, rows)
    grad_scores = probs * (grad_probs - jnp.sum(grad_probs * probs, axis=1, keepdims=True))
    grad_scores = grad_scores.reshape(feats, HEADS * keys, rows).astype(BF16)
    grad_query = jnp.concatenate([dot_tn(grad_scores[f], keys_b[f]) for f in range(feats)], axis=0)
    grad_query = (grad_query * (head**-0.5)).astype(BF16)
    grad_keys = [own_heads(dot_nn(grad_scores[f], query_f[f]), keys) for f in range(feats)]
    grad_values = [own_heads(dot_nn(probs_b[f], grad_f[f]), keys) for f in range(feats)]
    grad_kv = jnp.concatenate(
        [jnp.concatenate(grad_keys, axis=0) * (head**-0.5), jnp.concatenate(grad_values, axis=0)], axis=1
    ).astype(BF16)
    grad_qkv[:, 0:width] += dot_tn(normed_two, grad_query)
    grad_qkv[:, width : 3 * width] += dot_tn(slots, grad_kv)
    slots_ref[pl.ds(step * feats, feats)] = dot_nt(grad_kv, w_row_ref[:, width : 3 * width]).reshape(feats, keys, width)
    grad_normed = dot_nt(grad_query, w_row_ref[:, 0:width])
    gain_acc[1] += column_sum(grad_normed * xhat2)
    grad_after_ref[...] = (grad_two + norm_back(xhat2, scale2, gain_row, grad_normed)).reshape(feats, rows, width)

    @pl.when(step == last)
    def _():
        if fast:
            emit(idx_ref, stages[4:6], stages[6:8], [(grad_qkv, 0), (grad_out, 3 * width)])
            for send in sends[4:8]:
                send.start()
        gains_ref[...] = gain_acc[...]
        block = CTX_DEV * features
        core, line = idx_ref[1] % 2, idx_ref[1] // 2
        for q in range(keys // (2 * CTX_DEV)):
            low = pl.multiple_of((line ^ q) * 2 * CTX_DEV, 2 * CTX_DEV) if fast else q * 2 * CTX_DEV
            both = jnp.swapaxes(slots_ref[:, pl.ds(low, 2 * CTX_DEV), :], 0, 1).reshape(2 * block, width)
            if fast:
                even, odd = both[0:block], both[block:]
                slot_outs[0][q] = jnp.where(core == 0, even, odd).astype(BF16)
                slot_outs[1][q] = jnp.where(core == 0, odd, even).astype(BF16)
            else:
                slot_outs[0][2 * q * block : 2 * (q + 1) * block, :] = both.astype(BF16)
        if fast:
            for send in sends:
                send.wait()


def feature_backward(grad_one, packed, probs_b, att, start, gain, w_qkv, w_out, group):
    cells, width = start.shape
    head = width // HEADS
    branch = grad_one.astype(BF16)
    grad_w_out = dot_tn(att, branch)
    grad_att = dot_nt(branch, w_out).astype(BF16)
    queries, keys, values = (head_parts(packed, part, group, head) for part in range(3))
    grads = [
        grad_att[low : low + group, h * head : (h + 1) * head] for low in range(0, cells, group) for h in range(HEADS)
    ]
    probs = probs_b.astype(F32)
    grad_probs = jnp.stack([dot_nt(value, grad) for value, grad in zip(values, grads)])
    grad_scores = probs * (grad_probs - jnp.sum(grad_probs * probs, axis=1, keepdims=True))
    grad_scores = grad_scores.astype(BF16)
    grad_queries = join_parts([dot_tn(grad_scores[at], key) for at, key in enumerate(keys)]) * (head**-0.5)
    grad_keys = join_parts([dot_nn(grad_scores[at], query) for at, query in enumerate(queries)]) * (head**-0.5)
    grad_values = join_parts([dot_nn(probs_b[at], grad) for at, grad in enumerate(grads)])
    grad_qkv = jnp.concatenate([grad_queries.astype(BF16), grad_keys.astype(BF16), grad_values.astype(BF16)], axis=1)
    xhat, scale = normalize(start)
    grad_w_qkv = dot_tn((xhat * gain).astype(BF16), grad_qkv)
    grad_normed = dot_nt(grad_qkv, w_qkv)
    grad_start = grad_one + norm_back(xhat, scale, gain, grad_normed)
    return grad_w_qkv, grad_w_out, column_sum(grad_normed * xhat), grad_start


def feature_backward_kernel(slots, waits, fast, *refs):
    (
        idx_ref, cells_ref, mask_ref, vectors_ref, w_qkv_ref, w_out_ref, grad_after_ref, qkv_ref, probs_ref, att_ref,
        after_ref, row_gains,
    ), refs = refs[:12], refs[12:]
    slot_refs, refs = refs[:slots], refs[slots + waits :]
    (grad_cells_ref, gains_ref), refs = refs[:2], refs[2:]
    if fast:
        outs, refs = refs[:4], refs[4:]
    grad_w_qkv, grad_w_out, gains, columns, extra_ref = refs
    rows, features, width = cells_ref.shape
    cells = rows * features
    block = CTX_DEV * features
    group = GROUP_ROWS * features
    step = pl.program_id(0)

    @pl.when(step == 0)
    def _():
        for ref in (grad_w_qkv, grad_w_out, gains):
            ref[...] = jnp.zeros_like(ref)
        total = slot_refs[0][...].astype(F32)
        for ref in slot_refs[1:]:
            total = total + ref[...].astype(F32)
        xhat, scale = normalize(after_ref[...])
        extra_ref[...] = norm_back(xhat, scale, vector(vectors_ref, 2), total)
        gains[2] = row_gains[1] + column_sum(total * xhat)
        gains[3] = row_gains[0]

    @pl.when(step > 0)
    def _():
        extra_ref[...] = jnp.zeros_like(extra_ref)

    grad_one = jnp.swapaxes(grad_after_ref[...], 0, 1).reshape(cells, width)
    grad_one = jnp.concatenate([grad_one[0:block] + extra_ref[...], grad_one[block:]], axis=0)
    start, absent = start_cells(cells_ref[...], mask_ref[...], step * rows, vector(vectors_ref, 0))
    add_qkv, add_out, add_gain, grad_start = feature_backward(
        grad_one, qkv_ref[...], probs_ref[...].reshape(cells // group * HEADS, group, group), att_ref[...],
        start, vector(vectors_ref, 1), w_qkv_ref[...], w_out_ref[...], group,
    )
    grad_w_qkv[...] += add_qkv
    grad_w_out[...] += add_out
    gains[0] += add_gain
    grad_start = grad_start.reshape(rows, features, width)
    grad_cells_ref[...] = jnp.where(absent, 0.0, grad_start)
    gains[1] += column_sum(jnp.where(absent, grad_start, 0.0).reshape(cells, width))

    @pl.when(step == pl.num_programs(0) - 1)
    def _():
        sums = jnp.concatenate([jnp.sum(gains[at], axis=0, keepdims=True) for at in range(4)], axis=0)
        gains_ref[...] = sums
        if fast:
            columns[...] = jnp.concatenate([sums, jnp.zeros((124, width), F32)], axis=0).T
            emit(idx_ref, outs[0:2], outs[2:4], [(grad_w_qkv, 0), (grad_w_out, 3 * width), (columns, 4 * width)])


def output_kernel(output_t_ref, output_ref):
    output_ref[...] = jnp.swapaxes(output_t_ref[...].astype(F32), 0, 1).astype(BF16)


def join_kernel(count, *refs):
    rows = refs[0].shape[0]
    for at in range(count):
        refs[-1][at * rows : (at + 1) * rows, :] = refs[at][...]


def sum_kernel(count, groups, *refs):
    ins, outs = refs[:count], refs[len(refs) - len(groups) :]
    for group, out in zip(groups, outs):
        for at, part in enumerate(group):
            total = ins[0][part].astype(F32)
            for ref in ins[1:]:
                total = total + ref[part].astype(F32)
            out[at] = total.astype(BF16)


def whole(array):
    zeros = (0,) * array.ndim
    return pl.BlockSpec(array.shape, lambda i: zeros, pipeline_mode=pl.Buffered(1))


def whole_out(shape):
    zeros = (0,) * len(shape)
    return pl.BlockSpec(shape, lambda i: zeros, pipeline_mode=pl.Buffered(1))


def tiles(shape, axis, offset=0):
    def index(i):
        return tuple(i + offset if d == axis else 0 for d in range(len(shape)))

    return pl.BlockSpec(shape, index)


WAITS = 1e14
SCALARS = pl.BlockSpec(memory_space=pltpu.SMEM)
UNTOUCHED = pl.BlockSpec(memory_space=pl.ANY)


def struct(shape, dtype):
    return jax.ShapeDtypeStruct(shape, dtype)


def call(kernel, name, grid, args, in_specs, outs, out_specs, scratch, flops, aliases=None, vmem=VMEM_LIMIT, pinned=True):
    small = 1 << 15
    large = lambda a: pinned and math.prod(a.shape) >= 1 << 15
    args = [pltpu.with_memory_space_constraint(a, pltpu.HBM) if large(a) else a for a in args]
    outs = [pltpu.HBM(o.shape, o.dtype) if large(o) else o for o in outs]
    sizes = [math.prod(a.shape) * a.dtype.itemsize for a in [*args, *outs]]
    return pl.pallas_call(
        kernel,
        grid=(grid,),
        in_specs=in_specs,
        out_shape=outs,
        out_specs=out_specs,
        scratch_shapes=scratch,
        input_output_aliases=aliases or {},
        compiler_params=pltpu.CompilerParams(vmem_limit_bytes=vmem, dimension_semantics=("arbitrary",)),
        cost_estimate=pl.CostEstimate(flops=int(flops), bytes_accessed=int(sum(sizes)), transcendentals=0),
        name=name,
    )(*args)


def xor_pairs(size, bit):
    return [(i, i ^ bit) for i in range(size)]


def swap(array, axis, size, bit):
    return lax.ppermute(array, axis, xor_pairs(size, bit))


def add_all(terms):
    total = terms[0].astype(F32)
    for term in terms[1:]:
        total = total + term.astype(F32)
    return total.astype(BF16)


def exchange(parts, axis, size, unit):
    return [parts[0]] + [swap(parts[at], axis, size, at * unit) for at in range(1, len(parts))]


def sum_parts(parts, groups, name, after=(), flops=WAITS):
    outs = [struct((len(group), *parts[0].shape[1:]), BF16) for group in groups]
    return call(
        functools.partial(sum_kernel, len(parts), groups),
        name,
        1,
        [*parts, *after],
        [whole(a) for a in parts] + [UNTOUCHED] * len(after),
        outs,
        [whole_out(o.shape) for o in outs],
        [],
        flops,
        pinned=False,
    )


def place_kernel(tabs, moves, *refs):
    idx_ref, ins, outs = refs[0], refs[1 : 1 + tabs], refs[len(refs) - len(moves) :]
    tab = idx_ref[0]
    for out, (count, column) in zip(outs, moves):
        width = out.shape[1]
        for u in range(tabs):
            rows = ins[u].shape[0]
            for at in range(count):
                low = pl.multiple_of(((tab ^ u) * count + at) * rows, 16)
                out[pl.ds(low, rows), :] = ins[u][:, column + at * width : column + (at + 1) * width].astype(F32)


def place(idx, pieces, moves, outs, tabs, name, after):
    return call(
        functools.partial(place_kernel, tabs, moves),
        name,
        1,
        [idx, *pieces, *after],
        [SCALARS] + [whole(a) for a in pieces] + [UNTOUCHED] * len(after),
        outs,
        [whole_out(o.shape) for o in outs],
        [],
        WAITS,
        pinned=False,
    )


def per_device(
    tabs,
    blocks,
    cells,
    missing_mask,
    context_counts,
    missing_embedding,
    gain_feature,
    w_feature_qkv,
    w_feature_out,
    gain_row,
    w_row_qkv,
    w_row_out,
    gain_mlp,
    w_up,
    w_down,
    upstream,
):
    _, rows, features, width = cells.shape
    hidden = w_up.shape[1]
    keys = CTX_DEV * blocks
    cells, mask, upstream = cells[0], jnp.swapaxes(missing_mask[0], 0, 1), upstream[0]
    vectors = jnp.concatenate([missing_embedding, gain_feature, gain_row, gain_mlp]).astype(F32).reshape(-1, 128)
    all_cells = rows * features
    cost = all_cells * width * width
    fast = tabs == 4 and blocks == 8 and width == 16 * tabs * blocks and hidden % (16 * tabs * blocks) == 0
    tall = hidden // (16 * tabs * blocks)
    idx = jnp.stack([lax.axis_index("tab"), lax.axis_index("rows")]).astype(jnp.int32)

    block = CTX_DEV * features
    piece_rows = block + 16
    payload, after_ctx = call(
        context_kernel,
        "context_rows",
        1,
        [context_counts, cells, mask, vectors, w_feature_qkv, w_feature_out],
        [SCALARS, pl.BlockSpec((CTX_DEV, features, width), lambda i: (0, 0, 0))]
        + [whole(a) for a in (mask, vectors, w_feature_qkv, w_feature_out)],
        [struct((piece_rows, width), BF16), struct((block, width), F32)],
        [whole_out((piece_rows, width)), whole_out((block, width))],
        [],
        2 * block * width * 4 * width,
    )
    if fast:
        received = exchange([payload] * (blocks // 2), "rows", blocks, 2)


    tile = min(32, rows)
    steps = rows // tile
    groups = tile // GROUP_ROWS
    group = GROUP_ROWS * features
    after_one, upstream_t, qkv, probs, att = call(
        feature_kernel,
        "feature_forward",
        steps,
        [cells, mask, upstream, vectors, w_feature_qkv, w_feature_out],
        [tiles((tile, features, width), 0), whole(mask), tiles((tile, features, width), 0)]
        + [whole(a) for a in (vectors, w_feature_qkv, w_feature_out)],
        [
            struct((features, rows, width), F32),
            struct((features, rows, width), BF16),
            struct((all_cells, 3 * width), BF16),
            struct((rows // GROUP_ROWS, HEADS, group, group), BF16),
            struct((all_cells, width), BF16),
        ],
        [
            tiles((features, tile, width), 1),
            tiles((features, tile, width), 1),
            tiles((tile * features, 3 * width), 0),
            tiles((groups, HEADS, group, group), 0),
            tiles((tile * features, width), 0),
        ],
        [],
        2 * 5 * cost,
    )

    if fast:
        mine = call(
            functools.partial(join_kernel, len(received)),
            "join",
            1,
            received + [att],
            [whole(a) for a in received] + [UNTOUCHED],
            [struct((len(received) * piece_rows, width), BF16)],
            [whole_out((len(received) * piece_rows, width))],
            [],
            0,
        )[0]
        gathered = [mine, swap(mine, "rows", blocks, 1)]
    else:
        gathered = [lax.all_gather(payload, "rows", axis=0, tiled=True)]

    feats = 4
    cell_tile = (feats, rows, width)
    full = [struct(s, F32) for s in ((width, hidden), (hidden, width), (width, 3 * width), (width, width))]
    if fast:
        share = lambda w: [(blocks // 2, 16, w), (tabs - 1, blocks // 2, 16, w)] * 2
        shares = [struct(s, BF16) for s in share(hidden + (4 + tall) * width)]
        stages = [pltpu.VMEM(s, BF16) for w in (hidden + tall * width, 4 * width) for s in share(w)]
        stages += [pltpu.SemaphoreType.DMA((8,))]
    else:
        shares = full
    weights = [vectors, w_row_qkv, w_row_out, w_up, w_down]
    slot_outs = [struct((blocks // 2, block, width), BF16)] * 2 if fast else [struct((keys * features, width), BF16)]
    output_t, grad_after, row_gains, *row_shares = call(
        functools.partial(rows_kernel, len(gathered), fast),
        "rows_and_feed_forward",
        features // feats,
        [idx, after_one, upstream_t] + weights + gathered,
        [SCALARS] + [tiles(cell_tile, 0)] * 2 + [whole(a) for a in weights[:3]] + [UNTOUCHED] * 2 + [whole(a) for a in gathered],
        [
            struct((features, rows, width), BF16),
            struct((features, rows, width), F32),
            struct((2, 8, width), F32),
        ]
        + slot_outs
        + shares,
        [tiles(cell_tile, 0)] * 2
        + [whole_out((2, 8, width))]
        + [whole_out(s.shape) for s in slot_outs]
        + [UNTOUCHED if fast else whole_out(s.shape) for s in shares],
        [pltpu.VMEM(s.shape, F32) for s in (full if fast else [])]
        + [pltpu.VMEM(s, F32) for s in ((features, keys, width), (HEADS * keys, 128), (2, 8, width))]
        + [pltpu.VMEM(a.shape, BF16) for a in (w_up, w_down)]
        + [pltpu.SemaphoreType.DMA((2,))]
        + (stages if fast else []),
        2 * 34 * cost,
        vmem=(48 if fast else 62) * MIB,
    )
    slot_parts, row_shares = row_shares[: len(slot_outs)], row_shares[len(slot_outs) :]
    output = call(
        output_kernel,
        "output",
        steps,
        [output_t],
        [tiles((features, tile, width), 1)],
        [struct((rows, features, width), BF16)],
        [tiles((tile, features, width), 0)],
        [],
        0,
    )[0]
    if fast:
        keep, keep_rest, send, send_rest = row_shares
        got_rest = swap(send_rest, "rows", blocks, 1)
        parts = [add_all([keep_rest[u], got_rest[u]]) for u in range(tabs - 1)]
        got = swap(send, "rows", blocks, 1)
        row_parts = [keep, got] + [swap(parts[u - 1], "tab", tabs, u) for u in range(1, tabs)]
        slot_parts = [slot_parts[0], swap(slot_parts[1], "rows", blocks, 1)]
        slot_parts = sum_parts(slot_parts, [(q,) for q in range(blocks // 2)], "sum_core_slots", [parts[0], got])
        own_slots = exchange([part[0] for part in slot_parts], "rows", blocks, 2)
    else:
        own_slots = [lax.psum_scatter(slot_parts[0], "rows", scatter_dimension=0, tiled=True)]

    weights = [mask, vectors, w_feature_qkv, w_feature_out]
    sums = [struct((width, 3 * width), F32), struct((width, width), F32)]
    outs = [struct(s, BF16) for s in share(4 * width + 128)] if fast else sums
    waits = [output]
    rest = [after_ctx, row_gains, *own_slots]
    grad_cells, gains, *feature_shares = call(
        functools.partial(feature_backward_kernel, len(own_slots), len(waits), fast),
        "feature_backward",
        steps,
        [idx, cells] + weights + [grad_after, qkv, probs, att] + rest + waits,
        [SCALARS, tiles((tile, features, width), 0)]
        + [whole(a) for a in weights]
        + [
            tiles((features, tile, width), 1),
            tiles((tile * features, 3 * width), 0),
            tiles((groups, HEADS, group, group), 0),
            tiles((tile * features, width), 0),
        ]
        + [whole(a) for a in rest]
        + [UNTOUCHED] * len(waits),
        [struct((rows, features, width), F32), struct((4, width), F32)] + outs,
        [tiles((tile, features, width), 0), whole_out((4, width))] + [whole_out(o.shape) for o in outs],
        ([pltpu.VMEM(s.shape, F32) for s in sums] if fast else [])
        + [pltpu.VMEM(s, F32) for s in ((4, 8, width), (width, 128), (block, width))],
        0,
        vmem=40 * MIB,
    )

    if fast:
        shard = lambda height, columns: struct((height // blocks, columns), F32)
        keep, keep_rest, send, send_rest = feature_shares
        got_rest = swap(send_rest, "rows", blocks, 1)
        got = swap(send, "rows", blocks, 1)
        one = [(q,) for q in range(blocks // 2)]
        lines = sum_parts(row_parts, one, "sum_tab_rows", [keep_rest])
        row_parts = exchange(lines, "rows", blocks, 2)
        parts = sum_parts([keep_rest, got_rest], [(u,) for u in range(tabs - 1)], "sum_core_features", [lines[0]], 0)
        parts = [keep, got] + [swap(parts[u - 1][0], "tab", tabs, u) for u in range(1, tabs)]
        lines = sum_parts(parts, one, "sum_tab_features")
        parts = exchange(lines, "rows", blocks, 2)
        (own_rows,) = sum_parts(row_parts, [(0,)], "sum_rows_rows", [lines[0]])
        row_pieces = exchange([own_rows[0]] * tabs, "tab", tabs, 1)
        (own,) = sum_parts(parts, [(0,)], "sum_rows_features", [own_rows])
        pieces = exchange([own[0]] * tabs, "tab", tabs, 1)
        wide = hidden + tall * width
        moves = [(1, 0), (tall, hidden), (1, wide), (1, wide + 3 * width)]
        outs = [shard(width, hidden), shard(hidden, width), shard(width, 3 * width), shard(width, width)]
        grad_up, grad_down, grad_row_qkv, grad_row_out = place(idx, row_pieces, moves, outs, tabs, "place_rows", [])
        moves = [(1, 0), (1, 3 * width), (1, 4 * width)]
        outs = [shard(width, 3 * width), shard(width, width), shard(width, 128)]
        grad_feature_qkv, grad_feature_out, columns = place(idx, pieces, moves, outs, tabs, "place_features", [grad_up])
        gains = columns.T
    else:
        scatter = lambda a, axis: lax.psum_scatter(a, "rows", scatter_dimension=axis, tiled=True)
        gains = lax.psum(scatter(gains, 1), "tab")
        weights = lax.psum([scatter(w, 0) for w in [*row_shares, *feature_shares]], "tab")
        grad_up, grad_down, grad_row_qkv, grad_row_out, grad_feature_qkv, grad_feature_out = weights
    return (
        output[None],
        grad_cells[None],
        gains[1],
        gains[0],
        grad_feature_qkv,
        grad_feature_out,
        gains[2],
        grad_row_qkv,
        grad_row_out,
        gains[3],
        grad_up,
        grad_down,
    )


def solution(mesh):
    in_specs = (
        P("tab", "rows", None, None),
        P("tab", "rows", None),
        P("tab", "rows"),
        P(),
        P(),
        P(),
        P(),
        P(),
        P(),
        P(),
        P(),
        P(),
        P(),
        P("tab", "rows", None, None),
    )
    out_specs = (
        P("tab", "rows", None, None),
        P("tab", "rows", None, None),
        P("rows"),
        P("rows"),
        P("rows", None),
        P("rows", None),
        P("rows"),
        P("rows", None),
        P("rows", None),
        P("rows"),
        P("rows", None),
        P("rows", None),
    )
    return jax.shard_map(
        functools.partial(per_device, mesh.shape["tab"], mesh.shape["rows"]),
        mesh=mesh,
        in_specs=in_specs,
        out_specs=out_specs,
        check_vma=False,
    )
```

```python
import functools
import math

import jax
import jax.numpy as jnp
from jax import lax
from jax.experimental import pallas as pl
from jax.experimental.pallas import tpu as pltpu
from jax.sharding import PartitionSpec as P

HEADS = 4
CTX_DEV = 4
EPSILON = 1e-05
MASKED = -1e30
F32 = jnp.float32
BF16 = jnp.bfloat16
GROUP_ROWS = 8
MIB = 1024 * 1024
VMEM_LIMIT = 24 * MIB


def dot_nn(left, right):
    return lax.dot_general(left, right, (((1,), (0,)), ((), ())), preferred_element_type=F32)


def dot_nt(left, right):
    return lax.dot_general(left, right, (((1,), (1,)), ((), ())), preferred_element_type=F32)


def dot_tn(left, right):
    return lax.dot_general(left, right, (((0,), (0,)), ((), ())), preferred_element_type=F32)


def normalize(tensor):
    row_mean = jnp.mean(tensor, axis=-1, keepdims=True)
    centred = tensor - row_mean
    scale = lax.rsqrt(jnp.mean(centred * centred, axis=-1, keepdims=True) + EPSILON)
    return centred * scale, scale


def norm_back(xhat, scale, gain, gradient):
    scaled = gradient * gain
    first = jnp.mean(scaled, axis=-1, keepdims=True)
    second = jnp.mean(scaled * xhat, axis=-1, keepdims=True)
    return scale * (scaled - first - xhat * second)


def column_sum(tensor):
    rows, width = tensor.shape
    return jnp.sum(tensor.reshape(rows // 8, 8, width), axis=0)


def missing_column(mask, first, rows):
    features, lanes = mask.shape
    shape = (rows, features, lanes)
    pick = lax.broadcasted_iota(jnp.int32, shape, 2) == first + lax.broadcasted_iota(jnp.int32, shape, 0)
    spread = jnp.broadcast_to(mask.astype(F32)[None], shape)
    return jnp.sum(jnp.where(pick, spread, 0.0), axis=-1, keepdims=True)


def vector(ref, at):
    count = ref.shape[0] // 4
    return jnp.concatenate([ref[at * count + i : at * count + i + 1, :] for i in range(count)], axis=1)


def start_cells(cells, mask, first, missing):
    rows, features, width = cells.shape
    absent = missing_column(mask, first, rows) > 0.5
    return jnp.where(absent, missing.reshape(1, 1, width), cells.astype(F32)).reshape(rows * features, width), absent


def same_row_bias(size, features):
    shape = (size, size)
    left = lax.broadcasted_iota(jnp.int32, shape, 0) // features
    right = lax.broadcasted_iota(jnp.int32, shape, 1) // features
    return jnp.where(left == right, 0.0, MASKED)


def head_parts(packed, part, group, head):
    cells, width = packed.shape[0], packed.shape[1] // 3
    return [
        packed[low : low + group, part * width + h * head : part * width + (h + 1) * head]
        for low in range(0, cells, group)
        for h in range(HEADS)
    ]


def join_parts(parts):
    rows = [jnp.concatenate(parts[at : at + HEADS], axis=1) for at in range(0, len(parts), HEADS)]
    return jnp.concatenate(rows, axis=0)


def softmax_keys(scores):
    exp_terms = jnp.exp(scores - jnp.max(scores, axis=1, keepdims=True))
    return exp_terms * (1.0 / jnp.sum(exp_terms, axis=1, keepdims=True))


def feature_forward(start, gain, w_qkv, w_out, features, group):
    cells, width = start.shape
    head = width // HEADS
    xhat, _ = normalize(start)
    qkv = dot_nn((xhat * gain).astype(BF16), w_qkv).astype(BF16)
    queries, keys, values = (head_parts(qkv, part, group, head) for part in range(3))
    scores = jnp.stack([dot_nt(key, query) for key, query in zip(keys, queries)])
    probs = softmax_keys(scores * (head**-0.5) + same_row_bias(group, features)[None]).astype(BF16)
    att = join_parts([dot_tn(probs[at], value).astype(BF16) for at, value in enumerate(values)])
    return start + dot_nn(att, w_out), qkv, probs, att


def context_kernel(count_ref, cells_ref, mask_ref, vectors_ref, w_qkv_ref, w_out_ref, send_ref, after_ref):
    rows, features, width = cells_ref.shape
    cells = rows * features
    start, _ = start_cells(cells_ref[...], mask_ref[...], 0, vector(vectors_ref, 0))
    after, _, _, _ = feature_forward(start, vector(vectors_ref, 1), w_qkv_ref[...], w_out_ref[...], features, cells)
    after_ref[...] = after
    xhat, _ = normalize(after)
    send_ref[0:cells, :] = (xhat * vector(vectors_ref, 2)).astype(BF16)
    count = count_ref[0, 0].astype(F32)
    send_ref[cells : cells + 16, :] = jnp.full((16, width), count, F32).astype(BF16)


def feature_kernel(
    cells_ref, mask_ref, upstream_ref, vectors_ref, w_qkv_ref, w_out_ref,
    after_ref, upstream_t_ref, qkv_ref, probs_ref, att_ref,
):
    rows, features, width = cells_ref.shape
    start, _ = start_cells(cells_ref[...], mask_ref[...], pl.program_id(0) * rows, vector(vectors_ref, 0))
    after, qkv, probs, att = feature_forward(
        start, vector(vectors_ref, 1), w_qkv_ref[...], w_out_ref[...], features, GROUP_ROWS * features
    )
    qkv_ref[...] = qkv
    probs_ref[...] = probs.reshape(probs_ref.shape)
    att_ref[...] = att
    after_ref[...] = jnp.swapaxes(after.reshape(rows, features, width), 0, 1)
    upstream_t_ref[...] = jnp.swapaxes(upstream_ref[...].astype(F32), 0, 1).astype(BF16)


def head_blocks(tensor):
    keys, width = tensor.shape
    tiled = jnp.concatenate([tensor] * HEADS, axis=0)
    row_head = lax.broadcasted_iota(jnp.int32, tiled.shape, 0) // keys
    lane_head = lax.broadcasted_iota(jnp.int32, tiled.shape, 1) // (width // HEADS)
    return jnp.where(row_head == lane_head, tiled, jnp.zeros_like(tiled))


def own_heads(tensor, keys):
    head = tensor.shape[1] // HEADS
    return jnp.concatenate([tensor[h * keys : (h + 1) * keys, h * head : (h + 1) * head] for h in range(HEADS)], axis=1)


def gelu_parts(inner):
    const = 0.7978845608028654
    cubic = const * 0.044715
    inner = inner.astype(BF16)
    square = inner * inner
    half = 0.5 + 0.5 * jnp.tanh(inner * (const + cubic * square))
    hidden = inner * half
    slope = half + (hidden - hidden * half) * (2.0 * const + (6.0 * cubic) * square)
    return hidden, slope


def read_slots(gathered, idx_ref, slots_ref, bias_ref, features):
    keys, width = slots_ref.shape[1], slots_ref.shape[2]
    blocks = keys // CTX_DEV
    block = CTX_DEV * features
    piece = block + 16
    slot = lax.broadcasted_iota(jnp.int32, (keys, 128), 0)
    counts = jnp.zeros((keys, 128), F32)
    core, line = idx_ref[1] % 2, idx_ref[1] // 2
    for pair in range(blocks // 2):
        if len(gathered) == 2:
            mine, other = (ref[pair * piece : (pair + 1) * piece, :].astype(F32) for ref in gathered)
            even, odd = jnp.where(core == 0, mine, other), jnp.where(core == 0, other, mine)
            at = line ^ pair
        else:
            even, odd = (gathered[0][(2 * pair + j) * piece : (2 * pair + j + 1) * piece, :].astype(F32) for j in range(2))
            at = pair
        both = jnp.concatenate([even[0:block], odd[0:block]], axis=0).reshape(2 * CTX_DEV, features, width)
        slots_ref[:, pl.ds(pl.multiple_of(at * 2 * CTX_DEV, 2 * CTX_DEV), 2 * CTX_DEV), :] = jnp.swapaxes(both, 0, 1)
        for j, part in enumerate((even, odd)):
            counts = jnp.where(slot // CTX_DEV == 2 * at + j, part[block : block + 1, 0:128], counts)
    bias = jnp.where((slot % CTX_DEV).astype(F32) < counts, 0.0, MASKED)
    bias_ref[...] = jnp.concatenate([bias] * HEADS, axis=0)


def emit(idx_ref, keep, send, sources):
    tab, block = idx_ref[0], idx_ref[1]
    core, line = block % 2, block // 2
    lines, rows, _ = keep[0].shape
    tabs = keep[1].shape[0] + 1
    for u in range(tabs):
        for q in range(lines):
            for refs, shard in ((keep, core), (send, 1 - core)):
                ref = refs[0].at[q] if u == 0 else refs[1].at[u - 1, q]
                for acc, column in sources:
                    height, width = acc.shape
                    part = height // (2 * lines * tabs)
                    low = (((line ^ q) * 2 + shard) * tabs + (tab ^ u)) * part
                    for at in range(part // rows):
                        low_at = pl.multiple_of(low + at * rows, rows)
                        ref[:, column + at * width : column + (at + 1) * width] = acc[pl.ds(low_at, rows), :].astype(BF16)


def rows_kernel(pieces, fast, *refs):
    (idx_ref, after_ref, upstream_ref, vectors_ref, w_row_ref, w_out_ref, w_up_hbm, w_down_hbm), refs = refs[:8], refs[8:]
    gathered, refs = refs[:pieces], refs[pieces:]
    (output_ref, grad_after_ref, gains_ref), refs = refs[:3], refs[3:]
    slot_outs, refs = (refs[:2], refs[2:]) if fast else (refs[:1], refs[1:])
    if fast:
        outs, refs = refs[:4], refs[4:]
        stages, copies, refs = refs[-9:-1], refs[-1], refs[:-9]
    *refs, w_up_ref, w_down_ref, loads = refs
    grad_up, grad_down, grad_qkv, grad_out, slots_ref, bias_ref, gain_acc = refs
    feats, rows, width = after_ref.shape
    features, keys, _ = slots_ref.shape
    hidden_all = w_up_ref.shape[1]
    cells = feats * rows
    head = width // HEADS
    step = pl.program_id(0)
    gain_row, gain_mlp = vector(vectors_ref, 2), vector(vectors_ref, 3)

    last = pl.num_programs(0) - 1
    fetches = [
        pltpu.make_async_copy(source, target, loads.at[at])
        for at, (source, target) in enumerate(((w_up_hbm, w_up_ref), (w_down_hbm, w_down_ref)))
    ]

    @pl.when(step == 0)
    def _():
        for fetch in fetches:
            fetch.start()
        read_slots(gathered, idx_ref, slots_ref, bias_ref, features)
        for ref in (grad_qkv, grad_out, grad_up, grad_down, gain_acc):
            ref[...] = jnp.zeros_like(ref)

    after = after_ref[...].reshape(cells, width)
    xhat2, scale2 = normalize(after)
    normed_two = (xhat2 * gain_row).astype(BF16)
    query = dot_nn(normed_two, w_row_ref[:, 0:width]).astype(BF16)
    slots = slots_ref[pl.ds(step * feats, feats)].reshape(feats * keys, width).astype(BF16)
    kv = dot_nn(slots, w_row_ref[:, width : 3 * width]).astype(BF16)
    keys_b = [head_blocks(kv[f * keys : (f + 1) * keys, 0:width]) for f in range(feats)]
    values_b = [head_blocks(kv[f * keys : (f + 1) * keys, width : 2 * width]) for f in range(feats)]
    query_f = [query[f * rows : (f + 1) * rows] for f in range(feats)]
    scores = jnp.stack([dot_nt(keys_b[f], query_f[f]) for f in range(feats)])
    scores = scores * (head**-0.5) + bias_ref[:, 0:rows][None]
    probs = softmax_keys(scores.reshape(feats * HEADS, keys, rows))
    probs_b = probs.reshape(feats, HEADS * keys, rows).astype(BF16)
    att = jnp.concatenate([dot_tn(probs_b[f], values_b[f]).astype(BF16) for f in range(feats)], axis=0)
    after_two = after + dot_nn(att, w_out_ref[...])

    @pl.when(step == 0)
    def _():
        for fetch in fetches:
            fetch.wait()

    xhat3, scale3 = normalize(after_two)
    normed_three = (xhat3 * gain_mlp).astype(BF16)
    upstream = upstream_ref[...].reshape(cells, width)
    piece = 256
    hidden, grad_inner = [], []
    first = lambda at: (dot_nn(normed_three, w_up_ref[:, at : at + piece]), dot_nt(upstream, w_down_ref[at : at + piece, :]))
    ahead = first(0)
    for at in range(0, hidden_all, piece):
        inner, back = ahead
        if at + piece < hidden_all:
            ahead = first(at + piece)
        part, slope = gelu_parts(inner)
        hidden.append(part)
        grad_inner.append(back.astype(BF16) * slope)
    hidden = jnp.concatenate(hidden, axis=1)
    grad_inner = jnp.concatenate(grad_inner, axis=1)
    total = after_two + dot_nn(hidden, w_down_ref[...])
    grad3 = dot_nt(grad_inner, w_up_ref[...])
    grad_down[...] += dot_tn(hidden, upstream)
    grad_up[...] += dot_tn(normed_three, grad_inner)
    output_ref[...] = total.astype(BF16).reshape(feats, rows, width)
    gain_acc[0] += column_sum(grad3 * xhat3)
    grad_two = upstream.astype(F32) + norm_back(xhat3, scale3, gain_mlp, grad3)

    if fast:
        wide, narrow = stages[0].shape[-1], stages[4].shape[-1]
        sends = []
        for at, stage in enumerate(stages):
            low, size = (0, wide) if at < 4 else (wide, narrow)
            lead = (slice(None),) * (len(stage.shape) - 1)
            sends.append(pltpu.make_async_copy(stage, outs[at % 4].at[(*lead, pl.ds(low, size))], copies.at[at]))

        @pl.when(step == last)
        def _():
            emit(idx_ref, stages[0:2], stages[2:4], [(grad_up, 0), (grad_down, hidden_all)])
            for send in sends[0:4]:
                send.start()

    branch = grad_two.astype(BF16)
    grad_out[...] += dot_tn(att, branch)
    grad_att = dot_nt(branch, w_out_ref[...]).astype(BF16)
    grad_f = [grad_att[f * rows : (f + 1) * rows] for f in range(feats)]
    grad_probs = jnp.stack([dot_nt(values_b[f], grad_f[f]) for f in range(feats)]).reshape(feats * HEADS, keys, rows)
    grad_scores = probs * (grad_probs - jnp.sum(grad_probs * probs, axis=1, keepdims=True))
    grad_scores = grad_scores.reshape(feats, HEADS * keys, rows).astype(BF16)
    grad_query = jnp.concatenate([dot_tn(grad_scores[f], keys_b[f]) for f in range(feats)], axis=0)
    grad_query = (grad_query * (head**-0.5)).astype(BF16)
    grad_keys = [own_heads(dot_nn(grad_scores[f], query_f[f]), keys) for f in range(feats)]
    grad_values = [own_heads(dot_nn(probs_b[f], grad_f[f]), keys) for f in range(feats)]
    grad_kv = jnp.concatenate(
        [jnp.concatenate(grad_keys, axis=0) * (head**-0.5), jnp.concatenate(grad_values, axis=0)], axis=1
    ).astype(BF16)
    grad_qkv[:, 0:width] += dot_tn(normed_two, grad_query)
    grad_qkv[:, width : 3 * width] += dot_tn(slots, grad_kv)
    slots_ref[pl.ds(step * feats, feats)] = dot_nt(grad_kv, w_row_ref[:, width : 3 * width]).reshape(feats, keys, width)
    grad_normed = dot_nt(grad_query, w_row_ref[:, 0:width])
    gain_acc[1] += column_sum(grad_normed * xhat2)
    grad_after_ref[...] = (grad_two + norm_back(xhat2, scale2, gain_row, grad_normed)).reshape(feats, rows, width)

    @pl.when(step == last)
    def _():
        if fast:
            emit(idx_ref, stages[4:6], stages[6:8], [(grad_qkv, 0), (grad_out, 3 * width)])
            for send in sends[4:8]:
                send.start()
        gains_ref[...] = gain_acc[...]
        block = CTX_DEV * features
        core, line = idx_ref[1] % 2, idx_ref[1] // 2
        for q in range(keys // (2 * CTX_DEV)):
            low = pl.multiple_of((line ^ q) * 2 * CTX_DEV, 2 * CTX_DEV) if fast else q * 2 * CTX_DEV
            both = jnp.swapaxes(slots_ref[:, pl.ds(low, 2 * CTX_DEV), :], 0, 1).reshape(2 * block, width)
            if fast:
                even, odd = both[0:block], both[block:]
                slot_outs[0][q] = jnp.where(core == 0, even, odd).astype(BF16)
                slot_outs[1][q] = jnp.where(core == 0, odd, even).astype(BF16)
            else:
                slot_outs[0][2 * q * block : 2 * (q + 1) * block, :] = both.astype(BF16)
        if fast:
            for send in sends:
                send.wait()


def feature_backward(grad_one, packed, probs_b, att, start, gain, w_qkv, w_out, group):
    cells, width = start.shape
    head = width // HEADS
    branch = grad_one.astype(BF16)
    grad_w_out = dot_tn(att, branch)
    grad_att = dot_nt(branch, w_out).astype(BF16)
    queries, keys, values = (head_parts(packed, part, group, head) for part in range(3))
    grads = [
        grad_att[low : low + group, h * head : (h + 1) * head] for low in range(0, cells, group) for h in range(HEADS)
    ]
    probs = probs_b.astype(F32)
    grad_probs = jnp.stack([dot_nt(value, grad) for value, grad in zip(values, grads)])
    grad_scores = probs * (grad_probs - jnp.sum(grad_probs * probs, axis=1, keepdims=True))
    grad_scores = grad_scores.astype(BF16)
    grad_queries = join_parts([dot_tn(grad_scores[at], key) for at, key in enumerate(keys)]) * (head**-0.5)
    grad_keys = join_parts([dot_nn(grad_scores[at], query) for at, query in enumerate(queries)]) * (head**-0.5)
    grad_values = join_parts([dot_nn(probs_b[at], grad) for at, grad in enumerate(grads)])
    grad_qkv = jnp.concatenate([grad_queries.astype(BF16), grad_keys.astype(BF16), grad_values.astype(BF16)], axis=1)
    xhat, scale = normalize(start)
    grad_w_qkv = dot_tn((xhat * gain).astype(BF16), grad_qkv)
    grad_normed = dot_nt(grad_qkv, w_qkv)
    grad_start = grad_one + norm_back(xhat, scale, gain, grad_normed)
    return grad_w_qkv, grad_w_out, column_sum(grad_normed * xhat), grad_start


def feature_backward_kernel(slots, waits, fast, *refs):
    (
        idx_ref, cells_ref, mask_ref, vectors_ref, w_qkv_ref, w_out_ref, grad_after_ref, qkv_ref, probs_ref, att_ref,
        after_ref, row_gains,
    ), refs = refs[:12], refs[12:]
    slot_refs, refs = refs[:slots], refs[slots + waits :]
    (grad_cells_ref, gains_ref), refs = refs[:2], refs[2:]
    if fast:
        outs, refs = refs[:4], refs[4:]
    grad_w_qkv, grad_w_out, gains, columns, extra_ref = refs
    rows, features, width = cells_ref.shape
    cells = rows * features
    block = CTX_DEV * features
    group = GROUP_ROWS * features
    step = pl.program_id(0)

    @pl.when(step == 0)
    def _():
        for ref in (grad_w_qkv, grad_w_out, gains):
            ref[...] = jnp.zeros_like(ref)
        total = slot_refs[0][...].astype(F32)
        for ref in slot_refs[1:]:
            total = total + ref[...].astype(F32)
        xhat, scale = normalize(after_ref[...])
        extra_ref[...] = norm_back(xhat, scale, vector(vectors_ref, 2), total)
        gains[2] = row_gains[1] + column_sum(total * xhat)
        gains[3] = row_gains[0]

    @pl.when(step > 0)
    def _():
        extra_ref[...] = jnp.zeros_like(extra_ref)

    grad_one = jnp.swapaxes(grad_after_ref[...], 0, 1).reshape(cells, width)
    grad_one = jnp.concatenate([grad_one[0:block] + extra_ref[...], grad_one[block:]], axis=0)
    start, absent = start_cells(cells_ref[...], mask_ref[...], step * rows, vector(vectors_ref, 0))
    add_qkv, add_out, add_gain, grad_start = feature_backward(
        grad_one, qkv_ref[...], probs_ref[...].reshape(cells // group * HEADS, group, group), att_ref[...],
        start, vector(vectors_ref, 1), w_qkv_ref[...], w_out_ref[...], group,
    )
    grad_w_qkv[...] += add_qkv
    grad_w_out[...] += add_out
    gains[0] += add_gain
    grad_start = grad_start.reshape(rows, features, width)
    grad_cells_ref[...] = jnp.where(absent, 0.0, grad_start)
    gains[1] += column_sum(jnp.where(absent, grad_start, 0.0).reshape(cells, width))

    @pl.when(step == pl.num_programs(0) - 1)
    def _():
        sums = jnp.concatenate([jnp.sum(gains[at], axis=0, keepdims=True) for at in range(4)], axis=0)
        gains_ref[...] = sums
        if fast:
            columns[...] = jnp.concatenate([sums, jnp.zeros((124, width), F32)], axis=0).T
            emit(idx_ref, outs[0:2], outs[2:4], [(grad_w_qkv, 0), (grad_w_out, 3 * width), (columns, 4 * width)])


def output_kernel(output_t_ref, output_ref):
    output_ref[...] = jnp.swapaxes(output_t_ref[...].astype(F32), 0, 1).astype(BF16)


def join_kernel(count, *refs):
    rows = refs[0].shape[0]
    for at in range(count):
        refs[-1][at * rows : (at + 1) * rows, :] = refs[at][...]


def sum_kernel(count, groups, *refs):
    ins, outs = refs[:count], refs[len(refs) - len(groups) :]
    for group, out in zip(groups, outs):
        for at, part in enumerate(group):
            total = ins[0][part].astype(F32)
            for ref in ins[1:]:
                total = total + ref[part].astype(F32)
            out[at] = total.astype(BF16)


def whole(array):
    zeros = (0,) * array.ndim
    return pl.BlockSpec(array.shape, lambda i: zeros, pipeline_mode=pl.Buffered(1))


def whole_out(shape):
    zeros = (0,) * len(shape)
    return pl.BlockSpec(shape, lambda i: zeros, pipeline_mode=pl.Buffered(1))


def tiles(shape, axis, offset=0):
    def index(i):
        return tuple(i + offset if d == axis else 0 for d in range(len(shape)))

    return pl.BlockSpec(shape, index)


WAITS = 1e14
SCALARS = pl.BlockSpec(memory_space=pltpu.SMEM)
UNTOUCHED = pl.BlockSpec(memory_space=pl.ANY)


def struct(shape, dtype):
    return jax.ShapeDtypeStruct(shape, dtype)


def in_hbm(array):
    return pltpu.with_memory_space_constraint(array, pltpu.HBM)


def call(kernel, name, grid, args, in_specs, outs, out_specs, scratch, flops, aliases=None, vmem=VMEM_LIMIT, pinned=True):
    small = 1 << 15
    large = lambda a: pinned and math.prod(a.shape) >= 1 << 18
    args = [pltpu.with_memory_space_constraint(a, pltpu.HBM) if large(a) else a for a in args]
    outs = [pltpu.HBM(o.shape, o.dtype) if large(o) else o for o in outs]
    sizes = [math.prod(a.shape) * a.dtype.itemsize for a in [*args, *outs]]
    return pl.pallas_call(
        kernel,
        grid=(grid,),
        in_specs=in_specs,
        out_shape=outs,
        out_specs=out_specs,
        scratch_shapes=scratch,
        input_output_aliases=aliases or {},
        compiler_params=pltpu.CompilerParams(vmem_limit_bytes=vmem, dimension_semantics=("arbitrary",)),
        cost_estimate=pl.CostEstimate(flops=int(flops), bytes_accessed=int(sum(sizes)), transcendentals=0),
        name=name,
    )(*args)


def xor_pairs(size, bit):
    return [(i, i ^ bit) for i in range(size)]


def swap(array, axis, size, bit):
    return lax.ppermute(array, axis, xor_pairs(size, bit))


def add_all(terms):
    total = terms[0].astype(F32)
    for term in terms[1:]:
        total = total + term.astype(F32)
    return total.astype(BF16)


def exchange(parts, axis, size, unit):
    return [parts[0]] + [swap(parts[at], axis, size, at * unit) for at in range(1, len(parts))]


def sum_parts(parts, groups, name, after=(), flops=WAITS):
    outs = [struct((len(group), *parts[0].shape[1:]), BF16) for group in groups]
    return call(
        functools.partial(sum_kernel, len(parts), groups),
        name,
        1,
        [*parts, *after],
        [whole(a) for a in parts] + [UNTOUCHED] * len(after),
        outs,
        [whole_out(o.shape) for o in outs],
        [],
        flops,
        pinned=False,
    )


def place_kernel(tabs, moves, *refs):
    idx_ref, ins, outs = refs[0], refs[1 : 1 + tabs], refs[len(refs) - len(moves) :]
    tab = idx_ref[0]
    for out, (count, column) in zip(outs, moves):
        width = out.shape[1]
        for u in range(tabs):
            rows = ins[u].shape[0]
            for at in range(count):
                low = pl.multiple_of(((tab ^ u) * count + at) * rows, 16)
                out[pl.ds(low, rows), :] = ins[u][:, column + at * width : column + (at + 1) * width].astype(F32)


def place(idx, pieces, moves, outs, tabs, name, after):
    return call(
        functools.partial(place_kernel, tabs, moves),
        name,
        1,
        [idx, *pieces, *after],
        [SCALARS] + [whole(a) for a in pieces] + [UNTOUCHED] * len(after),
        outs,
        [whole_out(o.shape) for o in outs],
        [],
        WAITS,
        pinned=False,
    )


def per_device(
    tabs,
    blocks,
    cells,
    missing_mask,
    context_counts,
    missing_embedding,
    gain_feature,
    w_feature_qkv,
    w_feature_out,
    gain_row,
    w_row_qkv,
    w_row_out,
    gain_mlp,
    w_up,
    w_down,
    upstream,
):
    _, rows, features, width = cells.shape
    hidden = w_up.shape[1]
    keys = CTX_DEV * blocks
    cells, mask, upstream = cells[0], jnp.swapaxes(missing_mask[0], 0, 1), upstream[0]
    mask = in_hbm(mask)
    vectors = jnp.concatenate([missing_embedding, gain_feature, gain_row, gain_mlp]).astype(F32).reshape(-1, 128)
    all_cells = rows * features
    cost = all_cells * width * width
    fast = tabs == 4 and blocks == 8 and width == 16 * tabs * blocks and hidden % (16 * tabs * blocks) == 0
    tall = hidden // (16 * tabs * blocks)
    idx = jnp.stack([lax.axis_index("tab"), lax.axis_index("rows")]).astype(jnp.int32)

    block = CTX_DEV * features
    piece_rows = block + 16
    payload, after_ctx = call(
        context_kernel,
        "context_rows",
        1,
        [context_counts, cells, mask, vectors, w_feature_qkv, w_feature_out],
        [SCALARS, pl.BlockSpec((CTX_DEV, features, width), lambda i: (0, 0, 0))]
        + [whole(a) for a in (mask, vectors, w_feature_qkv, w_feature_out)],
        [struct((piece_rows, width), BF16), struct((block, width), F32)],
        [whole_out((piece_rows, width)), whole_out((block, width))],
        [],
        2 * block * width * 4 * width,
    )
    if fast:
        received = exchange([payload] * (blocks // 2), "rows", blocks, 2)


    tile = min(32, rows)
    steps = rows // tile
    groups = tile // GROUP_ROWS
    group = GROUP_ROWS * features
    after_one, upstream_t, qkv, probs, att = call(
        feature_kernel,
        "feature_forward",
        steps,
        [cells, mask, upstream, vectors, w_feature_qkv, w_feature_out],
        [tiles((tile, features, width), 0), whole(mask), tiles((tile, features, width), 0)]
        + [whole(a) for a in (vectors, w_feature_qkv, w_feature_out)],
        [
            struct((features, rows, width), F32),
            struct((features, rows, width), BF16),
            struct((all_cells, 3 * width), BF16),
            struct((rows // GROUP_ROWS, HEADS, group, group), BF16),
            struct((all_cells, width), BF16),
        ],
        [
            tiles((features, tile, width), 1),
            tiles((features, tile, width), 1),
            tiles((tile * features, 3 * width), 0),
            tiles((groups, HEADS, group, group), 0),
            tiles((tile * features, width), 0),
        ],
        [],
        2 * 5 * cost,
    )

    if fast:
        mine = call(
            functools.partial(join_kernel, len(received)),
            "join",
            1,
            received + [att],
            [whole(a) for a in received] + [UNTOUCHED],
            [struct((len(received) * piece_rows, width), BF16)],
            [whole_out((len(received) * piece_rows, width))],
            [],
            0,
        )[0]
        gathered = [mine, swap(mine, "rows", blocks, 1)]
    else:
        gathered = [lax.all_gather(payload, "rows", axis=0, tiled=True)]

    feats = 4
    cell_tile = (feats, rows, width)
    full = [struct(s, F32) for s in ((width, hidden), (hidden, width), (width, 3 * width), (width, width))]
    if fast:
        share = lambda w: [(blocks // 2, 16, w), (tabs - 1, blocks // 2, 16, w)] * 2
        shares = [struct(s, BF16) for s in share(hidden + (4 + tall) * width)]
        stages = [pltpu.VMEM(s, BF16) for w in (hidden + tall * width, 4 * width) for s in share(w)]
        stages += [pltpu.SemaphoreType.DMA((8,))]
    else:
        shares = full
    weights = [vectors, w_row_qkv, w_row_out, w_up, w_down]
    slot_outs = [struct((blocks // 2, block, width), BF16)] * 2 if fast else [struct((keys * features, width), BF16)]
    output_t, grad_after, row_gains, *row_shares = call(
        functools.partial(rows_kernel, len(gathered), fast),
        "rows_and_feed_forward",
        features // feats,
        [idx, after_one, upstream_t] + weights + gathered,
        [SCALARS] + [tiles(cell_tile, 0)] * 2 + [whole(a) for a in weights[:3]] + [UNTOUCHED] * 2 + [whole(a) for a in gathered],
        [
            struct((features, rows, width), BF16),
            struct((features, rows, width), F32),
            struct((2, 8, width), F32),
        ]
        + slot_outs
        + shares,
        [tiles(cell_tile, 0)] * 2
        + [whole_out((2, 8, width))]
        + [whole_out(s.shape) for s in slot_outs]
        + [UNTOUCHED if fast else whole_out(s.shape) for s in shares],
        [pltpu.VMEM(s.shape, F32) for s in (full if fast else [])]
        + [pltpu.VMEM(s, F32) for s in ((features, keys, width), (HEADS * keys, 128), (2, 8, width))]
        + [pltpu.VMEM(a.shape, BF16) for a in (w_up, w_down)]
        + [pltpu.SemaphoreType.DMA((2,))]
        + (stages if fast else []),
        2 * 34 * cost,
        vmem=(48 if fast else 62) * MIB,
    )
    slot_parts, row_shares = row_shares[: len(slot_outs)], row_shares[len(slot_outs) :]
    output = call(
        output_kernel,
        "output",
        steps,
        [output_t],
        [tiles((features, tile, width), 1)],
        [struct((rows, features, width), BF16)],
        [tiles((tile, features, width), 0)],
        [],
        0,
    )[0]
    if fast:
        keep, keep_rest, send, send_rest = row_shares
        got_rest = swap(send_rest, "rows", blocks, 1)
        parts = [add_all([keep_rest[u], got_rest[u]]) for u in range(tabs - 1)]
        got = swap(send, "rows", blocks, 1)
        row_parts = [keep, got] + [swap(parts[u - 1], "tab", tabs, u) for u in range(1, tabs)]
        slot_parts = [slot_parts[0], swap(slot_parts[1], "rows", blocks, 1)]
        slot_parts = sum_parts(slot_parts, [(q,) for q in range(blocks // 2)], "sum_core_slots", [parts[0], got])
        own_slots = exchange([part[0] for part in slot_parts], "rows", blocks, 2)
    else:
        own_slots = [lax.psum_scatter(slot_parts[0], "rows", scatter_dimension=0, tiled=True)]

    weights = [mask, vectors, w_feature_qkv, w_feature_out]
    sums = [struct((width, 3 * width), F32), struct((width, width), F32)]
    outs = [struct(s, BF16) for s in share(4 * width + 128)] if fast else sums
    waits = [output]
    rest = [after_ctx, row_gains, *own_slots]
    grad_cells, gains, *feature_shares = call(
        functools.partial(feature_backward_kernel, len(own_slots), len(waits), fast),
        "feature_backward",
        steps,
        [idx, cells] + weights + [grad_after, qkv, probs, att] + rest + waits,
        [SCALARS, tiles((tile, features, width), 0)]
        + [whole(a) for a in weights]
        + [
            tiles((features, tile, width), 1),
            tiles((tile * features, 3 * width), 0),
            tiles((groups, HEADS, group, group), 0),
            tiles((tile * features, width), 0),
        ]
        + [whole(a) for a in rest]
        + [UNTOUCHED] * len(waits),
        [struct((rows, features, width), F32), struct((4, width), F32)] + outs,
        [tiles((tile, features, width), 0), whole_out((4, width))] + [whole_out(o.shape) for o in outs],
        ([pltpu.VMEM(s.shape, F32) for s in sums] if fast else [])
        + [pltpu.VMEM(s, F32) for s in ((4, 8, width), (width, 128), (block, width))],
        0,
        vmem=40 * MIB,
    )

    if fast:
        shard = lambda height, columns: struct((height // blocks, columns), F32)
        keep, keep_rest, send, send_rest = feature_shares
        got_rest = swap(send_rest, "rows", blocks, 1)
        got = swap(send, "rows", blocks, 1)
        one = [(q,) for q in range(blocks // 2)]
        lines = sum_parts(row_parts, one, "sum_tab_rows", [in_hbm(keep_rest)])
        row_parts = exchange(lines, "rows", blocks, 2)
        parts = sum_parts([keep_rest, got_rest], [(u,) for u in range(tabs - 1)], "sum_core_features", [lines[0]], 0)
        parts = [keep, got] + [swap(parts[u - 1][0], "tab", tabs, u) for u in range(1, tabs)]
        lines = sum_parts(parts, one, "sum_tab_features")
        parts = exchange(lines, "rows", blocks, 2)
        (own_rows,) = sum_parts(row_parts, [(0,)], "sum_rows_rows", [lines[0]])
        row_pieces = exchange([own_rows[0]] * tabs, "tab", tabs, 1)
        (own,) = sum_parts(parts, [(0,)], "sum_rows_features", [own_rows])
        pieces = exchange([own[0]] * tabs, "tab", tabs, 1)
        wide = hidden + tall * width
        moves = [(1, 0), (tall, hidden), (1, wide), (1, wide + 3 * width)]
        outs = [shard(width, hidden), shard(hidden, width), shard(width, 3 * width), shard(width, width)]
        grad_up, grad_down, grad_row_qkv, grad_row_out = place(idx, row_pieces, moves, outs, tabs, "place_rows", [])
        moves = [(1, 0), (1, 3 * width), (1, 4 * width)]
        outs = [shard(width, 3 * width), shard(width, width), shard(width, 128)]
        grad_feature_qkv, grad_feature_out, columns = place(idx, pieces, moves, outs, tabs, "place_features", [in_hbm(grad_up)])
        gains = columns.T
    else:
        scatter = lambda a, axis: lax.psum_scatter(a, "rows", scatter_dimension=axis, tiled=True)
        gains = lax.psum(scatter(gains, 1), "tab")
        weights = lax.psum([scatter(w, 0) for w in [*row_shares, *feature_shares]], "tab")
        grad_up, grad_down, grad_row_qkv, grad_row_out, grad_feature_qkv, grad_feature_out = weights
    return (
        output[None],
        grad_cells[None],
        gains[1],
        gains[0],
        grad_feature_qkv,
        grad_feature_out,
        gains[2],
        grad_row_qkv,
        grad_row_out,
        gains[3],
        grad_up,
        grad_down,
    )


def solution(mesh):
    in_specs = (
        P("tab", "rows", None, None),
        P("tab", "rows", None),
        P("tab", "rows"),
        P(),
        P(),
        P(),
        P(),
        P(),
        P(),
        P(),
        P(),
        P(),
        P(),
        P("tab", "rows", None, None),
    )
    out_specs = (
        P("tab", "rows", None, None),
        P("tab", "rows", None, None),
        P("rows"),
        P("rows"),
        P("rows", None),
        P("rows", None),
        P("rows"),
        P("rows", None),
        P("rows", None),
        P("rows"),
        P("rows", None),
        P("rows", None),
    )
    return jax.shard_map(
        functools.partial(per_device, mesh.shape["tab"], mesh.shape["rows"]),
        mesh=mesh,
        in_specs=in_specs,
        out_specs=out_specs,
        check_vma=False,
    )
```

```python
import functools
import math

import jax
import jax.numpy as jnp
from jax import lax
from jax.experimental import pallas as pl
from jax.experimental.pallas import tpu as pltpu
from jax.sharding import PartitionSpec as P

HEADS = 4
CTX_DEV = 4
EPSILON = 1e-05
MASKED = -1e30
F32 = jnp.float32
BF16 = jnp.bfloat16
GROUP_ROWS = 8
MIB = 1024 * 1024
VMEM_LIMIT = 24 * MIB


def dot_nn(left, right):
    return lax.dot_general(left, right, (((1,), (0,)), ((), ())), preferred_element_type=F32)


def dot_nt(left, right):
    return lax.dot_general(left, right, (((1,), (1,)), ((), ())), preferred_element_type=F32)


def dot_tn(left, right):
    return lax.dot_general(left, right, (((0,), (0,)), ((), ())), preferred_element_type=F32)


def normalize(tensor):
    row_mean = jnp.mean(tensor, axis=-1, keepdims=True)
    centred = tensor - row_mean
    scale = lax.rsqrt(jnp.mean(centred * centred, axis=-1, keepdims=True) + EPSILON)
    return centred * scale, scale


def norm_back(xhat, scale, gain, gradient):
    scaled = gradient * gain
    first = jnp.mean(scaled, axis=-1, keepdims=True)
    second = jnp.mean(scaled * xhat, axis=-1, keepdims=True)
    return scale * (scaled - first - xhat * second)


def column_sum(tensor):
    rows, width = tensor.shape
    return jnp.sum(tensor.reshape(rows // 8, 8, width), axis=0)


def missing_column(mask, first, rows):
    features, lanes = mask.shape
    shape = (rows, features, lanes)
    pick = lax.broadcasted_iota(jnp.int32, shape, 2) == first + lax.broadcasted_iota(jnp.int32, shape, 0)
    spread = jnp.broadcast_to(mask.astype(F32)[None], shape)
    return jnp.sum(jnp.where(pick, spread, 0.0), axis=-1, keepdims=True)


def vector(ref, at):
    count = ref.shape[0] // 4
    return jnp.concatenate([ref[at * count + i : at * count + i + 1, :] for i in range(count)], axis=1)


def start_cells(cells, mask, first, missing):
    rows, features, width = cells.shape
    absent = missing_column(mask, first, rows) > 0.5
    return jnp.where(absent, missing.reshape(1, 1, width), cells.astype(F32)).reshape(rows * features, width), absent


def same_row_bias(size, features):
    shape = (size, size)
    left = lax.broadcasted_iota(jnp.int32, shape, 0) // features
    right = lax.broadcasted_iota(jnp.int32, shape, 1) // features
    return jnp.where(left == right, 0.0, MASKED)


def head_parts(packed, part, group, head):
    cells, width = packed.shape[0], packed.shape[1] // 3
    return [
        packed[low : low + group, part * width + h * head : part * width + (h + 1) * head]
        for low in range(0, cells, group)
        for h in range(HEADS)
    ]


def join_parts(parts):
    rows = [jnp.concatenate(parts[at : at + HEADS], axis=1) for at in range(0, len(parts), HEADS)]
    return jnp.concatenate(rows, axis=0)


def softmax_keys(scores):
    exp_terms = jnp.exp(scores - jnp.max(scores, axis=1, keepdims=True))
    return exp_terms * (1.0 / jnp.sum(exp_terms, axis=1, keepdims=True))


def dot_pieces(left, right, piece=256):
    return jnp.concatenate(
        [dot_nn(left, right[:, at : at + piece]).astype(BF16) for at in range(0, right.shape[1], piece)], axis=1
    )


def feature_forward(start, gain, w_qkv, w_out, features, group):
    cells, width = start.shape
    head = width // HEADS
    xhat, _ = normalize(start)
    qkv = dot_pieces((xhat * gain).astype(BF16), w_qkv)
    queries, keys, values = (head_parts(qkv, part, group, head) for part in range(3))
    scores = jnp.stack([dot_nt(key, query) for key, query in zip(keys, queries)])
    probs = softmax_keys(scores * (head**-0.5) + same_row_bias(group, features)[None]).astype(BF16)
    att = join_parts([dot_tn(probs[at], value).astype(BF16) for at, value in enumerate(values)])
    return start + dot_nn(att, w_out), qkv, probs, att


def context_kernel(count_ref, cells_ref, mask_ref, vectors_ref, w_qkv_ref, w_out_ref, send_ref, after_ref):
    rows, features, width = cells_ref.shape
    cells = rows * features
    start, _ = start_cells(cells_ref[...], mask_ref[...], 0, vector(vectors_ref, 0))
    after, _, _, _ = feature_forward(start, vector(vectors_ref, 1), w_qkv_ref[...], w_out_ref[...], features, cells)
    after_ref[...] = after
    xhat, _ = normalize(after)
    send_ref[0:cells, :] = (xhat * vector(vectors_ref, 2)).astype(BF16)
    count = count_ref[0, 0].astype(F32)
    send_ref[cells : cells + 16, :] = jnp.full((16, width), count, F32).astype(BF16)


def feature_kernel(
    cells_ref, mask_ref, upstream_ref, vectors_ref, w_qkv_ref, w_out_ref,
    after_ref, upstream_t_ref, qkv_ref, probs_ref, att_ref,
):
    rows, features, width = cells_ref.shape
    start, _ = start_cells(cells_ref[...], mask_ref[...], pl.program_id(0) * rows, vector(vectors_ref, 0))
    after, qkv, probs, att = feature_forward(
        start, vector(vectors_ref, 1), w_qkv_ref[...], w_out_ref[...], features, GROUP_ROWS * features
    )
    qkv_ref[...] = qkv
    probs_ref[...] = probs.reshape(probs_ref.shape)
    att_ref[...] = att
    after_ref[...] = jnp.swapaxes(after.reshape(rows, features, width), 0, 1)
    upstream_t_ref[...] = jnp.swapaxes(upstream_ref[...].astype(F32), 0, 1).astype(BF16)


def head_blocks(tensor):
    keys, width = tensor.shape
    tiled = jnp.concatenate([tensor] * HEADS, axis=0)
    row_head = lax.broadcasted_iota(jnp.int32, tiled.shape, 0) // keys
    lane_head = lax.broadcasted_iota(jnp.int32, tiled.shape, 1) // (width // HEADS)
    return jnp.where(row_head == lane_head, tiled, jnp.zeros_like(tiled))


def own_heads(tensor, keys):
    head = tensor.shape[1] // HEADS
    return jnp.concatenate([tensor[h * keys : (h + 1) * keys, h * head : (h + 1) * head] for h in range(HEADS)], axis=1)


def gelu_parts(inner):
    const = 0.7978845608028654
    cubic = const * 0.044715
    inner = inner.astype(BF16)
    square = inner * inner
    half = 0.5 + 0.5 * jnp.tanh(inner * (const + cubic * square))
    hidden = inner * half
    slope = half + (hidden - hidden * half) * (2.0 * const + (6.0 * cubic) * square)
    return hidden, slope


def read_slots(gathered, idx_ref, slots_ref, bias_ref, features):
    keys, width = slots_ref.shape[1], slots_ref.shape[2]
    blocks = keys // CTX_DEV
    block = CTX_DEV * features
    piece = block + 16
    slot = lax.broadcasted_iota(jnp.int32, (keys, 128), 0)
    counts = jnp.zeros((keys, 128), F32)
    core, line = idx_ref[1] % 2, idx_ref[1] // 2
    for pair in range(blocks // 2):
        if len(gathered) == 2:
            mine, other = (ref[pair * piece : (pair + 1) * piece, :].astype(F32) for ref in gathered)
            even, odd = jnp.where(core == 0, mine, other), jnp.where(core == 0, other, mine)
            at = line ^ pair
        else:
            even, odd = (gathered[0][(2 * pair + j) * piece : (2 * pair + j + 1) * piece, :].astype(F32) for j in range(2))
            at = pair
        both = jnp.concatenate([even[0:block], odd[0:block]], axis=0).reshape(2 * CTX_DEV, features, width)
        slots_ref[:, pl.ds(pl.multiple_of(at * 2 * CTX_DEV, 2 * CTX_DEV), 2 * CTX_DEV), :] = jnp.swapaxes(both, 0, 1)
        for j, part in enumerate((even, odd)):
            counts = jnp.where(slot // CTX_DEV == 2 * at + j, part[block : block + 1, 0:128], counts)
    bias = jnp.where((slot % CTX_DEV).astype(F32) < counts, 0.0, MASKED)
    bias_ref[...] = jnp.concatenate([bias] * HEADS, axis=0)


def emit(idx_ref, keep, send, sources):
    tab, block = idx_ref[0], idx_ref[1]
    core, line = block % 2, block // 2
    lines, rows, _ = keep[0].shape
    tabs = keep[1].shape[0] + 1
    for u in range(tabs):
        for q in range(lines):
            for refs, shard in ((keep, core), (send, 1 - core)):
                ref = refs[0].at[q] if u == 0 else refs[1].at[u - 1, q]
                for acc, column in sources:
                    height, width = acc.shape
                    part = height // (2 * lines * tabs)
                    low = (((line ^ q) * 2 + shard) * tabs + (tab ^ u)) * part
                    for at in range(part // rows):
                        low_at = pl.multiple_of(low + at * rows, rows)
                        ref[:, column + at * width : column + (at + 1) * width] = acc[pl.ds(low_at, rows), :].astype(BF16)


def rows_kernel(pieces, fast, *refs):
    (idx_ref, after_ref, upstream_ref, vectors_ref, w_row_ref, w_out_ref, w_up_hbm, w_down_hbm), refs = refs[:8], refs[8:]
    gathered, refs = refs[:pieces], refs[pieces:]
    (output_ref, grad_after_ref, gains_ref), refs = refs[:3], refs[3:]
    slot_outs, refs = (refs[:2], refs[2:]) if fast else (refs[:1], refs[1:])
    if fast:
        outs, refs = refs[:4], refs[4:]
        stages, copies, refs = refs[-9:-1], refs[-1], refs[:-9]
    *refs, w_up_ref, w_down_ref, loads = refs
    grad_up, grad_down, grad_qkv, grad_out, slots_ref, bias_ref, gain_acc = refs
    feats, rows, width = after_ref.shape
    features, keys, _ = slots_ref.shape
    hidden_all = w_up_ref.shape[1]
    cells = feats * rows
    head = width // HEADS
    step = pl.program_id(0)
    gain_row, gain_mlp = vector(vectors_ref, 2), vector(vectors_ref, 3)

    last = pl.num_programs(0) - 1
    fetches = [
        pltpu.make_async_copy(source, target, loads.at[at])
        for at, (source, target) in enumerate(((w_up_hbm, w_up_ref), (w_down_hbm, w_down_ref)))
    ]

    @pl.when(step == 0)
    def _():
        for fetch in fetches:
            fetch.start()
        read_slots(gathered, idx_ref, slots_ref, bias_ref, features)
        for ref in (grad_qkv, grad_out, grad_up, grad_down, gain_acc):
            ref[...] = jnp.zeros_like(ref)

    after = after_ref[...].reshape(cells, width)
    xhat2, scale2 = normalize(after)
    normed_two = (xhat2 * gain_row).astype(BF16)
    query = dot_nn(normed_two, w_row_ref[:, 0:width]).astype(BF16)
    slots = slots_ref[pl.ds(step * feats, feats)].reshape(feats * keys, width).astype(BF16)
    kv = dot_nn(slots, w_row_ref[:, width : 3 * width]).astype(BF16)
    keys_b = [head_blocks(kv[f * keys : (f + 1) * keys, 0:width]) for f in range(feats)]
    values_b = [head_blocks(kv[f * keys : (f + 1) * keys, width : 2 * width]) for f in range(feats)]
    query_f = [query[f * rows : (f + 1) * rows] for f in range(feats)]
    scores = jnp.stack([dot_nt(keys_b[f], query_f[f]) for f in range(feats)])
    scores = scores * (head**-0.5) + bias_ref[:, 0:rows][None]
    probs = softmax_keys(scores.reshape(feats * HEADS, keys, rows))
    probs_b = probs.reshape(feats, HEADS * keys, rows).astype(BF16)
    att = jnp.concatenate([dot_tn(probs_b[f], values_b[f]).astype(BF16) for f in range(feats)], axis=0)
    after_two = after + dot_nn(att, w_out_ref[...])

    @pl.when(step == 0)
    def _():
        for fetch in fetches:
            fetch.wait()

    xhat3, scale3 = normalize(after_two)
    normed_three = (xhat3 * gain_mlp).astype(BF16)
    upstream = upstream_ref[...].reshape(cells, width)
    piece = 256
    hidden, grad_inner = [], []
    first = lambda at: (dot_nn(normed_three, w_up_ref[:, at : at + piece]), dot_nt(upstream, w_down_ref[at : at + piece, :]))
    ahead = first(0)
    for at in range(0, hidden_all, piece):
        inner, back = ahead
        if at + piece < hidden_all:
            ahead = first(at + piece)
        part, slope = gelu_parts(inner)
        hidden.append(part)
        grad_inner.append(back.astype(BF16) * slope)
    hidden = jnp.concatenate(hidden, axis=1)
    grad_inner = jnp.concatenate(grad_inner, axis=1)
    total = after_two + dot_nn(hidden, w_down_ref[...])
    grad3 = dot_nt(grad_inner, w_up_ref[...])
    grad_down[...] += dot_tn(hidden, upstream)
    grad_up[...] += dot_tn(normed_three, grad_inner)
    output_ref[...] = total.astype(BF16).reshape(feats, rows, width)
    gain_acc[0] += column_sum(grad3 * xhat3)
    grad_two = upstream.astype(F32) + norm_back(xhat3, scale3, gain_mlp, grad3)

    if fast:
        wide, narrow = stages[0].shape[-1], stages[4].shape[-1]
        sends = []
        for at, stage in enumerate(stages):
            low, size = (0, wide) if at < 4 else (wide, narrow)
            lead = (slice(None),) * (len(stage.shape) - 1)
            sends.append(pltpu.make_async_copy(stage, outs[at % 4].at[(*lead, pl.ds(low, size))], copies.at[at]))

        @pl.when(step == last)
        def _():
            emit(idx_ref, stages[0:2], stages[2:4], [(grad_up, 0), (grad_down, hidden_all)])
            for send in sends[0:4]:
                send.start()

    branch = grad_two.astype(BF16)
    grad_out[...] += dot_tn(att, branch)
    grad_att = dot_nt(branch, w_out_ref[...]).astype(BF16)
    grad_f = [grad_att[f * rows : (f + 1) * rows] for f in range(feats)]
    grad_probs = jnp.stack([dot_nt(values_b[f], grad_f[f]) for f in range(feats)]).reshape(feats * HEADS, keys, rows)
    grad_scores = probs * (grad_probs - jnp.sum(grad_probs * probs, axis=1, keepdims=True))
    grad_scores = grad_scores.reshape(feats, HEADS * keys, rows).astype(BF16)
    grad_query = jnp.concatenate([dot_tn(grad_scores[f], keys_b[f]) for f in range(feats)], axis=0)
    grad_query = (grad_query * (head**-0.5)).astype(BF16)
    grad_keys = [own_heads(dot_nn(grad_scores[f], query_f[f]), keys) for f in range(feats)]
    grad_values = [own_heads(dot_nn(probs_b[f], grad_f[f]), keys) for f in range(feats)]
    grad_kv = jnp.concatenate(
        [jnp.concatenate(grad_keys, axis=0) * (head**-0.5), jnp.concatenate(grad_values, axis=0)], axis=1
    ).astype(BF16)
    grad_qkv[:, 0:width] += dot_tn(normed_two, grad_query)
    grad_qkv[:, width : 3 * width] += dot_tn(slots, grad_kv)
    slots_ref[pl.ds(step * feats, feats)] = dot_nt(grad_kv, w_row_ref[:, width : 3 * width]).reshape(feats, keys, width)
    grad_normed = dot_nt(grad_query, w_row_ref[:, 0:width])
    gain_acc[1] += column_sum(grad_normed * xhat2)
    grad_after_ref[...] = (grad_two + norm_back(xhat2, scale2, gain_row, grad_normed)).reshape(feats, rows, width)

    @pl.when(step == last)
    def _():
        if fast:
            emit(idx_ref, stages[4:6], stages[6:8], [(grad_qkv, 0), (grad_out, 3 * width)])
            for send in sends[4:8]:
                send.start()
        gains_ref[...] = gain_acc[...]
        block = CTX_DEV * features
        core, line = idx_ref[1] % 2, idx_ref[1] // 2
        for q in range(keys // (2 * CTX_DEV)):
            low = pl.multiple_of((line ^ q) * 2 * CTX_DEV, 2 * CTX_DEV) if fast else q * 2 * CTX_DEV
            both = jnp.swapaxes(slots_ref[:, pl.ds(low, 2 * CTX_DEV), :], 0, 1).reshape(2 * block, width)
            if fast:
                even, odd = both[0:block], both[block:]
                slot_outs[0][q] = jnp.where(core == 0, even, odd).astype(BF16)
                slot_outs[1][q] = jnp.where(core == 0, odd, even).astype(BF16)
            else:
                slot_outs[0][2 * q * block : 2 * (q + 1) * block, :] = both.astype(BF16)
        if fast:
            for send in sends:
                send.wait()


def feature_backward(grad_one, packed, probs_b, att, start, gain, w_qkv, w_out, group, grad_w_qkv, grad_w_out):
    cells, width = start.shape
    head = width // HEADS
    branch = grad_one.astype(BF16)
    grad_w_out[...] += dot_tn(att, branch)
    grad_att = dot_nt(branch, w_out).astype(BF16)
    queries, keys, values = (head_parts(packed, part, group, head) for part in range(3))
    grads = [
        grad_att[low : low + group, h * head : (h + 1) * head] for low in range(0, cells, group) for h in range(HEADS)
    ]
    probs = probs_b.astype(F32)
    grad_probs = jnp.stack([dot_nt(value, grad) for value, grad in zip(values, grads)])
    grad_scores = probs * (grad_probs - jnp.sum(grad_probs * probs, axis=1, keepdims=True))
    grad_scores = grad_scores.astype(BF16)
    grad_queries = join_parts([dot_tn(grad_scores[at], key) for at, key in enumerate(keys)]) * (head**-0.5)
    grad_keys = join_parts([dot_nn(grad_scores[at], query) for at, query in enumerate(queries)]) * (head**-0.5)
    grad_values = join_parts([dot_nn(probs_b[at], grad) for at, grad in enumerate(grads)])
    grad_qkv = jnp.concatenate([grad_queries.astype(BF16), grad_keys.astype(BF16), grad_values.astype(BF16)], axis=1)
    xhat, scale = normalize(start)
    normed = (xhat * gain).astype(BF16)
    piece = 256
    for at in range(0, 3 * width, piece):
        grad_w_qkv[:, at : at + piece] += dot_tn(normed, grad_qkv[:, at : at + piece])
    grad_normed = dot_nt(grad_qkv, w_qkv)
    grad_start = grad_one + norm_back(xhat, scale, gain, grad_normed)
    return column_sum(grad_normed * xhat), grad_start


def feature_backward_kernel(slots, waits, fast, *refs):
    (
        idx_ref, cells_ref, mask_ref, vectors_ref, w_qkv_ref, w_out_ref, grad_after_ref, qkv_ref, probs_ref, att_ref,
        after_ref, row_gains,
    ), refs = refs[:12], refs[12:]
    slot_refs, refs = refs[:slots], refs[slots + waits :]
    (grad_cells_ref, gains_ref), refs = refs[:2], refs[2:]
    if fast:
        outs, refs = refs[:4], refs[4:]
    grad_w_qkv, grad_w_out, gains, columns, extra_ref = refs
    rows, features, width = cells_ref.shape
    cells = rows * features
    block = CTX_DEV * features
    group = GROUP_ROWS * features
    step = pl.program_id(0)

    @pl.when(step == 0)
    def _():
        for ref in (grad_w_qkv, grad_w_out, gains):
            ref[...] = jnp.zeros_like(ref)
        total = slot_refs[0][...].astype(F32)
        for ref in slot_refs[1:]:
            total = total + ref[...].astype(F32)
        xhat, scale = normalize(after_ref[...])
        extra_ref[...] = norm_back(xhat, scale, vector(vectors_ref, 2), total)
        gains[2] = row_gains[1] + column_sum(total * xhat)
        gains[3] = row_gains[0]

    @pl.when(step > 0)
    def _():
        extra_ref[...] = jnp.zeros_like(extra_ref)

    grad_one = jnp.swapaxes(grad_after_ref[...], 0, 1).reshape(cells, width)
    grad_one = jnp.concatenate([grad_one[0:block] + extra_ref[...], grad_one[block:]], axis=0)
    start, absent = start_cells(cells_ref[...], mask_ref[...], step * rows, vector(vectors_ref, 0))
    add_gain, grad_start = feature_backward(
        grad_one, qkv_ref[...], probs_ref[...].reshape(cells // group * HEADS, group, group), att_ref[...],
        start, vector(vectors_ref, 1), w_qkv_ref[...], w_out_ref[...], group, grad_w_qkv, grad_w_out,
    )
    gains[0] += add_gain
    grad_start = grad_start.reshape(rows, features, width)
    grad_cells_ref[...] = jnp.where(absent, 0.0, grad_start)
    gains[1] += column_sum(jnp.where(absent, grad_start, 0.0).reshape(cells, width))

    @pl.when(step == pl.num_programs(0) - 1)
    def _():
        sums = jnp.concatenate([jnp.sum(gains[at], axis=0, keepdims=True) for at in range(4)], axis=0)
        gains_ref[...] = sums
        if fast:
            columns[...] = jnp.concatenate([sums, jnp.zeros((124, width), F32)], axis=0).T
            emit(idx_ref, outs[0:2], outs[2:4], [(grad_w_qkv, 0), (grad_w_out, 3 * width), (columns, 4 * width)])


def output_kernel(output_t_ref, output_ref):
    output_ref[...] = jnp.swapaxes(output_t_ref[...].astype(F32), 0, 1).astype(BF16)


def join_kernel(count, *refs):
    rows = refs[0].shape[0]
    for at in range(count):
        refs[-1][at * rows : (at + 1) * rows, :] = refs[at][...]


def sum_kernel(count, groups, *refs):
    ins, outs = refs[:count], refs[len(refs) - len(groups) :]
    for group, out in zip(groups, outs):
        for at, part in enumerate(group):
            total = ins[0][part].astype(F32)
            for ref in ins[1:]:
                total = total + ref[part].astype(F32)
            out[at] = total.astype(BF16)


def whole(array):
    zeros = (0,) * array.ndim
    return pl.BlockSpec(array.shape, lambda i: zeros, pipeline_mode=pl.Buffered(1))


def whole_out(shape):
    zeros = (0,) * len(shape)
    return pl.BlockSpec(shape, lambda i: zeros, pipeline_mode=pl.Buffered(1))


def tiles(shape, axis, offset=0):
    def index(i):
        return tuple(i + offset if d == axis else 0 for d in range(len(shape)))

    return pl.BlockSpec(shape, index)


WAITS = 1e14
SCALARS = pl.BlockSpec(memory_space=pltpu.SMEM)
UNTOUCHED = pl.BlockSpec(memory_space=pl.ANY)


def struct(shape, dtype):
    return jax.ShapeDtypeStruct(shape, dtype)


def in_hbm(array):
    return pltpu.with_memory_space_constraint(array, pltpu.HBM)


def call(kernel, name, grid, args, in_specs, outs, out_specs, scratch, flops, aliases=None, vmem=VMEM_LIMIT, pinned=True, ahead=(), free=(), fixed=()):
    small = 1 << 15
    large = lambda a: pinned and math.prod(a.shape) >= 1 << 18
    args = [
        pltpu.with_memory_space_constraint(a, pltpu.VMEM if i in ahead else pltpu.HBM) if large(a) else a
        for i, a in enumerate(args)
    ]
    outs = [
        pltpu.HBM(o.shape, o.dtype) if large(o) and i not in free else pltpu.VMEM(o.shape, o.dtype) if i in fixed else o
        for i, o in enumerate(outs)
    ]
    sizes = [math.prod(a.shape) * a.dtype.itemsize for a in [*args, *outs]]
    return pl.pallas_call(
        kernel,
        grid=(grid,),
        in_specs=in_specs,
        out_shape=outs,
        out_specs=out_specs,
        scratch_shapes=scratch,
        input_output_aliases=aliases or {},
        compiler_params=pltpu.CompilerParams(vmem_limit_bytes=vmem, dimension_semantics=("arbitrary",)),
        cost_estimate=pl.CostEstimate(flops=int(flops), bytes_accessed=int(sum(sizes)), transcendentals=0),
        name=name,
    )(*args)


def xor_pairs(size, bit):
    return [(i, i ^ bit) for i in range(size)]


def swap(array, axis, size, bit):
    return lax.ppermute(array, axis, xor_pairs(size, bit))


def add_all(terms):
    total = terms[0].astype(F32)
    for term in terms[1:]:
        total = total + term.astype(F32)
    return total.astype(BF16)


def exchange(parts, axis, size, unit):
    return [parts[0]] + [swap(parts[at], axis, size, at * unit) for at in range(1, len(parts))]


def sum_parts(parts, groups, name, after=(), flops=WAITS):
    outs = [struct((len(group), *parts[0].shape[1:]), BF16) for group in groups]
    return call(
        functools.partial(sum_kernel, len(parts), groups),
        name,
        1,
        [*parts, *after],
        [whole(a) for a in parts] + [UNTOUCHED] * len(after),
        outs,
        [whole_out(o.shape) for o in outs],
        [],
        flops,
        pinned=False,
    )


def place_kernel(tabs, moves, gains, *refs):
    idx_ref, ins = refs[0], refs[1 : 1 + tabs]
    outs = refs[len(refs) - len(moves) - gains :]
    if gains:
        outs, rows_out, columns = outs[: len(moves) - 1], outs[len(moves) - 1 : -1], outs[-1]
        outs = [*outs, columns]
    tab = idx_ref[0]
    for out, (count, column) in zip(outs, moves):
        width = out.shape[1]
        for u in range(tabs):
            rows = ins[u].shape[0]
            for at in range(count):
                low = pl.multiple_of(((tab ^ u) * count + at) * rows, 16)
                out[pl.ds(low, rows), :] = ins[u][:, column + at * width : column + (at + 1) * width].astype(F32)
    if gains:
        turned = columns[...].T
        for at, out in enumerate(rows_out):
            out[...] = turned[at : at + 1, 0 : out.shape[1]]


def place(idx, pieces, moves, outs, tabs, name, after, gains=0, scratch=()):
    return call(
        functools.partial(place_kernel, tabs, moves, gains),
        name,
        1,
        [idx, *pieces, *after],
        [SCALARS] + [whole(a) for a in pieces] + [UNTOUCHED] * len(after),
        outs,
        [whole_out(o.shape) for o in outs],
        list(scratch),
        WAITS,
        pinned=False,
    )


def per_device(
    tabs,
    blocks,
    cells,
    missing_mask,
    context_counts,
    missing_embedding,
    gain_feature,
    w_feature_qkv,
    w_feature_out,
    gain_row,
    w_row_qkv,
    w_row_out,
    gain_mlp,
    w_up,
    w_down,
    upstream,
):
    _, rows, features, width = cells.shape
    hidden = w_up.shape[1]
    keys = CTX_DEV * blocks
    cells, mask, upstream = cells[0], jnp.swapaxes(missing_mask[0], 0, 1), upstream[0]
    mask = in_hbm(mask)
    vectors = jnp.concatenate([missing_embedding, gain_feature, gain_row, gain_mlp]).astype(F32).reshape(-1, 128)
    all_cells = rows * features
    cost = all_cells * width * width
    fast = tabs == 4 and blocks == 8 and width == 16 * tabs * blocks and hidden % (16 * tabs * blocks) == 0
    tall = hidden // (16 * tabs * blocks)
    idx = jnp.stack([lax.axis_index("tab"), lax.axis_index("rows")]).astype(jnp.int32)

    block = CTX_DEV * features
    piece_rows = block + 16
    payload, after_ctx = call(
        context_kernel,
        "context_rows",
        1,
        [context_counts, cells, mask, vectors, w_feature_qkv, w_feature_out],
        [SCALARS, pl.BlockSpec((CTX_DEV, features, width), lambda i: (0, 0, 0))]
        + [whole(a) for a in (mask, vectors, w_feature_qkv, w_feature_out)],
        [struct((piece_rows, width), BF16), struct((block, width), F32)],
        [whole_out((piece_rows, width)), whole_out((block, width))],
        [],
        2 * block * width * 4 * width,
    )
    if fast:
        received = exchange([payload] * (blocks // 2), "rows", blocks, 2)


    tile = min(32, rows)
    steps = rows // tile
    groups = tile // GROUP_ROWS
    group = GROUP_ROWS * features
    after_one, upstream_t, qkv, probs, att = call(
        feature_kernel,
        "feature_forward",
        steps,
        [cells, mask, upstream, vectors, w_feature_qkv, w_feature_out],
        [tiles((tile, features, width), 0), whole(mask), tiles((tile, features, width), 0)]
        + [whole(a) for a in (vectors, w_feature_qkv, w_feature_out)],
        [
            struct((features, rows, width), F32),
            struct((features, rows, width), BF16),
            struct((all_cells, 3 * width), BF16),
            struct((rows // GROUP_ROWS, HEADS, group, group), BF16),
            struct((all_cells, width), BF16),
        ],
        [
            tiles((features, tile, width), 1),
            tiles((features, tile, width), 1),
            tiles((tile * features, 3 * width), 0),
            tiles((groups, HEADS, group, group), 0),
            tiles((tile * features, width), 0),
        ],
        [],
        2 * 5 * cost,
        ahead=(4, 5) if fast else (),
    )

    if fast:
        mine = call(
            functools.partial(join_kernel, len(received)),
            "join",
            1,
            received + [att],
            [whole(a) for a in received] + [UNTOUCHED],
            [struct((len(received) * piece_rows, width), BF16)],
            [whole_out((len(received) * piece_rows, width))],
            [],
            0,
        )[0]
        gathered = [mine, swap(mine, "rows", blocks, 1)]
    else:
        gathered = [lax.all_gather(payload, "rows", axis=0, tiled=True)]

    feats = 4
    cell_tile = (feats, rows, width)
    full = [struct(s, F32) for s in ((width, hidden), (hidden, width), (width, 3 * width), (width, width))]
    if fast:
        share = lambda w: [(blocks // 2, 16, w), (tabs - 1, blocks // 2, 16, w)] * 2
        shares = [struct(s, BF16) for s in share(hidden + (4 + tall) * width)]
        stages = [pltpu.VMEM(s, BF16) for w in (hidden + tall * width, 4 * width) for s in share(w)]
        stages += [pltpu.SemaphoreType.DMA((8,))]
    else:
        shares = full
    weights = [vectors, w_row_qkv, w_row_out, w_up, w_down]
    slot_outs = [struct((blocks // 2, block, width), BF16)] * 2 if fast else [struct((keys * features, width), BF16)]
    output_t, grad_after, row_gains, *row_shares = call(
        functools.partial(rows_kernel, len(gathered), fast),
        "rows_and_feed_forward",
        features // feats,
        [idx, after_one, upstream_t] + weights + gathered,
        [SCALARS] + [tiles(cell_tile, 0)] * 2 + [whole(a) for a in weights[:3]] + [UNTOUCHED] * 2 + [whole(a) for a in gathered],
        [
            struct((features, rows, width), BF16),
            struct((features, rows, width), F32),
            struct((2, 8, width), F32),
        ]
        + slot_outs
        + shares,
        [tiles(cell_tile, 0)] * 2
        + [whole_out((2, 8, width))]
        + [whole_out(s.shape) for s in slot_outs]
        + [UNTOUCHED if fast else whole_out(s.shape) for s in shares],
        [pltpu.VMEM(s.shape, F32) for s in (full if fast else [])]
        + [pltpu.VMEM(s, F32) for s in ((features, keys, width), (HEADS * keys, 128), (2, 8, width))]
        + [pltpu.VMEM(a.shape, BF16) for a in (w_up, w_down)]
        + [pltpu.SemaphoreType.DMA((2,))]
        + (stages if fast else []),
        2 * 34 * cost,
        vmem=(50 if fast else 62) * MIB,
        free=(6,) if fast else (),
        fixed=(6,) if fast else (),
        ahead=(4, 5) if fast else (),
    )
    slot_parts, row_shares = row_shares[: len(slot_outs)], row_shares[len(slot_outs) :]
    output = call(
        output_kernel,
        "output",
        steps,
        [output_t],
        [tiles((features, tile, width), 1)],
        [struct((rows, features, width), BF16)],
        [tiles((tile, features, width), 0)],
        [],
        0,
    )[0]
    if fast:
        keep, keep_rest, send, send_rest = row_shares
        got_rest = swap(send_rest, "rows", blocks, 1)
        parts = [add_all([keep_rest[u], got_rest[u]]) for u in range(tabs - 1)]
        got = swap(send, "rows", blocks, 1)
        row_parts = [keep, got] + [swap(parts[u - 1], "tab", tabs, u) for u in range(1, tabs)]
        slot_parts = [slot_parts[0], swap(slot_parts[1], "rows", blocks, 1)]
        slot_parts = sum_parts(slot_parts, [(q,) for q in range(blocks // 2)], "sum_core_slots", [parts[0], got])
        own_slots = exchange([part[0] for part in slot_parts], "rows", blocks, 2)
    else:
        own_slots = [lax.psum_scatter(slot_parts[0], "rows", scatter_dimension=0, tiled=True)]

    weights = [mask, vectors, w_feature_qkv, w_feature_out]
    sums = [struct((width, 3 * width), F32), struct((width, width), F32)]
    outs = [struct(s, BF16) for s in share(4 * width + 128)] if fast else sums
    waits = [output]
    rest = [after_ctx, row_gains, *own_slots]
    grad_cells, gains, *feature_shares = call(
        functools.partial(feature_backward_kernel, len(own_slots), len(waits), fast),
        "feature_backward",
        steps,
        [idx, cells] + weights + [grad_after, qkv, probs, att] + rest + waits,
        [SCALARS, tiles((tile, features, width), 0)]
        + [whole(a) for a in weights]
        + [
            tiles((features, tile, width), 1),
            tiles((tile * features, 3 * width), 0),
            tiles((groups, HEADS, group, group), 0),
            tiles((tile * features, width), 0),
        ]
        + [whole(a) for a in rest]
        + [UNTOUCHED] * len(waits),
        [struct((rows, features, width), F32), struct((4, width), F32)] + outs,
        [tiles((tile, features, width), 0), whole_out((4, width))] + [whole_out(o.shape) for o in outs],
        ([pltpu.VMEM(s.shape, F32) for s in sums] if fast else [])
        + [pltpu.VMEM(s, F32) for s in ((4, 8, width), (width, 128), (block, width))],
        0,
        vmem=40 * MIB,
        free=(3,) if fast else (),
        fixed=(3,) if fast else (),
        ahead=(4, 5) if fast else (),
    )

    if fast:
        shard = lambda height, columns: struct((height // blocks, columns), F32)
        keep, keep_rest, send, send_rest = feature_shares
        got_rest = swap(send_rest, "rows", blocks, 1)
        got = swap(send, "rows", blocks, 1)
        one = [(q,) for q in range(blocks // 2)]
        lines = sum_parts(row_parts, one, "sum_tab_rows", [in_hbm(grad_cells)])
        row_parts = exchange(lines, "rows", blocks, 2)
        parts = sum_parts([keep_rest, got_rest], [(u,) for u in range(tabs - 1)], "sum_core_features", [lines[0]], 0)
        parts = [keep, got] + [swap(parts[u - 1][0], "tab", tabs, u) for u in range(1, tabs)]
        lines = sum_parts(parts, one, "sum_tab_features")
        parts = exchange(lines, "rows", blocks, 2)
        (own_rows,) = sum_parts(row_parts, [(0,)], "sum_rows_rows", [lines[0]])
        row_pieces = exchange([own_rows[0]] * tabs, "tab", tabs, 1)
        (own,) = sum_parts(parts, [(0,)], "sum_rows_features", [own_rows])
        pieces = exchange([own[0]] * tabs, "tab", tabs, 1)
        wide = hidden + tall * width
        moves = [(1, 0), (tall, hidden), (1, wide), (1, wide + 3 * width)]
        outs = [shard(width, hidden), shard(hidden, width), shard(width, 3 * width), shard(width, width)]
        grad_up, grad_down, grad_row_qkv, grad_row_out = place(idx, row_pieces, moves, outs, tabs, "place_rows", [])
        moves = [(1, 0), (1, 3 * width), (1, 4 * width)]
        outs = [shard(width, 3 * width), shard(width, width)] + [struct((1, width // blocks), F32)] * 4
        grad_feature_qkv, grad_feature_out, *gains = place(
            idx, pieces, moves, outs, tabs, "place_features", [in_hbm(grad_up)], 4, [pltpu.VMEM((width // blocks, 128), F32)]
        )
        gains = [g.reshape(width // blocks) for g in gains]
    else:
        scatter = lambda a, axis: lax.psum_scatter(a, "rows", scatter_dimension=axis, tiled=True)
        gains = lax.psum(scatter(gains, 1), "tab")
        weights = lax.psum([scatter(w, 0) for w in [*row_shares, *feature_shares]], "tab")
        grad_up, grad_down, grad_row_qkv, grad_row_out, grad_feature_qkv, grad_feature_out = weights
    return (
        output[None],
        grad_cells[None],
        gains[1],
        gains[0],
        grad_feature_qkv,
        grad_feature_out,
        gains[2],
        grad_row_qkv,
        grad_row_out,
        gains[3],
        grad_up,
        grad_down,
    )


def solution(mesh):
    in_specs = (
        P("tab", "rows", None, None),
        P("tab", "rows", None),
        P("tab", "rows"),
        P(),
        P(),
        P(),
        P(),
        P(),
        P(),
        P(),
        P(),
        P(),
        P(),
        P("tab", "rows", None, None),
    )
    out_specs = (
        P("tab", "rows", None, None),
        P("tab", "rows", None, None),
        P("rows"),
        P("rows"),
        P("rows", None),
        P("rows", None),
        P("rows"),
        P("rows", None),
        P("rows", None),
        P("rows"),
        P("rows", None),
        P("rows", None),
    )
    return jax.shard_map(
        functools.partial(per_device, mesh.shape["tab"], mesh.shape["rows"]),
        mesh=mesh,
        in_specs=in_specs,
        out_specs=out_specs,
        check_vma=False,
    )
```

```python
import functools
import math

import jax
import jax.numpy as jnp
from jax import lax
from jax.experimental import pallas as pl
from jax.experimental.pallas import tpu as pltpu
from jax.sharding import PartitionSpec as P

HEADS = 4
CTX_DEV = 4
EPSILON = 1e-05
MASKED = -1e30
F32 = jnp.float32
BF16 = jnp.bfloat16
GROUP_ROWS = 8
MIB = 1024 * 1024
VMEM_LIMIT = 24 * MIB


def dot_nn(left, right):
    return lax.dot_general(left, right, (((1,), (0,)), ((), ())), preferred_element_type=F32)


def dot_nt(left, right):
    return lax.dot_general(left, right, (((1,), (1,)), ((), ())), preferred_element_type=F32)


def dot_tn(left, right):
    return lax.dot_general(left, right, (((0,), (0,)), ((), ())), preferred_element_type=F32)


def normalize(tensor):
    row_mean = jnp.mean(tensor, axis=-1, keepdims=True)
    centred = tensor - row_mean
    scale = lax.rsqrt(jnp.mean(centred * centred, axis=-1, keepdims=True) + EPSILON)
    return centred * scale, scale


def norm_back(xhat, scale, gain, gradient):
    scaled = gradient * gain
    first = jnp.mean(scaled, axis=-1, keepdims=True)
    second = jnp.mean(scaled * xhat, axis=-1, keepdims=True)
    return scale * (scaled - first - xhat * second)


def column_sum(tensor):
    rows, width = tensor.shape
    return jnp.sum(tensor.reshape(rows // 8, 8, width), axis=0)


def missing_column(mask, first, rows):
    features, lanes = mask.shape
    shape = (rows, features, lanes)
    pick = lax.broadcasted_iota(jnp.int32, shape, 2) == first + lax.broadcasted_iota(jnp.int32, shape, 0)
    spread = jnp.broadcast_to(mask.astype(F32)[None], shape)
    return jnp.sum(jnp.where(pick, spread, 0.0), axis=-1, keepdims=True)


def vector(ref, at):
    count = ref.shape[0] // 4
    return jnp.concatenate([ref[at * count + i : at * count + i + 1, :] for i in range(count)], axis=1)


def start_cells(cells, mask, first, missing):
    rows, features, width = cells.shape
    absent = missing_column(mask, first, rows) > 0.5
    return jnp.where(absent, missing.reshape(1, 1, width), cells.astype(F32)).reshape(rows * features, width), absent


def same_row_bias(size, features):
    shape = (size, size)
    left = lax.broadcasted_iota(jnp.int32, shape, 0) // features
    right = lax.broadcasted_iota(jnp.int32, shape, 1) // features
    return jnp.where(left == right, 0.0, MASKED)


def head_parts(packed, part, group, head):
    cells, width = packed.shape[0], packed.shape[1] // 3
    return [
        packed[low : low + group, part * width + h * head : part * width + (h + 1) * head]
        for low in range(0, cells, group)
        for h in range(HEADS)
    ]


def join_parts(parts):
    rows = [jnp.concatenate(parts[at : at + HEADS], axis=1) for at in range(0, len(parts), HEADS)]
    return jnp.concatenate(rows, axis=0)


def softmax_keys(scores):
    exp_terms = jnp.exp(scores - jnp.max(scores, axis=1, keepdims=True))
    return exp_terms * (1.0 / jnp.sum(exp_terms, axis=1, keepdims=True))


def dot_pieces(left, right, piece=256):
    return jnp.concatenate(
        [dot_nn(left, right[:, at : at + piece]).astype(BF16) for at in range(0, right.shape[1], piece)], axis=1
    )


def feature_forward(start, gain, w_qkv, w_out, features, group):
    cells, width = start.shape
    head = width // HEADS
    xhat, _ = normalize(start)
    qkv = dot_pieces((xhat * gain).astype(BF16), w_qkv)
    queries, keys, values = (head_parts(qkv, part, group, head) for part in range(3))
    scores = jnp.stack([dot_nt(key, query) for key, query in zip(keys, queries)])
    probs = softmax_keys(scores * (head**-0.5) + same_row_bias(group, features)[None]).astype(BF16)
    att = join_parts([dot_tn(probs[at], value).astype(BF16) for at, value in enumerate(values)])
    return start + dot_nn(att, w_out), qkv, probs, att


def context_kernel(count_ref, cells_ref, mask_ref, vectors_ref, w_qkv_ref, w_out_ref, send_ref, after_ref):
    rows, features, width = cells_ref.shape
    cells = rows * features
    start, _ = start_cells(cells_ref[...], mask_ref[...], 0, vector(vectors_ref, 0))
    after, _, _, _ = feature_forward(start, vector(vectors_ref, 1), w_qkv_ref[...], w_out_ref[...], features, cells)
    after_ref[...] = after
    xhat, _ = normalize(after)
    send_ref[0:cells, :] = (xhat * vector(vectors_ref, 2)).astype(BF16)
    count = count_ref[0, 0].astype(F32)
    send_ref[cells : cells + 16, :] = jnp.full((16, width), count, F32).astype(BF16)


def feature_kernel(
    cells_ref, mask_ref, upstream_ref, vectors_ref, w_qkv_ref, w_out_ref,
    after_ref, upstream_t_ref, qkv_ref, probs_ref, att_ref,
):
    rows, features, width = cells_ref.shape
    start, _ = start_cells(cells_ref[...], mask_ref[...], pl.program_id(0) * rows, vector(vectors_ref, 0))
    after, qkv, probs, att = feature_forward(
        start, vector(vectors_ref, 1), w_qkv_ref[...], w_out_ref[...], features, GROUP_ROWS * features
    )
    qkv_ref[...] = qkv
    probs_ref[...] = probs.reshape(probs_ref.shape)
    att_ref[...] = att
    after_ref[...] = jnp.swapaxes(after.reshape(rows, features, width), 0, 1)
    upstream_t_ref[...] = jnp.swapaxes(upstream_ref[...].astype(F32), 0, 1).astype(BF16)


def head_blocks(tensor):
    keys, width = tensor.shape
    tiled = jnp.concatenate([tensor] * HEADS, axis=0)
    row_head = lax.broadcasted_iota(jnp.int32, tiled.shape, 0) // keys
    lane_head = lax.broadcasted_iota(jnp.int32, tiled.shape, 1) // (width // HEADS)
    return jnp.where(row_head == lane_head, tiled, jnp.zeros_like(tiled))


def own_heads(tensor, keys):
    head = tensor.shape[1] // HEADS
    return jnp.concatenate([tensor[h * keys : (h + 1) * keys, h * head : (h + 1) * head] for h in range(HEADS)], axis=1)


def gelu_parts(inner):
    const = 0.7978845608028654
    cubic = const * 0.044715
    inner = inner.astype(BF16)
    square = inner * inner
    half = 0.5 + 0.5 * jnp.tanh(inner * (const + cubic * square))
    hidden = inner * half
    slope = half + (hidden - hidden * half) * (2.0 * const + (6.0 * cubic) * square)
    return hidden, slope


def read_slots(gathered, idx_ref, slots_ref, bias_ref, features):
    keys, width = slots_ref.shape[1], slots_ref.shape[2]
    blocks = keys // CTX_DEV
    block = CTX_DEV * features
    piece = block + 16
    slot = lax.broadcasted_iota(jnp.int32, (keys, 128), 0)
    counts = jnp.zeros((keys, 128), F32)
    core, line = idx_ref[1] % 2, idx_ref[1] // 2
    for pair in range(blocks // 2):
        if len(gathered) == 2:
            mine, other = (ref[pair * piece : (pair + 1) * piece, :].astype(F32) for ref in gathered)
            even, odd = jnp.where(core == 0, mine, other), jnp.where(core == 0, other, mine)
            at = line ^ pair
        else:
            even, odd = (gathered[0][(2 * pair + j) * piece : (2 * pair + j + 1) * piece, :].astype(F32) for j in range(2))
            at = pair
        both = jnp.concatenate([even[0:block], odd[0:block]], axis=0).reshape(2 * CTX_DEV, features, width)
        slots_ref[:, pl.ds(pl.multiple_of(at * 2 * CTX_DEV, 2 * CTX_DEV), 2 * CTX_DEV), :] = jnp.swapaxes(both, 0, 1)
        for j, part in enumerate((even, odd)):
            counts = jnp.where(slot // CTX_DEV == 2 * at + j, part[block : block + 1, 0:128], counts)
    bias = jnp.where((slot % CTX_DEV).astype(F32) < counts, 0.0, MASKED)
    bias_ref[...] = jnp.concatenate([bias] * HEADS, axis=0)


def emit(idx_ref, keep, send, sources):
    tab, block = idx_ref[0], idx_ref[1]
    core, line = block % 2, block // 2
    lines, rows, _ = keep[0].shape
    tabs = keep[1].shape[0] + 1
    for u in range(tabs):
        for q in range(lines):
            for refs, shard in ((keep, core), (send, 1 - core)):
                ref = refs[0].at[q] if u == 0 else refs[1].at[u - 1, q]
                for acc, column in sources:
                    height, width = acc.shape
                    part = height // (2 * lines * tabs)
                    low = (((line ^ q) * 2 + shard) * tabs + (tab ^ u)) * part
                    for at in range(part // rows):
                        low_at = pl.multiple_of(low + at * rows, rows)
                        ref[:, column + at * width : column + (at + 1) * width] = acc[pl.ds(low_at, rows), :].astype(BF16)


def rows_kernel(pieces, fast, *refs):
    (idx_ref, after_ref, upstream_ref, vectors_ref, w_row_ref, w_out_ref, w_up_hbm, w_down_hbm), refs = refs[:8], refs[8:]
    gathered, refs = refs[:pieces], refs[pieces:]
    (output_ref, grad_after_ref, gains_ref), refs = refs[:3], refs[3:]
    slot_outs, refs = (refs[:2], refs[2:]) if fast else (refs[:1], refs[1:])
    if fast:
        outs, refs = refs[:4], refs[4:]
        stages, copies, refs = refs[-9:-1], refs[-1], refs[:-9]
    *refs, w_up_ref, w_down_ref, loads = refs
    grad_up, grad_down, grad_qkv, grad_out, slots_ref, bias_ref, gain_acc = refs
    feats, rows, width = after_ref.shape
    features, keys, _ = slots_ref.shape
    hidden_all = w_up_ref.shape[1]
    cells = feats * rows
    head = width // HEADS
    step = pl.program_id(0)
    gain_row, gain_mlp = vector(vectors_ref, 2), vector(vectors_ref, 3)

    last = pl.num_programs(0) - 1
    fetches = [
        pltpu.make_async_copy(source, target, loads.at[at])
        for at, (source, target) in enumerate(((w_up_hbm, w_up_ref), (w_down_hbm, w_down_ref)))
    ]

    @pl.when(step == 0)
    def _():
        for fetch in fetches:
            fetch.start()
        read_slots(gathered, idx_ref, slots_ref, bias_ref, features)
        for ref in (grad_qkv, grad_out, grad_up, grad_down, gain_acc):
            ref[...] = jnp.zeros_like(ref)

    after = after_ref[...].reshape(cells, width)
    xhat2, scale2 = normalize(after)
    normed_two = (xhat2 * gain_row).astype(BF16)
    query = dot_nn(normed_two, w_row_ref[:, 0:width]).astype(BF16)
    slots = slots_ref[pl.ds(step * feats, feats)].reshape(feats * keys, width).astype(BF16)
    kv = dot_nn(slots, w_row_ref[:, width : 3 * width]).astype(BF16)
    keys_b = [head_blocks(kv[f * keys : (f + 1) * keys, 0:width]) for f in range(feats)]
    values_b = [head_blocks(kv[f * keys : (f + 1) * keys, width : 2 * width]) for f in range(feats)]
    query_f = [query[f * rows : (f + 1) * rows] for f in range(feats)]
    scores = jnp.stack([dot_nt(keys_b[f], query_f[f]) for f in range(feats)])
    scores = scores * (head**-0.5) + bias_ref[:, 0:rows][None]
    probs = softmax_keys(scores.reshape(feats * HEADS, keys, rows))
    probs_b = probs.reshape(feats, HEADS * keys, rows).astype(BF16)
    att = jnp.concatenate([dot_tn(probs_b[f], values_b[f]).astype(BF16) for f in range(feats)], axis=0)
    after_two = after + dot_nn(att, w_out_ref[...])

    @pl.when(step == 0)
    def _():
        for fetch in fetches:
            fetch.wait()

    xhat3, scale3 = normalize(after_two)
    normed_three = (xhat3 * gain_mlp).astype(BF16)
    upstream = upstream_ref[...].reshape(cells, width)
    piece = 256
    hidden, grad_inner = [], []
    first = lambda at: (dot_nn(normed_three, w_up_ref[:, at : at + piece]), dot_nt(upstream, w_down_ref[at : at + piece, :]))
    ahead = first(0)
    for at in range(0, hidden_all, piece):
        inner, back = ahead
        if at + piece < hidden_all:
            ahead = first(at + piece)
        part, slope = gelu_parts(inner)
        hidden.append(part)
        grad_inner.append(back.astype(BF16) * slope)
    hidden = jnp.concatenate(hidden, axis=1)
    grad_inner = jnp.concatenate(grad_inner, axis=1)
    total = after_two + dot_nn(hidden, w_down_ref[...])
    grad3 = dot_nt(grad_inner, w_up_ref[...])
    grad_down[...] += dot_tn(hidden, upstream)
    grad_up[...] += dot_tn(normed_three, grad_inner)
    output_ref[...] = total.astype(BF16).reshape(feats, rows, width)
    gain_acc[0] += column_sum(grad3 * xhat3)
    grad_two = upstream.astype(F32) + norm_back(xhat3, scale3, gain_mlp, grad3)

    if fast:
        wide, narrow = stages[0].shape[-1], stages[4].shape[-1]
        sends = []
        for at, stage in enumerate(stages):
            low, size = (0, wide) if at < 4 else (wide, narrow)
            lead = (slice(None),) * (len(stage.shape) - 1)
            sends.append(pltpu.make_async_copy(stage, outs[at % 4].at[(*lead, pl.ds(low, size))], copies.at[at]))

        @pl.when(step == last)
        def _():
            emit(idx_ref, stages[0:2], stages[2:4], [(grad_up, 0), (grad_down, hidden_all)])
            for send in sends[0:4]:
                send.start()

    branch = grad_two.astype(BF16)
    grad_out[...] += dot_tn(att, branch)
    grad_att = dot_nt(branch, w_out_ref[...]).astype(BF16)
    grad_f = [grad_att[f * rows : (f + 1) * rows] for f in range(feats)]
    grad_probs = jnp.stack([dot_nt(values_b[f], grad_f[f]) for f in range(feats)]).reshape(feats * HEADS, keys, rows)
    grad_scores = probs * (grad_probs - jnp.sum(grad_probs * probs, axis=1, keepdims=True))
    grad_scores = grad_scores.reshape(feats, HEADS * keys, rows).astype(BF16)
    grad_query = jnp.concatenate([dot_tn(grad_scores[f], keys_b[f]) for f in range(feats)], axis=0)
    grad_query = (grad_query * (head**-0.5)).astype(BF16)
    grad_keys = [own_heads(dot_nn(grad_scores[f], query_f[f]), keys) for f in range(feats)]
    grad_values = [own_heads(dot_nn(probs_b[f], grad_f[f]), keys) for f in range(feats)]
    grad_kv = jnp.concatenate(
        [jnp.concatenate(grad_keys, axis=0) * (head**-0.5), jnp.concatenate(grad_values, axis=0)], axis=1
    ).astype(BF16)
    grad_qkv[:, 0:width] += dot_tn(normed_two, grad_query)
    grad_qkv[:, width : 3 * width] += dot_tn(slots, grad_kv)
    slots_ref[pl.ds(step * feats, feats)] = dot_nt(grad_kv, w_row_ref[:, width : 3 * width]).reshape(feats, keys, width)
    grad_normed = dot_nt(grad_query, w_row_ref[:, 0:width])
    gain_acc[1] += column_sum(grad_normed * xhat2)
    grad_after_ref[...] = (grad_two + norm_back(xhat2, scale2, gain_row, grad_normed)).reshape(feats, rows, width)

    @pl.when(step == last)
    def _():
        if fast:
            emit(idx_ref, stages[4:6], stages[6:8], [(grad_qkv, 0), (grad_out, 3 * width)])
            for send in sends[4:8]:
                send.start()
        gains_ref[...] = gain_acc[...]
        block = CTX_DEV * features
        core, line = idx_ref[1] % 2, idx_ref[1] // 2
        for q in range(keys // (2 * CTX_DEV)):
            low = pl.multiple_of((line ^ q) * 2 * CTX_DEV, 2 * CTX_DEV) if fast else q * 2 * CTX_DEV
            both = jnp.swapaxes(slots_ref[:, pl.ds(low, 2 * CTX_DEV), :], 0, 1).reshape(2 * block, width)
            if fast:
                even, odd = both[0:block], both[block:]
                slot_outs[0][q] = jnp.where(core == 0, even, odd).astype(BF16)
                slot_outs[1][q] = jnp.where(core == 0, odd, even).astype(BF16)
            else:
                slot_outs[0][2 * q * block : 2 * (q + 1) * block, :] = both.astype(BF16)
        if fast:
            for send in sends:
                send.wait()


def feature_backward(grad_one, packed, probs_b, att, start, gain, w_qkv, w_out, group, grad_w_qkv, grad_w_out):
    cells, width = start.shape
    head = width // HEADS
    branch = grad_one.astype(BF16)
    grad_w_out[...] += dot_tn(att, branch)
    grad_att = dot_nt(branch, w_out).astype(BF16)
    queries, keys, values = (head_parts(packed, part, group, head) for part in range(3))
    grads = [
        grad_att[low : low + group, h * head : (h + 1) * head] for low in range(0, cells, group) for h in range(HEADS)
    ]
    probs = probs_b.astype(F32)
    grad_probs = jnp.stack([dot_nt(value, grad) for value, grad in zip(values, grads)])
    grad_scores = probs * (grad_probs - jnp.sum(grad_probs * probs, axis=1, keepdims=True))
    grad_scores = grad_scores.astype(BF16)
    grad_queries = join_parts([dot_tn(grad_scores[at], key) for at, key in enumerate(keys)]) * (head**-0.5)
    grad_keys = join_parts([dot_nn(grad_scores[at], query) for at, query in enumerate(queries)]) * (head**-0.5)
    grad_values = join_parts([dot_nn(probs_b[at], grad) for at, grad in enumerate(grads)])
    grad_qkv = jnp.concatenate([grad_queries.astype(BF16), grad_keys.astype(BF16), grad_values.astype(BF16)], axis=1)
    xhat, scale = normalize(start)
    normed = (xhat * gain).astype(BF16)
    piece = 256
    for at in range(0, 3 * width, piece):
        grad_w_qkv[:, at : at + piece] += dot_tn(normed, grad_qkv[:, at : at + piece])
    grad_normed = dot_nt(grad_qkv, w_qkv)
    grad_start = grad_one + norm_back(xhat, scale, gain, grad_normed)
    return column_sum(grad_normed * xhat), grad_start


def feature_backward_kernel(slots, waits, fast, *refs):
    (
        idx_ref, cells_ref, mask_ref, vectors_ref, w_qkv_ref, w_out_ref, grad_after_ref, qkv_ref, probs_ref, att_ref,
        after_ref, row_gains,
    ), refs = refs[:12], refs[12:]
    slot_refs, refs = refs[:slots], refs[slots + waits :]
    (grad_cells_ref, gains_ref), refs = refs[:2], refs[2:]
    if fast:
        outs, refs = refs[:4], refs[4:]
    grad_w_qkv, grad_w_out, gains, columns, extra_ref = refs
    rows, features, width = cells_ref.shape
    cells = rows * features
    block = CTX_DEV * features
    group = GROUP_ROWS * features
    step = pl.program_id(0)

    @pl.when(step == 0)
    def _():
        for ref in (grad_w_qkv, grad_w_out, gains):
            ref[...] = jnp.zeros_like(ref)
        total = slot_refs[0][...].astype(F32)
        for ref in slot_refs[1:]:
            total = total + ref[...].astype(F32)
        xhat, scale = normalize(after_ref[...])
        extra_ref[...] = norm_back(xhat, scale, vector(vectors_ref, 2), total)
        gains[2] = row_gains[1] + column_sum(total * xhat)
        gains[3] = row_gains[0]

    @pl.when(step > 0)
    def _():
        extra_ref[...] = jnp.zeros_like(extra_ref)

    grad_one = jnp.swapaxes(grad_after_ref[...], 0, 1).reshape(cells, width)
    grad_one = jnp.concatenate([grad_one[0:block] + extra_ref[...], grad_one[block:]], axis=0)
    start, absent = start_cells(cells_ref[...], mask_ref[...], step * rows, vector(vectors_ref, 0))
    add_gain, grad_start = feature_backward(
        grad_one, qkv_ref[...], probs_ref[...].reshape(cells // group * HEADS, group, group), att_ref[...],
        start, vector(vectors_ref, 1), w_qkv_ref[...], w_out_ref[...], group, grad_w_qkv, grad_w_out,
    )
    gains[0] += add_gain
    grad_start = grad_start.reshape(rows, features, width)
    grad_cells_ref[...] = jnp.where(absent, 0.0, grad_start)
    gains[1] += column_sum(jnp.where(absent, grad_start, 0.0).reshape(cells, width))

    @pl.when(step == pl.num_programs(0) - 1)
    def _():
        sums = jnp.concatenate([jnp.sum(gains[at], axis=0, keepdims=True) for at in range(4)], axis=0)
        gains_ref[...] = sums
        if fast:
            columns[...] = jnp.concatenate([sums, jnp.zeros((124, width), F32)], axis=0).T
            emit(idx_ref, outs[0:2], outs[2:4], [(grad_w_qkv, 0), (grad_w_out, 3 * width), (columns, 4 * width)])


def output_kernel(output_t_ref, output_ref):
    output_ref[...] = jnp.swapaxes(output_t_ref[...].astype(F32), 0, 1).astype(BF16)


def join_kernel(count, *refs):
    rows = refs[0].shape[0]
    for at in range(count):
        refs[-1][at * rows : (at + 1) * rows, :] = refs[at][...]


def sum_kernel(count, groups, *refs):
    ins, outs = refs[:count], refs[len(refs) - len(groups) :]
    for group, out in zip(groups, outs):
        for at, part in enumerate(group):
            total = ins[0][part].astype(F32)
            for ref in ins[1:]:
                total = total + ref[part].astype(F32)
            out[at] = total.astype(BF16)


def whole(array):
    zeros = (0,) * array.ndim
    return pl.BlockSpec(array.shape, lambda i: zeros, pipeline_mode=pl.Buffered(1))


def whole_out(shape):
    zeros = (0,) * len(shape)
    return pl.BlockSpec(shape, lambda i: zeros, pipeline_mode=pl.Buffered(1))


def tiles(shape, axis, offset=0):
    def index(i):
        return tuple(i + offset if d == axis else 0 for d in range(len(shape)))

    return pl.BlockSpec(shape, index)


WAITS = 1e14
SCALARS = pl.BlockSpec(memory_space=pltpu.SMEM)
UNTOUCHED = pl.BlockSpec(memory_space=pl.ANY)


def struct(shape, dtype):
    return jax.ShapeDtypeStruct(shape, dtype)


def in_hbm(array):
    return pltpu.with_memory_space_constraint(array, pltpu.HBM)


def call(kernel, name, grid, args, in_specs, outs, out_specs, scratch, flops, aliases=None, vmem=VMEM_LIMIT, pinned=True, ahead=(), free=(), fixed=()):
    small = 1 << 15
    large = lambda a: pinned and math.prod(a.shape) >= 1 << 18
    args = [
        pltpu.with_memory_space_constraint(a, pltpu.VMEM if i in ahead else pltpu.HBM) if large(a) else a
        for i, a in enumerate(args)
    ]
    outs = [
        pltpu.HBM(o.shape, o.dtype) if large(o) and i not in free else pltpu.VMEM(o.shape, o.dtype) if i in fixed else o
        for i, o in enumerate(outs)
    ]
    sizes = [math.prod(a.shape) * a.dtype.itemsize for a in [*args, *outs]]
    return pl.pallas_call(
        kernel,
        grid=(grid,),
        in_specs=in_specs,
        out_shape=outs,
        out_specs=out_specs,
        scratch_shapes=scratch,
        input_output_aliases=aliases or {},
        compiler_params=pltpu.CompilerParams(vmem_limit_bytes=vmem, dimension_semantics=("arbitrary",)),
        cost_estimate=pl.CostEstimate(flops=int(flops), bytes_accessed=int(sum(sizes)), transcendentals=0),
        name=name,
    )(*args)


def xor_pairs(size, bit):
    return [(i, i ^ bit) for i in range(size)]


def swap(array, axis, size, bit):
    return lax.ppermute(array, axis, xor_pairs(size, bit))


def add_all(terms):
    total = terms[0].astype(F32)
    for term in terms[1:]:
        total = total + term.astype(F32)
    return total.astype(BF16)


def exchange(parts, axis, size, unit):
    return [parts[0]] + [swap(parts[at], axis, size, at * unit) for at in range(1, len(parts))]


def sum_parts(parts, groups, name, after=(), flops=WAITS):
    outs = [struct((len(group), *parts[0].shape[1:]), BF16) for group in groups]
    return call(
        functools.partial(sum_kernel, len(parts), groups),
        name,
        1,
        [*parts, *after],
        [whole(a) for a in parts] + [UNTOUCHED] * len(after),
        outs,
        [whole_out(o.shape) for o in outs],
        [],
        flops,
        pinned=False,
    )


def place_kernel(tabs, moves, gains, *refs):
    idx_ref, ins = refs[0], refs[1 : 1 + tabs]
    outs = refs[len(refs) - len(moves) - gains :]
    if gains:
        outs, rows_out, columns = outs[: len(moves) - 1], outs[len(moves) - 1 : -1], outs[-1]
        outs = [*outs, columns]
    tab = idx_ref[0]
    for out, (count, column) in zip(outs, moves):
        width = out.shape[1]
        for u in range(tabs):
            rows = ins[u].shape[0]
            for at in range(count):
                low = pl.multiple_of(((tab ^ u) * count + at) * rows, 16)
                out[pl.ds(low, rows), :] = ins[u][:, column + at * width : column + (at + 1) * width].astype(F32)
    if gains:
        turned = columns[...].T
        for at, out in enumerate(rows_out):
            out[...] = turned[at : at + 1, 0 : out.shape[1]]


def place(idx, pieces, moves, outs, tabs, name, after, gains=0, scratch=()):
    return call(
        functools.partial(place_kernel, tabs, moves, gains),
        name,
        1,
        [idx, *pieces, *after],
        [SCALARS] + [whole(a) for a in pieces] + [UNTOUCHED] * len(after),
        outs,
        [whole_out(o.shape) for o in outs],
        list(scratch),
        WAITS,
        pinned=False,
    )


def per_device(
    tabs,
    blocks,
    cells,
    missing_mask,
    context_counts,
    missing_embedding,
    gain_feature,
    w_feature_qkv,
    w_feature_out,
    gain_row,
    w_row_qkv,
    w_row_out,
    gain_mlp,
    w_up,
    w_down,
    upstream,
):
    _, rows, features, width = cells.shape
    hidden = w_up.shape[1]
    keys = CTX_DEV * blocks
    cells, mask, upstream = cells[0], jnp.swapaxes(missing_mask[0], 0, 1), upstream[0]
    mask = in_hbm(mask)
    vectors = jnp.concatenate([missing_embedding, gain_feature, gain_row, gain_mlp]).astype(F32).reshape(-1, 128)
    all_cells = rows * features
    cost = all_cells * width * width
    fast = tabs == 4 and blocks == 8 and width == 16 * tabs * blocks and hidden % (16 * tabs * blocks) == 0
    tall = hidden // (16 * tabs * blocks)
    idx = jnp.stack([lax.axis_index("tab"), lax.axis_index("rows")]).astype(jnp.int32)

    block = CTX_DEV * features
    piece_rows = block + 16
    payload, after_ctx = call(
        context_kernel,
        "context_rows",
        1,
        [context_counts, cells, mask, vectors, w_feature_qkv, w_feature_out],
        [SCALARS, pl.BlockSpec((CTX_DEV, features, width), lambda i: (0, 0, 0))]
        + [whole(a) for a in (mask, vectors, w_feature_qkv, w_feature_out)],
        [struct((piece_rows, width), BF16), struct((block, width), F32)],
        [whole_out((piece_rows, width)), whole_out((block, width))],
        [],
        2 * block * width * 4 * width,
    )
    if fast:
        received = exchange([payload] * (blocks // 2), "rows", blocks, 2)


    tile = min(32, rows)
    steps = rows // tile
    groups = tile // GROUP_ROWS
    group = GROUP_ROWS * features
    after_one, upstream_t, qkv, probs, att = call(
        feature_kernel,
        "feature_forward",
        steps,
        [cells, mask, upstream, vectors, w_feature_qkv, w_feature_out],
        [tiles((tile, features, width), 0), whole(mask), tiles((tile, features, width), 0)]
        + [whole(a) for a in (vectors, w_feature_qkv, w_feature_out)],
        [
            struct((features, rows, width), F32),
            struct((features, rows, width), BF16),
            struct((all_cells, 3 * width), BF16),
            struct((rows // GROUP_ROWS, HEADS, group, group), BF16),
            struct((all_cells, width), BF16),
        ],
        [
            tiles((features, tile, width), 1),
            tiles((features, tile, width), 1),
            tiles((tile * features, 3 * width), 0),
            tiles((groups, HEADS, group, group), 0),
            tiles((tile * features, width), 0),
        ],
        [],
        2 * 5 * cost,
        ahead=(4, 5) if fast else (),
    )

    if fast:
        mine = call(
            functools.partial(join_kernel, len(received)),
            "join",
            1,
            received + [att],
            [whole(a) for a in received] + [UNTOUCHED],
            [struct((len(received) * piece_rows, width), BF16)],
            [whole_out((len(received) * piece_rows, width))],
            [],
            0,
        )[0]
        gathered = [mine, swap(mine, "rows", blocks, 1)]
    else:
        gathered = [lax.all_gather(payload, "rows", axis=0, tiled=True)]

    feats = 4
    cell_tile = (feats, rows, width)
    full = [struct(s, F32) for s in ((width, hidden), (hidden, width), (width, 3 * width), (width, width))]
    if fast:
        share = lambda w: [(blocks // 2, 16, w), (tabs - 1, blocks // 2, 16, w)] * 2
        shares = [struct(s, BF16) for s in share(hidden + (4 + tall) * width)]
        stages = [pltpu.VMEM(s, BF16) for w in (hidden + tall * width, 4 * width) for s in share(w)]
        stages += [pltpu.SemaphoreType.DMA((8,))]
    else:
        shares = full
    weights = [vectors, w_row_qkv, w_row_out, w_up, w_down]
    slot_outs = [struct((blocks // 2, block, width), BF16)] * 2 if fast else [struct((keys * features, width), BF16)]
    output_t, grad_after, row_gains, *row_shares = call(
        functools.partial(rows_kernel, len(gathered), fast),
        "rows_and_feed_forward",
        features // feats,
        [idx, after_one, upstream_t] + weights + gathered,
        [SCALARS] + [tiles(cell_tile, 0)] * 2 + [whole(a) for a in weights[:3]] + [UNTOUCHED] * 2 + [whole(a) for a in gathered],
        [
            struct((features, rows, width), BF16),
            struct((features, rows, width), F32),
            struct((2, 8, width), F32),
        ]
        + slot_outs
        + shares,
        [tiles(cell_tile, 0)] * 2
        + [whole_out((2, 8, width))]
        + [whole_out(s.shape) for s in slot_outs]
        + [UNTOUCHED if fast else whole_out(s.shape) for s in shares],
        [pltpu.VMEM(s.shape, F32) for s in (full if fast else [])]
        + [pltpu.VMEM(s, F32) for s in ((features, keys, width), (HEADS * keys, 128), (2, 8, width))]
        + [pltpu.VMEM(a.shape, BF16) for a in (w_up, w_down)]
        + [pltpu.SemaphoreType.DMA((2,))]
        + (stages if fast else []),
        2 * 34 * cost,
        vmem=(50 if fast else 62) * MIB,
        free=(6,) if fast else (),
        fixed=(6,) if fast else (),
        ahead=(4, 5) if fast else (),
    )
    slot_parts, row_shares = row_shares[: len(slot_outs)], row_shares[len(slot_outs) :]
    output = call(
        output_kernel,
        "output",
        steps,
        [output_t],
        [tiles((features, tile, width), 1)],
        [struct((rows, features, width), BF16)],
        [tiles((tile, features, width), 0)],
        [],
        0,
    )[0]
    if fast:
        keep, keep_rest, send, send_rest = row_shares
        got_rest = swap(send_rest, "rows", blocks, 1)
        parts = [add_all([keep_rest[u], got_rest[u]]) for u in range(tabs - 1)]
        got = swap(send, "rows", blocks, 1)
        row_parts = [keep, got] + [swap(parts[u - 1], "tab", tabs, u) for u in range(1, tabs)]
        slot_parts = [slot_parts[0], swap(slot_parts[1], "rows", blocks, 1)]
        slot_parts = sum_parts(slot_parts, [(q,) for q in range(blocks // 2)], "sum_core_slots", [parts[0], got])
        own_slots = exchange([part[0] for part in slot_parts], "rows", blocks, 2)
    else:
        own_slots = [lax.psum_scatter(slot_parts[0], "rows", scatter_dimension=0, tiled=True)]

    weights = [mask, vectors, w_feature_qkv, w_feature_out]
    sums = [struct((width, 3 * width), F32), struct((width, width), F32)]
    outs = [struct(s, BF16) for s in share(4 * width + 128)] if fast else sums
    waits = [output]
    rest = [after_ctx, row_gains, *own_slots]
    grad_cells, gains, *feature_shares = call(
        functools.partial(feature_backward_kernel, len(own_slots), len(waits), fast),
        "feature_backward",
        steps,
        [idx, cells] + weights + [grad_after, qkv, probs, att] + rest + waits,
        [SCALARS, tiles((tile, features, width), 0)]
        + [whole(a) for a in weights]
        + [
            tiles((features, tile, width), 1),
            tiles((tile * features, 3 * width), 0),
            tiles((groups, HEADS, group, group), 0),
            tiles((tile * features, width), 0),
        ]
        + [whole(a) for a in rest]
        + [UNTOUCHED] * len(waits),
        [struct((rows, features, width), F32), struct((4, width), F32)] + outs,
        [tiles((tile, features, width), 0), whole_out((4, width))] + [whole_out(o.shape) for o in outs],
        ([pltpu.VMEM(s.shape, F32) for s in sums] if fast else [])
        + [pltpu.VMEM(s, F32) for s in ((4, 8, width), (width, 128), (block, width))],
        0,
        vmem=40 * MIB,
        free=(3,) if fast else (),
        fixed=(3,) if fast else (),
        ahead=(4, 5) if fast else (),
    )

    if fast:
        shard = lambda height, columns: struct((height // blocks, columns), F32)
        keep, keep_rest, send, send_rest = feature_shares
        got_rest = swap(send_rest, "rows", blocks, 1)
        got = swap(send, "rows", blocks, 1)
        one = [(q,) for q in range(blocks // 2)]
        lines = sum_parts(row_parts, one, "sum_tab_rows", [in_hbm(grad_cells)])
        row_parts = exchange(lines, "rows", blocks, 2)
        parts = sum_parts([keep_rest, got_rest], [(u,) for u in range(tabs - 1)], "sum_core_features", [lines[0]], 0)
        parts = [keep, got] + [swap(parts[u - 1][0], "tab", tabs, u) for u in range(1, tabs)]
        lines = sum_parts(parts, one, "sum_tab_features")
        parts = exchange(lines, "rows", blocks, 2)
        (own_rows,) = sum_parts(row_parts, [(0,)], "sum_rows_rows", [lines[0]])
        row_pieces = exchange([own_rows[0]] * tabs, "tab", tabs, 1)
        own = add_all([part[0] for part in parts])
        pieces = exchange([own] * tabs, "tab", tabs, 1)
        wide = hidden + tall * width
        moves = [(1, 0), (tall, hidden), (1, wide), (1, wide + 3 * width)]
        outs = [shard(width, hidden), shard(hidden, width), shard(width, 3 * width), shard(width, width)]
        grad_up, grad_down, grad_row_qkv, grad_row_out = place(idx, row_pieces, moves, outs, tabs, "place_rows", [])
        moves = [(1, 0), (1, 3 * width), (1, 4 * width)]
        outs = [shard(width, 3 * width), shard(width, width)] + [struct((1, width // blocks), F32)] * 4
        grad_feature_qkv, grad_feature_out, *gains = place(
            idx, pieces, moves, outs, tabs, "place_features", [in_hbm(grad_up)], 4, [pltpu.VMEM((width // blocks, 128), F32)]
        )
        gains = [g.reshape(width // blocks) for g in gains]
    else:
        scatter = lambda a, axis: lax.psum_scatter(a, "rows", scatter_dimension=axis, tiled=True)
        gains = lax.psum(scatter(gains, 1), "tab")
        weights = lax.psum([scatter(w, 0) for w in [*row_shares, *feature_shares]], "tab")
        grad_up, grad_down, grad_row_qkv, grad_row_out, grad_feature_qkv, grad_feature_out = weights
    return (
        output[None],
        grad_cells[None],
        gains[1],
        gains[0],
        grad_feature_qkv,
        grad_feature_out,
        gains[2],
        grad_row_qkv,
        grad_row_out,
        gains[3],
        grad_up,
        grad_down,
    )


def solution(mesh):
    in_specs = (
        P("tab", "rows", None, None),
        P("tab", "rows", None),
        P("tab", "rows"),
        P(),
        P(),
        P(),
        P(),
        P(),
        P(),
        P(),
        P(),
        P(),
        P(),
        P("tab", "rows", None, None),
    )
    out_specs = (
        P("tab", "rows", None, None),
        P("tab", "rows", None, None),
        P("rows"),
        P("rows"),
        P("rows", None),
        P("rows", None),
        P("rows"),
        P("rows", None),
        P("rows", None),
        P("rows"),
        P("rows", None),
        P("rows", None),
    )
    return jax.shard_map(
        functools.partial(per_device, mesh.shape["tab"], mesh.shape["rows"]),
        mesh=mesh,
        in_specs=in_specs,
        out_specs=out_specs,
        check_vma=False,
    )
```

```python
import functools
import math

import jax
import jax.numpy as jnp
from jax import lax
from jax.experimental import pallas as pl
from jax.experimental.pallas import tpu as pltpu
from jax.sharding import PartitionSpec as P

HEADS = 4
CTX_DEV = 4
EPSILON = 1e-05
MASKED = -1e30
F32 = jnp.float32
BF16 = jnp.bfloat16
GROUP_ROWS = 8
MIB = 1024 * 1024
VMEM_LIMIT = 24 * MIB


def dot_nn(left, right):
    return lax.dot_general(left, right, (((1,), (0,)), ((), ())), preferred_element_type=F32)


def dot_nt(left, right):
    return lax.dot_general(left, right, (((1,), (1,)), ((), ())), preferred_element_type=F32)


def dot_tn(left, right):
    return lax.dot_general(left, right, (((0,), (0,)), ((), ())), preferred_element_type=F32)


def normalize(tensor):
    row_mean = jnp.mean(tensor, axis=-1, keepdims=True)
    centred = tensor - row_mean
    scale = lax.rsqrt(jnp.mean(centred * centred, axis=-1, keepdims=True) + EPSILON)
    return centred * scale, scale


def norm_back(xhat, scale, gain, gradient):
    scaled = gradient * gain
    first = jnp.mean(scaled, axis=-1, keepdims=True)
    second = jnp.mean(scaled * xhat, axis=-1, keepdims=True)
    return scale * (scaled - first - xhat * second)


def column_sum(tensor):
    rows, width = tensor.shape
    return jnp.sum(tensor.reshape(rows // 8, 8, width), axis=0)


def missing_column(mask, first, rows):
    features, lanes = mask.shape
    shape = (rows, features, lanes)
    pick = lax.broadcasted_iota(jnp.int32, shape, 2) == first + lax.broadcasted_iota(jnp.int32, shape, 0)
    spread = jnp.broadcast_to(mask.astype(F32)[None], shape)
    return jnp.sum(jnp.where(pick, spread, 0.0), axis=-1, keepdims=True)


def vector(refs, at):
    rows = refs[at][...].astype(F32)
    return jnp.concatenate([rows[i : i + 1, :] for i in range(rows.shape[0])], axis=1)


def start_cells(cells, mask, first, missing):
    rows, features, width = cells.shape
    absent = missing_column(mask, first, rows) > 0.5
    return jnp.where(absent, missing.reshape(1, 1, width), cells.astype(F32)).reshape(rows * features, width), absent


def same_row_bias(size, features):
    shape = (size, size)
    left = lax.broadcasted_iota(jnp.int32, shape, 0) // features
    right = lax.broadcasted_iota(jnp.int32, shape, 1) // features
    return jnp.where(left == right, 0.0, MASKED)


def head_parts(packed, part, group, head):
    cells, width = packed.shape[0], packed.shape[1] // 3
    return [
        packed[low : low + group, part * width + h * head : part * width + (h + 1) * head]
        for low in range(0, cells, group)
        for h in range(HEADS)
    ]


def join_parts(parts):
    rows = [jnp.concatenate(parts[at : at + HEADS], axis=1) for at in range(0, len(parts), HEADS)]
    return jnp.concatenate(rows, axis=0)


def softmax_keys(scores):
    exp_terms = jnp.exp(scores - jnp.max(scores, axis=1, keepdims=True))
    return exp_terms * (1.0 / jnp.sum(exp_terms, axis=1, keepdims=True))


def dot_pieces(left, right, piece=256):
    return jnp.concatenate(
        [dot_nn(left, right[:, at : at + piece]).astype(BF16) for at in range(0, right.shape[1], piece)], axis=1
    )


def feature_forward(start, gain, w_qkv, w_out, features, group):
    cells, width = start.shape
    head = width // HEADS
    xhat, _ = normalize(start)
    qkv = dot_pieces((xhat * gain).astype(BF16), w_qkv)
    queries, keys, values = (head_parts(qkv, part, group, head) for part in range(3))
    scores = jnp.stack([dot_nt(key, query) for key, query in zip(keys, queries)])
    probs = softmax_keys(scores * (head**-0.5) + same_row_bias(group, features)[None]).astype(BF16)
    att = join_parts([dot_tn(probs[at], value).astype(BF16) for at, value in enumerate(values)])
    return start + dot_nn(att, w_out), qkv, probs, att


def context_kernel(count_ref, cells_ref, mask_ref, *refs):
    vectors_ref, (w_qkv_ref, w_out_ref, send_ref, after_ref) = refs[:4], refs[4:]
    rows, features, width = cells_ref.shape
    cells = rows * features
    start, _ = start_cells(cells_ref[...], mask_ref[...], 0, vector(vectors_ref, 0))
    after, _, _, _ = feature_forward(start, vector(vectors_ref, 1), w_qkv_ref[...], w_out_ref[...], features, cells)
    after_ref[...] = after
    xhat, _ = normalize(after)
    send_ref[0:cells, :] = (xhat * vector(vectors_ref, 2)).astype(BF16)
    count = count_ref[0, 0].astype(F32)
    send_ref[cells : cells + 16, :] = jnp.full((16, width), count, F32).astype(BF16)


def feature_kernel(cells_ref, mask_ref, upstream_ref, *refs):
    vectors_ref, refs = refs[:4], refs[4:]
    w_qkv_ref, w_out_ref, after_ref, upstream_t_ref, qkv_ref, probs_ref, att_ref = refs
    rows, features, width = cells_ref.shape
    start, _ = start_cells(cells_ref[...], mask_ref[...], pl.program_id(0) * rows, vector(vectors_ref, 0))
    after, qkv, probs, att = feature_forward(
        start, vector(vectors_ref, 1), w_qkv_ref[...], w_out_ref[...], features, GROUP_ROWS * features
    )
    qkv_ref[...] = qkv
    probs_ref[...] = probs.reshape(probs_ref.shape)
    att_ref[...] = att
    after_ref[...] = jnp.swapaxes(after.reshape(rows, features, width), 0, 1)
    upstream_t_ref[...] = jnp.swapaxes(upstream_ref[...].astype(F32), 0, 1).astype(BF16)


def head_blocks(tensor):
    keys, width = tensor.shape
    tiled = jnp.concatenate([tensor] * HEADS, axis=0)
    row_head = lax.broadcasted_iota(jnp.int32, tiled.shape, 0) // keys
    lane_head = lax.broadcasted_iota(jnp.int32, tiled.shape, 1) // (width // HEADS)
    return jnp.where(row_head == lane_head, tiled, jnp.zeros_like(tiled))


def own_heads(tensor, keys):
    head = tensor.shape[1] // HEADS
    return jnp.concatenate([tensor[h * keys : (h + 1) * keys, h * head : (h + 1) * head] for h in range(HEADS)], axis=1)


def gelu_parts(inner):
    const = 0.7978845608028654
    cubic = const * 0.044715
    inner = inner.astype(BF16)
    square = inner * inner
    half = 0.5 + 0.5 * jnp.tanh(inner * (const + cubic * square))
    hidden = inner * half
    slope = half + (hidden - hidden * half) * (2.0 * const + (6.0 * cubic) * square)
    return hidden, slope


def read_slots(gathered, idx_ref, slots_ref, bias_ref, features):
    keys, width = slots_ref.shape[1], slots_ref.shape[2]
    blocks = keys // CTX_DEV
    block = CTX_DEV * features
    piece = block + 16
    slot = lax.broadcasted_iota(jnp.int32, (keys, 128), 0)
    counts = jnp.zeros((keys, 128), F32)
    core, line = idx_ref[1] % 2, idx_ref[1] // 2
    for pair in range(blocks // 2):
        if len(gathered) == 2:
            mine, other = (ref[pair * piece : (pair + 1) * piece, :].astype(F32) for ref in gathered)
            even, odd = jnp.where(core == 0, mine, other), jnp.where(core == 0, other, mine)
            at = line ^ pair
        else:
            even, odd = (gathered[0][(2 * pair + j) * piece : (2 * pair + j + 1) * piece, :].astype(F32) for j in range(2))
            at = pair
        both = jnp.concatenate([even[0:block], odd[0:block]], axis=0).reshape(2 * CTX_DEV, features, width)
        slots_ref[:, pl.ds(pl.multiple_of(at * 2 * CTX_DEV, 2 * CTX_DEV), 2 * CTX_DEV), :] = jnp.swapaxes(both, 0, 1)
        for j, part in enumerate((even, odd)):
            counts = jnp.where(slot // CTX_DEV == 2 * at + j, part[block : block + 1, 0:128], counts)
    bias = jnp.where((slot % CTX_DEV).astype(F32) < counts, 0.0, MASKED)
    bias_ref[...] = jnp.concatenate([bias] * HEADS, axis=0)


def emit(idx_ref, keep, send, sources):
    tab, block = idx_ref[0], idx_ref[1]
    core, line = block % 2, block // 2
    lines, rows, _ = keep[0].shape
    tabs = keep[1].shape[0] + 1
    for u in range(tabs):
        for q in range(lines):
            for refs, shard in ((keep, core), (send, 1 - core)):
                ref = refs[0].at[q] if u == 0 else refs[1].at[u - 1, q]
                for acc, column in sources:
                    height, width = acc.shape
                    part = height // (2 * lines * tabs)
                    low = (((line ^ q) * 2 + shard) * tabs + (tab ^ u)) * part
                    for at in range(part // rows):
                        low_at = pl.multiple_of(low + at * rows, rows)
                        ref[:, column + at * width : column + (at + 1) * width] = acc[pl.ds(low_at, rows), :].astype(BF16)


def rows_kernel(pieces, fast, *refs):
    (idx_ref, after_ref, upstream_ref), vectors_ref, refs = refs[:3], refs[3:7], refs[7:]
    (w_row_ref, w_out_ref, w_up_hbm, w_down_hbm), refs = refs[:4], refs[4:]
    gathered, refs = refs[:pieces], refs[pieces:]
    (output_ref, grad_after_ref, gains_ref), refs = refs[:3], refs[3:]
    slot_outs, refs = (refs[:2], refs[2:]) if fast else (refs[:1], refs[1:])
    if fast:
        outs, refs = refs[:4], refs[4:]
        stages, copies, refs = refs[-9:-1], refs[-1], refs[:-9]
    *refs, w_up_ref, w_down_ref, loads = refs
    grad_up, grad_down, grad_qkv, grad_out, slots_ref, bias_ref, gain_acc = refs
    feats, rows, width = after_ref.shape
    features, keys, _ = slots_ref.shape
    hidden_all = w_up_ref.shape[1]
    cells = feats * rows
    head = width // HEADS
    step = pl.program_id(0)
    gain_row, gain_mlp = vector(vectors_ref, 2), vector(vectors_ref, 3)

    last = pl.num_programs(0) - 1
    fetches = [
        pltpu.make_async_copy(source, target, loads.at[at])
        for at, (source, target) in enumerate(((w_up_hbm, w_up_ref), (w_down_hbm, w_down_ref)))
    ]

    @pl.when(step == 0)
    def _():
        for fetch in fetches:
            fetch.start()
        read_slots(gathered, idx_ref, slots_ref, bias_ref, features)
        for ref in (grad_qkv, grad_out, grad_up, grad_down, gain_acc):
            ref[...] = jnp.zeros_like(ref)

    after = after_ref[...].reshape(cells, width)
    xhat2, scale2 = normalize(after)
    normed_two = (xhat2 * gain_row).astype(BF16)
    query = dot_nn(normed_two, w_row_ref[:, 0:width]).astype(BF16)
    slots = slots_ref[pl.ds(step * feats, feats)].reshape(feats * keys, width).astype(BF16)
    kv = dot_nn(slots, w_row_ref[:, width : 3 * width]).astype(BF16)
    keys_b = [head_blocks(kv[f * keys : (f + 1) * keys, 0:width]) for f in range(feats)]
    values_b = [head_blocks(kv[f * keys : (f + 1) * keys, width : 2 * width]) for f in range(feats)]
    query_f = [query[f * rows : (f + 1) * rows] for f in range(feats)]
    scores = jnp.stack([dot_nt(keys_b[f], query_f[f]) for f in range(feats)])
    scores = scores * (head**-0.5) + bias_ref[:, 0:rows][None]
    probs = softmax_keys(scores.reshape(feats * HEADS, keys, rows))
    probs_b = probs.reshape(feats, HEADS * keys, rows).astype(BF16)
    att = jnp.concatenate([dot_tn(probs_b[f], values_b[f]).astype(BF16) for f in range(feats)], axis=0)
    after_two = after + dot_nn(att, w_out_ref[...])

    @pl.when(step == 0)
    def _():
        for fetch in fetches:
            fetch.wait()

    xhat3, scale3 = normalize(after_two)
    normed_three = (xhat3 * gain_mlp).astype(BF16)
    upstream = upstream_ref[...].reshape(cells, width)
    piece = 256
    hidden, grad_inner = [], []
    first = lambda at: (dot_nn(normed_three, w_up_ref[:, at : at + piece]), dot_nt(upstream, w_down_ref[at : at + piece, :]))
    ahead = first(0)
    for at in range(0, hidden_all, piece):
        inner, back = ahead
        if at + piece < hidden_all:
            ahead = first(at + piece)
        part, slope = gelu_parts(inner)
        hidden.append(part)
        grad_inner.append(back.astype(BF16) * slope)
    hidden = jnp.concatenate(hidden, axis=1)
    grad_inner = jnp.concatenate(grad_inner, axis=1)
    total = after_two + dot_nn(hidden, w_down_ref[...])
    grad3 = dot_nt(grad_inner, w_up_ref[...])
    grad_down[...] += dot_tn(hidden, upstream)
    grad_up[...] += dot_tn(normed_three, grad_inner)
    output_ref[...] = total.astype(BF16).reshape(feats, rows, width)
    gain_acc[0] += column_sum(grad3 * xhat3)
    grad_two = upstream.astype(F32) + norm_back(xhat3, scale3, gain_mlp, grad3)

    if fast:
        wide, narrow = stages[0].shape[-1], stages[4].shape[-1]
        sends = []
        for at, stage in enumerate(stages):
            low, size = (0, wide) if at < 4 else (wide, narrow)
            lead = (slice(None),) * (len(stage.shape) - 1)
            sends.append(pltpu.make_async_copy(stage, outs[at % 4].at[(*lead, pl.ds(low, size))], copies.at[at]))

        @pl.when(step == last)
        def _():
            emit(idx_ref, stages[0:2], stages[2:4], [(grad_up, 0), (grad_down, hidden_all)])
            for send in sends[0:4]:
                send.start()

    branch = grad_two.astype(BF16)
    grad_out[...] += dot_tn(att, branch)
    grad_att = dot_nt(branch, w_out_ref[...]).astype(BF16)
    grad_f = [grad_att[f * rows : (f + 1) * rows] for f in range(feats)]
    grad_probs = jnp.stack([dot_nt(values_b[f], grad_f[f]) for f in range(feats)]).reshape(feats * HEADS, keys, rows)
    grad_scores = probs * (grad_probs - jnp.sum(grad_probs * probs, axis=1, keepdims=True))
    grad_scores = grad_scores.reshape(feats, HEADS * keys, rows).astype(BF16)
    grad_query = jnp.concatenate([dot_tn(grad_scores[f], keys_b[f]) for f in range(feats)], axis=0)
    grad_query = (grad_query * (head**-0.5)).astype(BF16)
    grad_keys = [own_heads(dot_nn(grad_scores[f], query_f[f]), keys) for f in range(feats)]
    grad_values = [own_heads(dot_nn(probs_b[f], grad_f[f]), keys) for f in range(feats)]
    grad_kv = jnp.concatenate(
        [jnp.concatenate(grad_keys, axis=0) * (head**-0.5), jnp.concatenate(grad_values, axis=0)], axis=1
    ).astype(BF16)
    grad_qkv[:, 0:width] += dot_tn(normed_two, grad_query)
    grad_qkv[:, width : 3 * width] += dot_tn(slots, grad_kv)
    slots_ref[pl.ds(step * feats, feats)] = dot_nt(grad_kv, w_row_ref[:, width : 3 * width]).reshape(feats, keys, width)
    grad_normed = dot_nt(grad_query, w_row_ref[:, 0:width])
    gain_acc[1] += column_sum(grad_normed * xhat2)
    grad_after_ref[...] = (grad_two + norm_back(xhat2, scale2, gain_row, grad_normed)).reshape(feats, rows, width)

    @pl.when(step == last)
    def _():
        if fast:
            emit(idx_ref, stages[4:6], stages[6:8], [(grad_qkv, 0), (grad_out, 3 * width)])
            for send in sends[4:8]:
                send.start()
        gains_ref[...] = gain_acc[...]
        block = CTX_DEV * features
        core, line = idx_ref[1] % 2, idx_ref[1] // 2
        for q in range(keys // (2 * CTX_DEV)):
            low = pl.multiple_of((line ^ q) * 2 * CTX_DEV, 2 * CTX_DEV) if fast else q * 2 * CTX_DEV
            both = jnp.swapaxes(slots_ref[:, pl.ds(low, 2 * CTX_DEV), :], 0, 1).reshape(2 * block, width)
            if fast:
                even, odd = both[0:block], both[block:]
                slot_outs[0][q] = jnp.where(core == 0, even, odd).astype(BF16)
                slot_outs[1][q] = jnp.where(core == 0, odd, even).astype(BF16)
            else:
                slot_outs[0][2 * q * block : 2 * (q + 1) * block, :] = both.astype(BF16)
        if fast:
            for send in sends:
                send.wait()


def feature_backward(grad_one, packed, probs_b, att, start, gain, w_qkv, w_out, group, grad_w_qkv, grad_w_out):
    cells, width = start.shape
    head = width // HEADS
    branch = grad_one.astype(BF16)
    grad_w_out[...] += dot_tn(att, branch)
    grad_att = dot_nt(branch, w_out).astype(BF16)
    queries, keys, values = (head_parts(packed, part, group, head) for part in range(3))
    grads = [
        grad_att[low : low + group, h * head : (h + 1) * head] for low in range(0, cells, group) for h in range(HEADS)
    ]
    probs = probs_b.astype(F32)
    grad_probs = jnp.stack([dot_nt(value, grad) for value, grad in zip(values, grads)])
    grad_scores = probs * (grad_probs - jnp.sum(grad_probs * probs, axis=1, keepdims=True))
    grad_scores = grad_scores.astype(BF16)
    grad_queries = join_parts([dot_tn(grad_scores[at], key) for at, key in enumerate(keys)]) * (head**-0.5)
    grad_keys = join_parts([dot_nn(grad_scores[at], query) for at, query in enumerate(queries)]) * (head**-0.5)
    grad_values = join_parts([dot_nn(probs_b[at], grad) for at, grad in enumerate(grads)])
    grad_qkv = jnp.concatenate([grad_queries.astype(BF16), grad_keys.astype(BF16), grad_values.astype(BF16)], axis=1)
    xhat, scale = normalize(start)
    normed = (xhat * gain).astype(BF16)
    piece = 256
    for at in range(0, 3 * width, piece):
        grad_w_qkv[:, at : at + piece] += dot_tn(normed, grad_qkv[:, at : at + piece])
    grad_normed = dot_nt(grad_qkv, w_qkv)
    grad_start = grad_one + norm_back(xhat, scale, gain, grad_normed)
    return column_sum(grad_normed * xhat), grad_start


def feature_backward_kernel(slots, waits, fast, *refs):
    (idx_ref, cells_ref, mask_ref), vectors_ref, refs = refs[:3], refs[3:7], refs[7:]
    (
        w_qkv_ref, w_out_ref, grad_after_ref, qkv_ref, probs_ref, att_ref, after_ref, row_gains,
    ), refs = refs[:8], refs[8:]
    slot_refs, refs = refs[:slots], refs[slots + waits :]
    (grad_cells_ref, gains_ref), refs = refs[:2], refs[2:]
    if fast:
        outs, refs = refs[:4], refs[4:]
    grad_w_qkv, grad_w_out, gains, columns, extra_ref = refs
    rows, features, width = cells_ref.shape
    cells = rows * features
    block = CTX_DEV * features
    group = GROUP_ROWS * features
    step = pl.program_id(0)

    @pl.when(step == 0)
    def _():
        for ref in (grad_w_qkv, grad_w_out, gains):
            ref[...] = jnp.zeros_like(ref)
        total = slot_refs[0][...].astype(F32)
        for ref in slot_refs[1:]:
            total = total + ref[...].astype(F32)
        xhat, scale = normalize(after_ref[...])
        extra_ref[...] = norm_back(xhat, scale, vector(vectors_ref, 2), total)
        gains[2] = row_gains[1] + column_sum(total * xhat)
        gains[3] = row_gains[0]

    @pl.when(step > 0)
    def _():
        extra_ref[...] = jnp.zeros_like(extra_ref)

    grad_one = jnp.swapaxes(grad_after_ref[...], 0, 1).reshape(cells, width)
    grad_one = jnp.concatenate([grad_one[0:block] + extra_ref[...], grad_one[block:]], axis=0)
    start, absent = start_cells(cells_ref[...], mask_ref[...], step * rows, vector(vectors_ref, 0))
    add_gain, grad_start = feature_backward(
        grad_one, qkv_ref[...], probs_ref[...].reshape(cells // group * HEADS, group, group), att_ref[...],
        start, vector(vectors_ref, 1), w_qkv_ref[...], w_out_ref[...], group, grad_w_qkv, grad_w_out,
    )
    gains[0] += add_gain
    grad_start = grad_start.reshape(rows, features, width)
    grad_cells_ref[...] = jnp.where(absent, 0.0, grad_start)
    gains[1] += column_sum(jnp.where(absent, grad_start, 0.0).reshape(cells, width))

    @pl.when(step == pl.num_programs(0) - 1)
    def _():
        sums = jnp.concatenate([jnp.sum(gains[at], axis=0, keepdims=True) for at in range(4)], axis=0)
        gains_ref[...] = sums
        if fast:
            columns[...] = jnp.concatenate([sums, jnp.zeros((124, width), F32)], axis=0).T
            emit(idx_ref, outs[0:2], outs[2:4], [(grad_w_qkv, 0), (grad_w_out, 3 * width), (columns, 4 * width)])


def output_kernel(output_t_ref, output_ref):
    output_ref[...] = jnp.swapaxes(output_t_ref[...].astype(F32), 0, 1).astype(BF16)


def join_kernel(count, *refs):
    rows = refs[0].shape[0]
    for at in range(count):
        refs[-1][at * rows : (at + 1) * rows, :] = refs[at][...]


def sum_kernel(count, groups, *refs):
    ins, outs = refs[:count], refs[len(refs) - len(groups) :]
    for group, out in zip(groups, outs):
        for at, part in enumerate(group):
            total = ins[0][part].astype(F32)
            for ref in ins[1:]:
                total = total + ref[part].astype(F32)
            out[at] = total.astype(BF16)


def whole(array):
    zeros = (0,) * array.ndim
    return pl.BlockSpec(array.shape, lambda i: zeros, pipeline_mode=pl.Buffered(1))


def whole_out(shape):
    zeros = (0,) * len(shape)
    return pl.BlockSpec(shape, lambda i: zeros, pipeline_mode=pl.Buffered(1))


def tiles(shape, axis, offset=0):
    def index(i):
        return tuple(i + offset if d == axis else 0 for d in range(len(shape)))

    return pl.BlockSpec(shape, index)


WAITS = 1e14
SCALARS = pl.BlockSpec(memory_space=pltpu.SMEM)
UNTOUCHED = pl.BlockSpec(memory_space=pl.ANY)


def struct(shape, dtype):
    return jax.ShapeDtypeStruct(shape, dtype)


def in_hbm(array):
    return pltpu.with_memory_space_constraint(array, pltpu.HBM)


def call(kernel, name, grid, args, in_specs, outs, out_specs, scratch, flops, aliases=None, vmem=VMEM_LIMIT, pinned=True, ahead=(), free=(), fixed=()):
    small = 1 << 15
    large = lambda a: pinned and math.prod(a.shape) >= 1 << 18
    args = [
        pltpu.with_memory_space_constraint(a, pltpu.VMEM if i in ahead else pltpu.HBM) if large(a) else a
        for i, a in enumerate(args)
    ]
    outs = [
        pltpu.HBM(o.shape, o.dtype) if large(o) and i not in free else pltpu.VMEM(o.shape, o.dtype) if i in fixed else o
        for i, o in enumerate(outs)
    ]
    sizes = [math.prod(a.shape) * a.dtype.itemsize for a in [*args, *outs]]
    return pl.pallas_call(
        kernel,
        grid=(grid,),
        in_specs=in_specs,
        out_shape=outs,
        out_specs=out_specs,
        scratch_shapes=scratch,
        input_output_aliases=aliases or {},
        compiler_params=pltpu.CompilerParams(vmem_limit_bytes=vmem, dimension_semantics=("arbitrary",)),
        cost_estimate=pl.CostEstimate(flops=int(flops), bytes_accessed=int(sum(sizes)), transcendentals=0),
        name=name,
    )(*args)


def xor_pairs(size, bit):
    return [(i, i ^ bit) for i in range(size)]


def swap(array, axis, size, bit):
    return lax.ppermute(array, axis, xor_pairs(size, bit))


def add_all(terms):
    total = terms[0].astype(F32)
    for term in terms[1:]:
        total = total + term.astype(F32)
    return total.astype(BF16)


def exchange(parts, axis, size, unit):
    return [parts[0]] + [swap(parts[at], axis, size, at * unit) for at in range(1, len(parts))]


def sum_parts(parts, groups, name, after=(), flops=WAITS):
    outs = [struct((len(group), *parts[0].shape[1:]), BF16) for group in groups]
    return call(
        functools.partial(sum_kernel, len(parts), groups),
        name,
        1,
        [*parts, *after],
        [whole(a) for a in parts] + [UNTOUCHED] * len(after),
        outs,
        [whole_out(o.shape) for o in outs],
        [],
        flops,
        pinned=False,
    )


def place_kernel(tabs, moves, gains, *refs):
    idx_ref, ins = refs[0], refs[1 : 1 + tabs]
    outs = refs[len(refs) - len(moves) - gains :]
    if gains:
        outs, rows_out, columns = outs[: len(moves) - 1], outs[len(moves) - 1 : -1], outs[-1]
        outs = [*outs, columns]
    tab = idx_ref[0]
    for out, (count, column) in zip(outs, moves):
        width = out.shape[1]
        for u in range(tabs):
            rows = ins[u].shape[0]
            for at in range(count):
                low = pl.multiple_of(((tab ^ u) * count + at) * rows, 16)
                out[pl.ds(low, rows), :] = ins[u][:, column + at * width : column + (at + 1) * width].astype(F32)
    if gains:
        turned = columns[...].T
        for at, out in enumerate(rows_out):
            out[...] = turned[at : at + 1, 0 : out.shape[1]]


def place(idx, pieces, moves, outs, tabs, name, after, gains=0, scratch=()):
    return call(
        functools.partial(place_kernel, tabs, moves, gains),
        name,
        1,
        [idx, *pieces, *after],
        [SCALARS] + [whole(a) for a in pieces] + [UNTOUCHED] * len(after),
        outs,
        [whole_out(o.shape) for o in outs],
        list(scratch),
        WAITS,
        pinned=False,
    )


def per_device(
    tabs,
    blocks,
    cells,
    missing_mask,
    context_counts,
    missing_embedding,
    gain_feature,
    w_feature_qkv,
    w_feature_out,
    gain_row,
    w_row_qkv,
    w_row_out,
    gain_mlp,
    w_up,
    w_down,
    upstream,
):
    _, rows, features, width = cells.shape
    hidden = w_up.shape[1]
    keys = CTX_DEV * blocks
    cells, mask, upstream = cells[0], jnp.swapaxes(missing_mask[0], 0, 1), upstream[0]
    mask = in_hbm(mask)
    vectors = [in_hbm(v.reshape(-1, 128)) for v in (missing_embedding, gain_feature, gain_row, gain_mlp)]
    all_cells = rows * features
    cost = all_cells * width * width
    fast = tabs == 4 and blocks == 8 and width == 16 * tabs * blocks and hidden % (16 * tabs * blocks) == 0
    tall = hidden // (16 * tabs * blocks)
    idx = jnp.stack([lax.axis_index("tab"), lax.axis_index("rows")]).astype(jnp.int32)

    block = CTX_DEV * features
    piece_rows = block + 16
    payload, after_ctx = call(
        context_kernel,
        "context_rows",
        1,
        [context_counts, cells, mask, *vectors, w_feature_qkv, w_feature_out],
        [SCALARS, pl.BlockSpec((CTX_DEV, features, width), lambda i: (0, 0, 0))]
        + [whole(a) for a in (mask, *vectors, w_feature_qkv, w_feature_out)],
        [struct((piece_rows, width), BF16), struct((block, width), F32)],
        [whole_out((piece_rows, width)), whole_out((block, width))],
        [],
        2 * block * width * 4 * width,
    )
    if fast:
        received = exchange([payload] * (blocks // 2), "rows", blocks, 2)


    tile = min(32, rows)
    steps = rows // tile
    groups = tile // GROUP_ROWS
    group = GROUP_ROWS * features
    after_one, upstream_t, qkv, probs, att = call(
        feature_kernel,
        "feature_forward",
        steps,
        [cells, mask, upstream, *vectors, w_feature_qkv, w_feature_out],
        [tiles((tile, features, width), 0), whole(mask), tiles((tile, features, width), 0)]
        + [whole(a) for a in (*vectors, w_feature_qkv, w_feature_out)],
        [
            struct((features, rows, width), F32),
            struct((features, rows, width), BF16),
            struct((all_cells, 3 * width), BF16),
            struct((rows // GROUP_ROWS, HEADS, group, group), BF16),
            struct((all_cells, width), BF16),
        ],
        [
            tiles((features, tile, width), 1),
            tiles((features, tile, width), 1),
            tiles((tile * features, 3 * width), 0),
            tiles((groups, HEADS, group, group), 0),
            tiles((tile * features, width), 0),
        ],
        [],
        2 * 5 * cost,
        ahead=(7, 8) if fast else (),
    )

    if fast:
        mine = call(
            functools.partial(join_kernel, len(received)),
            "join",
            1,
            received + [att],
            [whole(a) for a in received] + [UNTOUCHED],
            [struct((len(received) * piece_rows, width), BF16)],
            [whole_out((len(received) * piece_rows, width))],
            [],
            0,
        )[0]
        gathered = [mine, swap(mine, "rows", blocks, 1)]
    else:
        gathered = [lax.all_gather(payload, "rows", axis=0, tiled=True)]

    feats = 4
    cell_tile = (feats, rows, width)
    full = [struct(s, F32) for s in ((width, hidden), (hidden, width), (width, 3 * width), (width, width))]
    if fast:
        share = lambda w: [(blocks // 2, 16, w), (tabs - 1, blocks // 2, 16, w)] * 2
        shares = [struct(s, BF16) for s in share(hidden + (4 + tall) * width)]
        stages = [pltpu.VMEM(s, BF16) for w in (hidden + tall * width, 4 * width) for s in share(w)]
        stages += [pltpu.SemaphoreType.DMA((8,))]
    else:
        shares = full
    weights = [*vectors, w_row_qkv, w_row_out, w_up, w_down]
    slot_outs = [struct((blocks // 2, block, width), BF16)] * 2 if fast else [struct((keys * features, width), BF16)]
    output_t, grad_after, row_gains, *row_shares = call(
        functools.partial(rows_kernel, len(gathered), fast),
        "rows_and_feed_forward",
        features // feats,
        [idx, after_one, upstream_t] + weights + gathered,
        [SCALARS] + [tiles(cell_tile, 0)] * 2 + [whole(a) for a in weights[:6]] + [UNTOUCHED] * 2 + [whole(a) for a in gathered],
        [
            struct((features, rows, width), BF16),
            struct((features, rows, width), F32),
            struct((2, 8, width), F32),
        ]
        + slot_outs
        + shares,
        [tiles(cell_tile, 0)] * 2
        + [whole_out((2, 8, width))]
        + [whole_out(s.shape) for s in slot_outs]
        + [UNTOUCHED if fast else whole_out(s.shape) for s in shares],
        [pltpu.VMEM(s.shape, F32) for s in (full if fast else [])]
        + [pltpu.VMEM(s, F32) for s in ((features, keys, width), (HEADS * keys, 128), (2, 8, width))]
        + [pltpu.VMEM(a.shape, BF16) for a in (w_up, w_down)]
        + [pltpu.SemaphoreType.DMA((2,))]
        + (stages if fast else []),
        2 * 34 * cost,
        vmem=(50 if fast else 62) * MIB,
        free=(6,) if fast else (),
        fixed=(6,) if fast else (),
        ahead=(7, 8) if fast else (),
    )
    slot_parts, row_shares = row_shares[: len(slot_outs)], row_shares[len(slot_outs) :]
    output = call(
        output_kernel,
        "output",
        steps,
        [output_t],
        [tiles((features, tile, width), 1)],
        [struct((rows, features, width), BF16)],
        [tiles((tile, features, width), 0)],
        [],
        0,
    )[0]
    if fast:
        keep, keep_rest, send, send_rest = row_shares
        got_rest = swap(send_rest, "rows", blocks, 1)
        parts = [add_all([keep_rest[u], got_rest[u]]) for u in range(tabs - 1)]
        got = swap(send, "rows", blocks, 1)
        row_parts = [keep, got] + [swap(parts[u - 1], "tab", tabs, u) for u in range(1, tabs)]
        slot_parts = [slot_parts[0], swap(slot_parts[1], "rows", blocks, 1)]
        slot_parts = sum_parts(slot_parts, [(q,) for q in range(blocks // 2)], "sum_core_slots", [parts[0], got])
        own_slots = exchange([part[0] for part in slot_parts], "rows", blocks, 2)
    else:
        own_slots = [lax.psum_scatter(slot_parts[0], "rows", scatter_dimension=0, tiled=True)]

    weights = [mask, *vectors, w_feature_qkv, w_feature_out]
    sums = [struct((width, 3 * width), F32), struct((width, width), F32)]
    outs = [struct(s, BF16) for s in share(4 * width + 128)] if fast else sums
    waits = [output]
    rest = [after_ctx, row_gains, *own_slots]
    grad_cells, gains, *feature_shares = call(
        functools.partial(feature_backward_kernel, len(own_slots), len(waits), fast),
        "feature_backward",
        steps,
        [idx, cells] + weights + [grad_after, qkv, probs, att] + rest + waits,
        [SCALARS, tiles((tile, features, width), 0)]
        + [whole(a) for a in weights]
        + [
            tiles((features, tile, width), 1),
            tiles((tile * features, 3 * width), 0),
            tiles((groups, HEADS, group, group), 0),
            tiles((tile * features, width), 0),
        ]
        + [whole(a) for a in rest]
        + [UNTOUCHED] * len(waits),
        [struct((rows, features, width), F32), struct((4, width), F32)] + outs,
        [tiles((tile, features, width), 0), whole_out((4, width))] + [whole_out(o.shape) for o in outs],
        ([pltpu.VMEM(s.shape, F32) for s in sums] if fast else [])
        + [pltpu.VMEM(s, F32) for s in ((4, 8, width), (width, 128), (block, width))],
        0,
        vmem=40 * MIB,
        free=(3,) if fast else (),
        fixed=(3,) if fast else (),
        ahead=(7, 8) if fast else (),
    )

    if fast:
        shard = lambda height, columns: struct((height // blocks, columns), F32)
        keep, keep_rest, send, send_rest = feature_shares
        got_rest = swap(send_rest, "rows", blocks, 1)
        got = swap(send, "rows", blocks, 1)
        one = [(q,) for q in range(blocks // 2)]
        lines = sum_parts(row_parts, one, "sum_tab_rows", [in_hbm(grad_cells)])
        row_parts = exchange(lines, "rows", blocks, 2)
        parts = sum_parts([keep_rest, got_rest], [(u,) for u in range(tabs - 1)], "sum_core_features", [lines[0]], 0)
        parts = [keep, got] + [swap(parts[u - 1][0], "tab", tabs, u) for u in range(1, tabs)]
        lines = sum_parts(parts, one, "sum_tab_features")
        parts = exchange(lines, "rows", blocks, 2)
        (own_rows,) = sum_parts(row_parts, [(0,)], "sum_rows_rows", [lines[0]])
        row_pieces = exchange([own_rows[0]] * tabs, "tab", tabs, 1)
        own = add_all([part[0] for part in parts])
        pieces = exchange([own] * tabs, "tab", tabs, 1)
        wide = hidden + tall * width
        moves = [(1, 0), (tall, hidden), (1, wide), (1, wide + 3 * width)]
        outs = [shard(width, hidden), shard(hidden, width), shard(width, 3 * width), shard(width, width)]
        grad_up, grad_down, grad_row_qkv, grad_row_out = place(idx, row_pieces, moves, outs, tabs, "place_rows", [])
        moves = [(1, 0), (1, 3 * width), (1, 4 * width)]
        outs = [shard(width, 3 * width), shard(width, width)] + [struct((1, width // blocks), F32)] * 4
        grad_feature_qkv, grad_feature_out, *gains = place(
            idx, pieces, moves, outs, tabs, "place_features", [in_hbm(grad_up)], 4, [pltpu.VMEM((width // blocks, 128), F32)]
        )
        gains = [g.reshape(width // blocks) for g in gains]
    else:
        scatter = lambda a, axis: lax.psum_scatter(a, "rows", scatter_dimension=axis, tiled=True)
        gains = lax.psum(scatter(gains, 1), "tab")
        weights = lax.psum([scatter(w, 0) for w in [*row_shares, *feature_shares]], "tab")
        grad_up, grad_down, grad_row_qkv, grad_row_out, grad_feature_qkv, grad_feature_out = weights
    return (
        output[None],
        grad_cells[None],
        gains[1],
        gains[0],
        grad_feature_qkv,
        grad_feature_out,
        gains[2],
        grad_row_qkv,
        grad_row_out,
        gains[3],
        grad_up,
        grad_down,
    )


def solution(mesh):
    in_specs = (
        P("tab", "rows", None, None),
        P("tab", "rows", None),
        P("tab", "rows"),
        P(),
        P(),
        P(),
        P(),
        P(),
        P(),
        P(),
        P(),
        P(),
        P(),
        P("tab", "rows", None, None),
    )
    out_specs = (
        P("tab", "rows", None, None),
        P("tab", "rows", None, None),
        P("rows"),
        P("rows"),
        P("rows", None),
        P("rows", None),
        P("rows"),
        P("rows", None),
        P("rows", None),
        P("rows"),
        P("rows", None),
        P("rows", None),
    )
    return jax.shard_map(
        functools.partial(per_device, mesh.shape["tab"], mesh.shape["rows"]),
        mesh=mesh,
        in_specs=in_specs,
        out_specs=out_specs,
        check_vma=False,
    )
```

```python
import functools
import math

import jax
import jax.numpy as jnp
from jax import lax
from jax.experimental import pallas as pl
from jax.experimental.pallas import tpu as pltpu
from jax.sharding import PartitionSpec as P

HEADS = 4
CTX_DEV = 4
EPSILON = 1e-05
MASKED = -1e30
F32 = jnp.float32
BF16 = jnp.bfloat16
GROUP_ROWS = 8
MIB = 1024 * 1024
VMEM_LIMIT = 24 * MIB


def dot_nn(left, right):
    return lax.dot_general(left, right, (((1,), (0,)), ((), ())), preferred_element_type=F32)


def dot_nt(left, right):
    return lax.dot_general(left, right, (((1,), (1,)), ((), ())), preferred_element_type=F32)


def dot_tn(left, right):
    return lax.dot_general(left, right, (((0,), (0,)), ((), ())), preferred_element_type=F32)


def normalize(tensor):
    row_mean = jnp.mean(tensor, axis=-1, keepdims=True)
    centred = tensor - row_mean
    scale = lax.rsqrt(jnp.mean(centred * centred, axis=-1, keepdims=True) + EPSILON)
    return centred * scale, scale


def norm_back(xhat, scale, gain, gradient):
    scaled = gradient * gain
    first = jnp.mean(scaled, axis=-1, keepdims=True)
    second = jnp.mean(scaled * xhat, axis=-1, keepdims=True)
    return scale * (scaled - first - xhat * second)


def column_sum(tensor):
    rows, width = tensor.shape
    return jnp.sum(tensor.reshape(rows // 8, 8, width), axis=0)


def missing_column(mask, first, rows):
    features, lanes = mask.shape
    shape = (rows, features, lanes)
    pick = lax.broadcasted_iota(jnp.int32, shape, 2) == first + lax.broadcasted_iota(jnp.int32, shape, 0)
    spread = jnp.broadcast_to(mask.astype(F32)[None], shape)
    return jnp.sum(jnp.where(pick, spread, 0.0), axis=-1, keepdims=True)


def vector(refs, at):
    rows = refs[at][...].astype(F32)
    return jnp.concatenate([rows[i : i + 1, :] for i in range(rows.shape[0])], axis=1)


def start_cells(cells, mask, first, missing):
    rows, features, width = cells.shape
    absent = missing_column(mask, first, rows) > 0.5
    return jnp.where(absent, missing.reshape(1, 1, width), cells.astype(F32)).reshape(rows * features, width), absent


def same_row_bias(size, features):
    shape = (size, size)
    left = lax.broadcasted_iota(jnp.int32, shape, 0) // features
    right = lax.broadcasted_iota(jnp.int32, shape, 1) // features
    return jnp.where(left == right, 0.0, MASKED)


def head_parts(packed, part, group, head):
    cells, width = packed.shape[0], packed.shape[1] // 3
    return [
        packed[low : low + group, part * width + h * head : part * width + (h + 1) * head]
        for low in range(0, cells, group)
        for h in range(HEADS)
    ]


def join_parts(parts):
    rows = [jnp.concatenate(parts[at : at + HEADS], axis=1) for at in range(0, len(parts), HEADS)]
    return jnp.concatenate(rows, axis=0)


def softmax_keys(scores):
    exp_terms = jnp.exp(scores - jnp.max(scores, axis=1, keepdims=True))
    return exp_terms * (1.0 / jnp.sum(exp_terms, axis=1, keepdims=True))


def dot_pieces(left, right, piece=256):
    return jnp.concatenate(
        [dot_nn(left, right[:, at : at + piece]).astype(BF16) for at in range(0, right.shape[1], piece)], axis=1
    )


def feature_forward(start, gain, w_qkv, w_out, features, group):
    cells, width = start.shape
    head = width // HEADS
    xhat, _ = normalize(start)
    qkv = dot_pieces((xhat * gain).astype(BF16), w_qkv)
    queries, keys, values = (head_parts(qkv, part, group, head) for part in range(3))
    scores = jnp.stack([dot_nt(key, query) for key, query in zip(keys, queries)])
    probs = softmax_keys(scores * (head**-0.5) + same_row_bias(group, features)[None]).astype(BF16)
    att = join_parts([dot_tn(probs[at], value).astype(BF16) for at, value in enumerate(values)])
    return start + dot_nn(att, w_out), qkv, probs, att


def context_kernel(count_ref, cells_ref, mask_ref, *refs):
    vectors_ref, (w_qkv_ref, w_out_ref, send_ref, after_ref) = refs[:4], refs[4:]
    rows, features, width = cells_ref.shape
    cells = rows * features
    start, _ = start_cells(cells_ref[...], mask_ref[...], 0, vector(vectors_ref, 0))
    after, _, _, _ = feature_forward(start, vector(vectors_ref, 1), w_qkv_ref[...], w_out_ref[...], features, cells)
    after_ref[...] = after
    xhat, _ = normalize(after)
    send_ref[0:cells, :] = (xhat * vector(vectors_ref, 2)).astype(BF16)
    count = count_ref[0, 0].astype(F32)
    send_ref[cells : cells + 16, :] = jnp.full((16, width), count, F32).astype(BF16)


def feature_kernel(cells_ref, mask_ref, upstream_ref, *refs):
    vectors_ref, refs = refs[:4], refs[4:]
    w_qkv_ref, w_out_ref, after_ref, upstream_t_ref, qkv_ref, probs_ref, att_ref = refs
    rows, features, width = cells_ref.shape
    start, _ = start_cells(cells_ref[...], mask_ref[...], pl.program_id(0) * rows, vector(vectors_ref, 0))
    after, qkv, probs, att = feature_forward(
        start, vector(vectors_ref, 1), w_qkv_ref[...], w_out_ref[...], features, GROUP_ROWS * features
    )
    qkv_ref[...] = qkv
    probs_ref[...] = probs.reshape(probs_ref.shape)
    att_ref[...] = att
    after_ref[...] = jnp.swapaxes(after.reshape(rows, features, width), 0, 1)
    upstream_t_ref[...] = jnp.swapaxes(upstream_ref[...].astype(F32), 0, 1).astype(BF16)


def head_blocks(tensor):
    keys, width = tensor.shape
    tiled = jnp.concatenate([tensor] * HEADS, axis=0)
    row_head = lax.broadcasted_iota(jnp.int32, tiled.shape, 0) // keys
    lane_head = lax.broadcasted_iota(jnp.int32, tiled.shape, 1) // (width // HEADS)
    return jnp.where(row_head == lane_head, tiled, jnp.zeros_like(tiled))


def own_heads(tensor, keys):
    head = tensor.shape[1] // HEADS
    return jnp.concatenate([tensor[h * keys : (h + 1) * keys, h * head : (h + 1) * head] for h in range(HEADS)], axis=1)


def gelu_parts(inner):
    const = 0.7978845608028654
    cubic = const * 0.044715
    inner = inner.astype(BF16)
    square = inner * inner
    half = 0.5 + 0.5 * jnp.tanh(inner * (const + cubic * square))
    hidden = inner * half
    slope = half + (hidden - hidden * half) * (2.0 * const + (6.0 * cubic) * square)
    return hidden, slope


def read_slots(gathered, idx_ref, slots_ref, bias_ref, features):
    keys, width = slots_ref.shape[1], slots_ref.shape[2]
    blocks = keys // CTX_DEV
    block = CTX_DEV * features
    piece = block + 16
    slot = lax.broadcasted_iota(jnp.int32, (keys, 128), 0)
    counts = jnp.zeros((keys, 128), F32)
    core, line = idx_ref[1] % 2, idx_ref[1] // 2
    for pair in range(blocks // 2):
        if len(gathered) == 2:
            mine, other = (ref[pair * piece : (pair + 1) * piece, :].astype(F32) for ref in gathered)
            even, odd = jnp.where(core == 0, mine, other), jnp.where(core == 0, other, mine)
            at = line ^ pair
        else:
            even, odd = (gathered[0][(2 * pair + j) * piece : (2 * pair + j + 1) * piece, :].astype(F32) for j in range(2))
            at = pair
        both = jnp.concatenate([even[0:block], odd[0:block]], axis=0).reshape(2 * CTX_DEV, features, width)
        slots_ref[:, pl.ds(pl.multiple_of(at * 2 * CTX_DEV, 2 * CTX_DEV), 2 * CTX_DEV), :] = jnp.swapaxes(both, 0, 1)
        for j, part in enumerate((even, odd)):
            counts = jnp.where(slot // CTX_DEV == 2 * at + j, part[block : block + 1, 0:128], counts)
    bias = jnp.where((slot % CTX_DEV).astype(F32) < counts, 0.0, MASKED)
    bias_ref[...] = jnp.concatenate([bias] * HEADS, axis=0)


def emit(idx_ref, keep, send, sources):
    tab, block = idx_ref[0], idx_ref[1]
    core, line = block % 2, block // 2
    lines, rows, _ = keep[0].shape
    tabs = keep[1].shape[0] + 1
    for u in range(tabs):
        for q in range(lines):
            for refs, shard in ((keep, core), (send, 1 - core)):
                ref = refs[0].at[q] if u == 0 else refs[1].at[u - 1, q]
                for acc, column in sources:
                    height, width = acc.shape
                    part = height // (2 * lines * tabs)
                    low = (((line ^ q) * 2 + shard) * tabs + (tab ^ u)) * part
                    for at in range(part // rows):
                        low_at = pl.multiple_of(low + at * rows, rows)
                        ref[:, column + at * width : column + (at + 1) * width] = acc[pl.ds(low_at, rows), :].astype(BF16)


def rows_kernel(pieces, fast, *refs):
    (idx_ref, after_ref, upstream_ref), vectors_ref, refs = refs[:3], refs[3:7], refs[7:]
    (w_row_ref, w_out_ref, w_up_hbm, w_down_hbm), refs = refs[:4], refs[4:]
    gathered, refs = refs[:pieces], refs[pieces:]
    (output_ref, grad_after_ref, gains_ref), refs = refs[:3], refs[3:]
    slot_outs, refs = (refs[:2], refs[2:]) if fast else (refs[:1], refs[1:])
    if fast:
        outs, refs = refs[:4], refs[4:]
        stages, copies, refs = refs[-9:-1], refs[-1], refs[:-9]
    *refs, w_up_ref, w_down_ref, loads = refs
    grad_up, grad_down, grad_qkv, grad_out, slots_ref, bias_ref, gain_acc = refs
    feats, rows, width = after_ref.shape
    features, keys, _ = slots_ref.shape
    hidden_all = w_up_ref.shape[1]
    cells = feats * rows
    head = width // HEADS
    step = pl.program_id(0)
    gain_row, gain_mlp = vector(vectors_ref, 2), vector(vectors_ref, 3)

    last = pl.num_programs(0) - 1
    fetches = [
        pltpu.make_async_copy(source, target, loads.at[at])
        for at, (source, target) in enumerate(((w_up_hbm, w_up_ref), (w_down_hbm, w_down_ref)))
    ]

    @pl.when(step == 0)
    def _():
        for fetch in fetches:
            fetch.start()
        read_slots(gathered, idx_ref, slots_ref, bias_ref, features)
        for ref in (grad_qkv, grad_out, grad_up, grad_down, gain_acc):
            ref[...] = jnp.zeros_like(ref)

    after = after_ref[...].reshape(cells, width)
    xhat2, scale2 = normalize(after)
    normed_two = (xhat2 * gain_row).astype(BF16)
    query = dot_nn(normed_two, w_row_ref[:, 0:width]).astype(BF16)
    slots = slots_ref[pl.ds(step * feats, feats)].reshape(feats * keys, width).astype(BF16)
    kv = dot_nn(slots, w_row_ref[:, width : 3 * width]).astype(BF16)
    keys_b = [head_blocks(kv[f * keys : (f + 1) * keys, 0:width]) for f in range(feats)]
    values_b = [head_blocks(kv[f * keys : (f + 1) * keys, width : 2 * width]) for f in range(feats)]
    query_f = [query[f * rows : (f + 1) * rows] for f in range(feats)]
    scores = jnp.stack([dot_nt(keys_b[f], query_f[f]) for f in range(feats)])
    scores = scores * (head**-0.5) + bias_ref[:, 0:rows][None]
    probs = softmax_keys(scores.reshape(feats * HEADS, keys, rows))
    probs_b = probs.reshape(feats, HEADS * keys, rows).astype(BF16)
    att = jnp.concatenate([dot_tn(probs_b[f], values_b[f]).astype(BF16) for f in range(feats)], axis=0)
    after_two = after + dot_nn(att, w_out_ref[...])

    @pl.when(step == 0)
    def _():
        for fetch in fetches:
            fetch.wait()

    xhat3, scale3 = normalize(after_two)
    normed_three = (xhat3 * gain_mlp).astype(BF16)
    upstream = upstream_ref[...].reshape(cells, width)
    piece = 256
    hidden, grad_inner = [], []
    first = lambda at: (dot_nn(normed_three, w_up_ref[:, at : at + piece]), dot_nt(upstream, w_down_ref[at : at + piece, :]))
    ahead = first(0)
    for at in range(0, hidden_all, piece):
        inner, back = ahead
        if at + piece < hidden_all:
            ahead = first(at + piece)
        part, slope = gelu_parts(inner)
        hidden.append(part)
        grad_inner.append(back.astype(BF16) * slope)
    hidden = jnp.concatenate(hidden, axis=1)
    grad_inner = jnp.concatenate(grad_inner, axis=1)
    total = after_two + dot_nn(hidden, w_down_ref[...])
    grad3 = dot_nt(grad_inner, w_up_ref[...])
    grad_down[...] += dot_tn(hidden, upstream)
    grad_up[...] += dot_tn(normed_three, grad_inner)
    output_ref[...] = total.astype(BF16).reshape(feats, rows, width)
    gain_acc[0] += column_sum(grad3 * xhat3)
    grad_two = upstream.astype(F32) + norm_back(xhat3, scale3, gain_mlp, grad3)

    if fast:
        wide, narrow = stages[0].shape[-1], stages[4].shape[-1]
        sends = []
        for at, stage in enumerate(stages):
            low, size = (0, wide) if at < 4 else (wide, narrow)
            lead = (slice(None),) * (len(stage.shape) - 1)
            sends.append(pltpu.make_async_copy(stage, outs[at % 4].at[(*lead, pl.ds(low, size))], copies.at[at]))

        @pl.when(step == last)
        def _():
            emit(idx_ref, stages[0:2], stages[2:4], [(grad_up, 0), (grad_down, hidden_all)])
            for send in sends[0:4]:
                send.start()

    branch = grad_two.astype(BF16)
    grad_out[...] += dot_tn(att, branch)
    grad_att = dot_nt(branch, w_out_ref[...]).astype(BF16)
    grad_f = [grad_att[f * rows : (f + 1) * rows] for f in range(feats)]
    grad_probs = jnp.stack([dot_nt(values_b[f], grad_f[f]) for f in range(feats)]).reshape(feats * HEADS, keys, rows)
    grad_scores = probs * (grad_probs - jnp.sum(grad_probs * probs, axis=1, keepdims=True))
    grad_scores = grad_scores.reshape(feats, HEADS * keys, rows).astype(BF16)
    grad_query = jnp.concatenate([dot_tn(grad_scores[f], keys_b[f]) for f in range(feats)], axis=0)
    grad_query = (grad_query * (head**-0.5)).astype(BF16)
    grad_keys = [own_heads(dot_nn(grad_scores[f], query_f[f]), keys) for f in range(feats)]
    grad_values = [own_heads(dot_nn(probs_b[f], grad_f[f]), keys) for f in range(feats)]
    grad_kv = jnp.concatenate(
        [jnp.concatenate(grad_keys, axis=0) * (head**-0.5), jnp.concatenate(grad_values, axis=0)], axis=1
    ).astype(BF16)
    grad_qkv[:, 0:width] += dot_tn(normed_two, grad_query)
    grad_qkv[:, width : 3 * width] += dot_tn(slots, grad_kv)
    slots_ref[pl.ds(step * feats, feats)] = dot_nt(grad_kv, w_row_ref[:, width : 3 * width]).reshape(feats, keys, width)
    grad_normed = dot_nt(grad_query, w_row_ref[:, 0:width])
    gain_acc[1] += column_sum(grad_normed * xhat2)
    grad_after_ref[...] = (grad_two + norm_back(xhat2, scale2, gain_row, grad_normed)).reshape(feats, rows, width)

    @pl.when(step == last)
    def _():
        if fast:
            emit(idx_ref, stages[4:6], stages[6:8], [(grad_qkv, 0), (grad_out, 3 * width)])
            for send in sends[4:8]:
                send.start()
        gains_ref[...] = gain_acc[...]
        block = CTX_DEV * features
        core, line = idx_ref[1] % 2, idx_ref[1] // 2
        for q in range(keys // (2 * CTX_DEV)):
            low = pl.multiple_of((line ^ q) * 2 * CTX_DEV, 2 * CTX_DEV) if fast else q * 2 * CTX_DEV
            both = jnp.swapaxes(slots_ref[:, pl.ds(low, 2 * CTX_DEV), :], 0, 1).reshape(2 * block, width)
            if fast:
                even, odd = both[0:block], both[block:]
                slot_outs[0][q] = jnp.where(core == 0, even, odd).astype(BF16)
                slot_outs[1][q] = jnp.where(core == 0, odd, even).astype(BF16)
            else:
                slot_outs[0][2 * q * block : 2 * (q + 1) * block, :] = both.astype(BF16)
        if fast:
            for send in sends:
                send.wait()


def feature_backward(grad_one, packed, probs_b, att, start, gain, w_qkv, w_out, group, grad_w_qkv, grad_w_out):
    cells, width = start.shape
    head = width // HEADS
    branch = grad_one.astype(BF16)
    grad_w_out[...] += dot_tn(att, branch)
    grad_att = dot_nt(branch, w_out).astype(BF16)
    queries, keys, values = (head_parts(packed, part, group, head) for part in range(3))
    grads = [
        grad_att[low : low + group, h * head : (h + 1) * head] for low in range(0, cells, group) for h in range(HEADS)
    ]
    probs = probs_b.astype(F32)
    grad_probs = jnp.stack([dot_nt(value, grad) for value, grad in zip(values, grads)])
    grad_scores = probs * (grad_probs - jnp.sum(grad_probs * probs, axis=1, keepdims=True))
    grad_scores = grad_scores.astype(BF16)
    grad_queries = join_parts([dot_tn(grad_scores[at], key) for at, key in enumerate(keys)]) * (head**-0.5)
    grad_keys = join_parts([dot_nn(grad_scores[at], query) for at, query in enumerate(queries)]) * (head**-0.5)
    grad_values = join_parts([dot_nn(probs_b[at], grad) for at, grad in enumerate(grads)])
    grad_qkv = jnp.concatenate([grad_queries.astype(BF16), grad_keys.astype(BF16), grad_values.astype(BF16)], axis=1)
    xhat, scale = normalize(start)
    normed = (xhat * gain).astype(BF16)
    piece = 256
    for at in range(0, 3 * width, piece):
        grad_w_qkv[:, at : at + piece] += dot_tn(normed, grad_qkv[:, at : at + piece])
    grad_normed = dot_nt(grad_qkv, w_qkv)
    grad_start = grad_one + norm_back(xhat, scale, gain, grad_normed)
    return column_sum(grad_normed * xhat), grad_start


def feature_backward_kernel(slots, waits, fast, *refs):
    (idx_ref, cells_ref, mask_ref), vectors_ref, refs = refs[:3], refs[3:7], refs[7:]
    (
        w_qkv_ref, w_out_ref, grad_after_ref, qkv_ref, probs_ref, att_ref, after_ref, row_gains,
    ), refs = refs[:8], refs[8:]
    slot_refs, refs = refs[:slots], refs[slots + waits :]
    (grad_cells_ref, gains_ref), refs = refs[:2], refs[2:]
    if fast:
        outs, refs = refs[:4], refs[4:]
    grad_w_qkv, grad_w_out, gains, columns, extra_ref = refs
    rows, features, width = cells_ref.shape
    cells = rows * features
    block = CTX_DEV * features
    group = GROUP_ROWS * features
    step = pl.program_id(0)

    @pl.when(step == 0)
    def _():
        for ref in (grad_w_qkv, grad_w_out, gains):
            ref[...] = jnp.zeros_like(ref)
        total = slot_refs[0][...].astype(F32)
        for ref in slot_refs[1:]:
            total = total + ref[...].astype(F32)
        xhat, scale = normalize(after_ref[...])
        extra_ref[...] = norm_back(xhat, scale, vector(vectors_ref, 2), total)
        gains[2] = row_gains[1] + column_sum(total * xhat)
        gains[3] = row_gains[0]

    @pl.when(step > 0)
    def _():
        extra_ref[...] = jnp.zeros_like(extra_ref)

    grad_one = jnp.swapaxes(grad_after_ref[...], 0, 1).reshape(cells, width)
    grad_one = jnp.concatenate([grad_one[0:block] + extra_ref[...], grad_one[block:]], axis=0)
    start, absent = start_cells(cells_ref[...], mask_ref[...], step * rows, vector(vectors_ref, 0))
    add_gain, grad_start = feature_backward(
        grad_one, qkv_ref[...], probs_ref[...].reshape(cells // group * HEADS, group, group), att_ref[...],
        start, vector(vectors_ref, 1), w_qkv_ref[...], w_out_ref[...], group, grad_w_qkv, grad_w_out,
    )
    gains[0] += add_gain
    grad_start = grad_start.reshape(rows, features, width)
    grad_cells_ref[...] = jnp.where(absent, 0.0, grad_start)
    gains[1] += column_sum(jnp.where(absent, grad_start, 0.0).reshape(cells, width))

    @pl.when(step == pl.num_programs(0) - 1)
    def _():
        sums = jnp.concatenate([jnp.sum(gains[at], axis=0, keepdims=True) for at in range(4)], axis=0)
        gains_ref[...] = sums
        if fast:
            columns[...] = jnp.concatenate([sums, jnp.zeros((124, width), F32)], axis=0).T
            emit(idx_ref, outs[0:2], outs[2:4], [(grad_w_qkv, 0), (grad_w_out, 3 * width), (columns, 4 * width)])


def output_kernel(output_t_ref, output_ref):
    output_ref[...] = jnp.swapaxes(output_t_ref[...].astype(F32), 0, 1).astype(BF16)


def join_kernel(count, *refs):
    rows = refs[0].shape[0]
    for at in range(count):
        refs[-1][at * rows : (at + 1) * rows, :] = refs[at][...]


def sum_kernel(count, groups, *refs):
    ins, outs = refs[:count], refs[len(refs) - len(groups) :]
    for group, out in zip(groups, outs):
        for at, part in enumerate(group):
            total = ins[0][part].astype(F32)
            for ref in ins[1:]:
                total = total + ref[part].astype(F32)
            out[at] = total.astype(BF16)


def whole(array):
    zeros = (0,) * array.ndim
    return pl.BlockSpec(array.shape, lambda i: zeros, pipeline_mode=pl.Buffered(1))


def whole_out(shape):
    zeros = (0,) * len(shape)
    return pl.BlockSpec(shape, lambda i: zeros, pipeline_mode=pl.Buffered(1))


def tiles(shape, axis, offset=0):
    def index(i):
        return tuple(i + offset if d == axis else 0 for d in range(len(shape)))

    return pl.BlockSpec(shape, index)


WAITS = 1e14
SCALARS = pl.BlockSpec(memory_space=pltpu.SMEM)
UNTOUCHED = pl.BlockSpec(memory_space=pl.ANY)


def struct(shape, dtype):
    return jax.ShapeDtypeStruct(shape, dtype)


def in_hbm(array):
    return pltpu.with_memory_space_constraint(array, pltpu.HBM)


def call(kernel, name, grid, args, in_specs, outs, out_specs, scratch, flops, aliases=None, vmem=VMEM_LIMIT, pinned=True, ahead=(), free=(), fixed=()):
    small = 1 << 15
    large = lambda a: pinned and math.prod(a.shape) >= 1 << 18
    args = [
        pltpu.with_memory_space_constraint(a, pltpu.VMEM if i in ahead else pltpu.HBM) if large(a) else a
        for i, a in enumerate(args)
    ]
    outs = [
        pltpu.HBM(o.shape, o.dtype) if large(o) and i not in free else pltpu.VMEM(o.shape, o.dtype) if i in fixed else o
        for i, o in enumerate(outs)
    ]
    sizes = [math.prod(a.shape) * a.dtype.itemsize for a in [*args, *outs]]
    return pl.pallas_call(
        kernel,
        grid=(grid,),
        in_specs=in_specs,
        out_shape=outs,
        out_specs=out_specs,
        scratch_shapes=scratch,
        input_output_aliases=aliases or {},
        compiler_params=pltpu.CompilerParams(vmem_limit_bytes=vmem, dimension_semantics=("arbitrary",)),
        cost_estimate=pl.CostEstimate(flops=int(flops), bytes_accessed=int(sum(sizes)), transcendentals=0),
        name=name,
    )(*args)


def xor_pairs(size, bit):
    return [(i, i ^ bit) for i in range(size)]


def swap(array, axis, size, bit):
    return lax.ppermute(array, axis, xor_pairs(size, bit))


def add_all(terms):
    total = terms[0].astype(F32)
    for term in terms[1:]:
        total = total + term.astype(F32)
    return total.astype(BF16)


def exchange(parts, axis, size, unit):
    return [parts[0]] + [swap(parts[at], axis, size, at * unit) for at in range(1, len(parts))]


def sum_parts(parts, groups, name, after=(), flops=WAITS):
    outs = [struct((len(group), *parts[0].shape[1:]), BF16) for group in groups]
    return call(
        functools.partial(sum_kernel, len(parts), groups),
        name,
        1,
        [*parts, *after],
        [whole(a) for a in parts] + [UNTOUCHED] * len(after),
        outs,
        [whole_out(o.shape) for o in outs],
        [],
        flops,
        pinned=False,
    )


def place_kernel(tabs, moves, gains, *refs):
    idx_ref, ins = refs[0], refs[1 : 1 + tabs]
    outs = refs[len(refs) - len(moves) - gains :]
    if gains:
        outs, rows_out, columns = outs[: len(moves) - 1], outs[len(moves) - 1 : -1], outs[-1]
        outs = [*outs, columns]
    tab = idx_ref[0]
    for out, (count, column) in zip(outs, moves):
        width = out.shape[1]
        for u in range(tabs):
            rows = ins[u].shape[0]
            for at in range(count):
                low = pl.multiple_of(((tab ^ u) * count + at) * rows, 16)
                out[pl.ds(low, rows), :] = ins[u][:, column + at * width : column + (at + 1) * width].astype(F32)
    if gains:
        turned = columns[...].T
        for at, out in enumerate(rows_out):
            out[...] = turned[at : at + 1, 0 : out.shape[1]]


def place(idx, pieces, moves, outs, tabs, name, after, gains=0, scratch=()):
    return call(
        functools.partial(place_kernel, tabs, moves, gains),
        name,
        1,
        [idx, *pieces, *after],
        [SCALARS] + [whole(a) for a in pieces] + [UNTOUCHED] * len(after),
        outs,
        [whole_out(o.shape) for o in outs],
        list(scratch),
        WAITS,
        pinned=False,
    )


def per_device(
    tabs,
    blocks,
    cells,
    missing_mask,
    context_counts,
    missing_embedding,
    gain_feature,
    w_feature_qkv,
    w_feature_out,
    gain_row,
    w_row_qkv,
    w_row_out,
    gain_mlp,
    w_up,
    w_down,
    upstream,
):
    _, rows, features, width = cells.shape
    hidden = w_up.shape[1]
    keys = CTX_DEV * blocks
    cells, mask, upstream = cells[0], jnp.swapaxes(missing_mask[0], 0, 1), upstream[0]
    mask = in_hbm(mask)
    vectors = [in_hbm(v.reshape(-1, 128)) for v in (missing_embedding, gain_feature, gain_row, gain_mlp)]
    all_cells = rows * features
    cost = all_cells * width * width
    fast = tabs == 4 and blocks == 8 and width == 16 * tabs * blocks and hidden % (16 * tabs * blocks) == 0
    tall = hidden // (16 * tabs * blocks)
    idx = jnp.stack([lax.axis_index("tab"), lax.axis_index("rows")]).astype(jnp.int32)

    block = CTX_DEV * features
    piece_rows = block + 16
    payload, after_ctx = call(
        context_kernel,
        "context_rows",
        1,
        [context_counts, cells, mask, *vectors, w_feature_qkv, w_feature_out],
        [SCALARS, pl.BlockSpec((CTX_DEV, features, width), lambda i: (0, 0, 0))]
        + [whole(a) for a in (mask, *vectors, w_feature_qkv, w_feature_out)],
        [struct((piece_rows, width), BF16), struct((block, width), F32)],
        [whole_out((piece_rows, width)), whole_out((block, width))],
        [],
        2 * block * width * 4 * width,
    )
    if fast:
        received = exchange([payload] * (blocks // 2), "rows", blocks, 2)


    tile = min(32, rows)
    steps = rows // tile
    groups = tile // GROUP_ROWS
    group = GROUP_ROWS * features
    after_one, upstream_t, qkv, probs, att = call(
        feature_kernel,
        "feature_forward",
        steps,
        [cells, mask, upstream, *vectors, w_feature_qkv, w_feature_out],
        [tiles((tile, features, width), 0), whole(mask), tiles((tile, features, width), 0)]
        + [whole(a) for a in (*vectors, w_feature_qkv, w_feature_out)],
        [
            struct((features, rows, width), F32),
            struct((features, rows, width), BF16),
            struct((all_cells, 3 * width), BF16),
            struct((rows // GROUP_ROWS, HEADS, group, group), BF16),
            struct((all_cells, width), BF16),
        ],
        [
            tiles((features, tile, width), 1),
            tiles((features, tile, width), 1),
            tiles((tile * features, 3 * width), 0),
            tiles((groups, HEADS, group, group), 0),
            tiles((tile * features, width), 0),
        ],
        [],
        2 * 5 * cost,
        ahead=(7, 8) if fast else (),
    )

    if fast:
        mine = call(
            functools.partial(join_kernel, len(received)),
            "join",
            1,
            received + [att],
            [whole(a) for a in received] + [UNTOUCHED],
            [struct((len(received) * piece_rows, width), BF16)],
            [whole_out((len(received) * piece_rows, width))],
            [],
            0,
        )[0]
        gathered = [mine, swap(mine, "rows", blocks, 1)]
    else:
        gathered = [lax.all_gather(payload, "rows", axis=0, tiled=True)]

    feats = 4
    cell_tile = (feats, rows, width)
    full = [struct(s, F32) for s in ((width, hidden), (hidden, width), (width, 3 * width), (width, width))]
    if fast:
        share = lambda w: [(blocks // 2, 16, w), (tabs - 1, blocks // 2, 16, w)] * 2
        shares = [struct(s, BF16) for s in share(hidden + (4 + tall) * width)]
        stages = [pltpu.VMEM(s, BF16) for w in (hidden + tall * width, 4 * width) for s in share(w)]
        stages += [pltpu.SemaphoreType.DMA((8,))]
    else:
        shares = full
    weights = [*vectors, w_row_qkv, w_row_out, w_up, w_down]
    slot_outs = [struct((blocks // 2, block, width), BF16)] * 2 if fast else [struct((keys * features, width), BF16)]
    output_t, grad_after, row_gains, *row_shares = call(
        functools.partial(rows_kernel, len(gathered), fast),
        "rows_and_feed_forward",
        features // feats,
        [idx, after_one, upstream_t] + weights + gathered,
        [SCALARS] + [tiles(cell_tile, 0)] * 2 + [whole(a) for a in weights[:6]] + [UNTOUCHED] * 2 + [whole(a) for a in gathered],
        [
            struct((features, rows, width), BF16),
            struct((features, rows, width), F32),
            struct((2, 8, width), F32),
        ]
        + slot_outs
        + shares,
        [tiles(cell_tile, 0)] * 2
        + [whole_out((2, 8, width))]
        + [whole_out(s.shape) for s in slot_outs]
        + [UNTOUCHED if fast else whole_out(s.shape) for s in shares],
        [pltpu.VMEM(s.shape, F32) for s in (full if fast else [])]
        + [pltpu.VMEM(s, F32) for s in ((features, keys, width), (HEADS * keys, 128), (2, 8, width))]
        + [pltpu.VMEM(a.shape, BF16) for a in (w_up, w_down)]
        + [pltpu.SemaphoreType.DMA((2,))]
        + (stages if fast else []),
        2 * 34 * cost,
        vmem=(50 if fast else 62) * MIB,
        free=(0, 6) if fast else (),
        fixed=(0, 6) if fast else (),
        ahead=(7, 8) if fast else (),
    )
    slot_parts, row_shares = row_shares[: len(slot_outs)], row_shares[len(slot_outs) :]
    output = call(
        output_kernel,
        "output",
        steps,
        [output_t],
        [tiles((features, tile, width), 1)],
        [struct((rows, features, width), BF16)],
        [tiles((tile, features, width), 0)],
        [],
        0,
        ahead=(0,) if fast else (),
    )[0]
    if fast:
        keep, keep_rest, send, send_rest = row_shares
        got_rest = swap(send_rest, "rows", blocks, 1)
        parts = [add_all([keep_rest[u], got_rest[u]]) for u in range(tabs - 1)]
        got = swap(send, "rows", blocks, 1)
        row_parts = [keep, got] + [swap(parts[u - 1], "tab", tabs, u) for u in range(1, tabs)]
        slot_parts = [slot_parts[0], swap(slot_parts[1], "rows", blocks, 1)]
        slot_parts = sum_parts(slot_parts, [(q,) for q in range(blocks // 2)], "sum_core_slots", [parts[0], got])
        own_slots = exchange([part[0] for part in slot_parts], "rows", blocks, 2)
    else:
        own_slots = [lax.psum_scatter(slot_parts[0], "rows", scatter_dimension=0, tiled=True)]

    weights = [mask, *vectors, w_feature_qkv, w_feature_out]
    sums = [struct((width, 3 * width), F32), struct((width, width), F32)]
    outs = [struct(s, BF16) for s in share(4 * width + 128)] if fast else sums
    waits = [output]
    rest = [after_ctx, row_gains, *own_slots]
    grad_cells, gains, *feature_shares = call(
        functools.partial(feature_backward_kernel, len(own_slots), len(waits), fast),
        "feature_backward",
        steps,
        [idx, cells] + weights + [grad_after, qkv, probs, att] + rest + waits,
        [SCALARS, tiles((tile, features, width), 0)]
        + [whole(a) for a in weights]
        + [
            tiles((features, tile, width), 1),
            tiles((tile * features, 3 * width), 0),
            tiles((groups, HEADS, group, group), 0),
            tiles((tile * features, width), 0),
        ]
        + [whole(a) for a in rest]
        + [UNTOUCHED] * len(waits),
        [struct((rows, features, width), F32), struct((4, width), F32)] + outs,
        [tiles((tile, features, width), 0), whole_out((4, width))] + [whole_out(o.shape) for o in outs],
        ([pltpu.VMEM(s.shape, F32) for s in sums] if fast else [])
        + [pltpu.VMEM(s, F32) for s in ((4, 8, width), (width, 128), (block, width))],
        0,
        vmem=40 * MIB,
        free=(3,) if fast else (),
        fixed=(3,) if fast else (),
        ahead=(7, 8) if fast else (),
    )

    if fast:
        shard = lambda height, columns: struct((height // blocks, columns), F32)
        keep, keep_rest, send, send_rest = feature_shares
        got_rest = swap(send_rest, "rows", blocks, 1)
        got = swap(send, "rows", blocks, 1)
        one = [(q,) for q in range(blocks // 2)]
        lines = sum_parts(row_parts, one, "sum_tab_rows", [in_hbm(grad_cells)])
        row_parts = exchange(lines, "rows", blocks, 2)
        parts = sum_parts([keep_rest, got_rest], [(u,) for u in range(tabs - 1)], "sum_core_features", [lines[0]], 0)
        parts = [keep, got] + [swap(parts[u - 1][0], "tab", tabs, u) for u in range(1, tabs)]
        lines = sum_parts(parts, one, "sum_tab_features")
        parts = exchange(lines, "rows", blocks, 2)
        (own_rows,) = sum_parts(row_parts, [(0,)], "sum_rows_rows", [lines[0]])
        row_pieces = exchange([own_rows[0]] * tabs, "tab", tabs, 1)
        own = add_all([part[0] for part in parts])
        pieces = exchange([own] * tabs, "tab", tabs, 1)
        wide = hidden + tall * width
        moves = [(1, 0), (tall, hidden), (1, wide), (1, wide + 3 * width)]
        outs = [shard(width, hidden), shard(hidden, width), shard(width, 3 * width), shard(width, width)]
        grad_up, grad_down, grad_row_qkv, grad_row_out = place(idx, row_pieces, moves, outs, tabs, "place_rows", [])
        moves = [(1, 0), (1, 3 * width), (1, 4 * width)]
        outs = [shard(width, 3 * width), shard(width, width)] + [struct((1, width // blocks), F32)] * 4
        grad_feature_qkv, grad_feature_out, *gains = place(
            idx, pieces, moves, outs, tabs, "place_features", [in_hbm(grad_up)], 4, [pltpu.VMEM((width // blocks, 128), F32)]
        )
        gains = [g.reshape(width // blocks) for g in gains]
    else:
        scatter = lambda a, axis: lax.psum_scatter(a, "rows", scatter_dimension=axis, tiled=True)
        gains = lax.psum(scatter(gains, 1), "tab")
        weights = lax.psum([scatter(w, 0) for w in [*row_shares, *feature_shares]], "tab")
        grad_up, grad_down, grad_row_qkv, grad_row_out, grad_feature_qkv, grad_feature_out = weights
    return (
        output[None],
        grad_cells[None],
        gains[1],
        gains[0],
        grad_feature_qkv,
        grad_feature_out,
        gains[2],
        grad_row_qkv,
        grad_row_out,
        gains[3],
        grad_up,
        grad_down,
    )


def solution(mesh):
    in_specs = (
        P("tab", "rows", None, None),
        P("tab", "rows", None),
        P("tab", "rows"),
        P(),
        P(),
        P(),
        P(),
        P(),
        P(),
        P(),
        P(),
        P(),
        P(),
        P("tab", "rows", None, None),
    )
    out_specs = (
        P("tab", "rows", None, None),
        P("tab", "rows", None, None),
        P("rows"),
        P("rows"),
        P("rows", None),
        P("rows", None),
        P("rows"),
        P("rows", None),
        P("rows", None),
        P("rows"),
        P("rows", None),
        P("rows", None),
    )
    return jax.shard_map(
        functools.partial(per_device, mesh.shape["tab"], mesh.shape["rows"]),
        mesh=mesh,
        in_specs=in_specs,
        out_specs=out_specs,
        check_vma=False,
    )
```
